256 devices in a mesh: kvp: 64 (over z, x, core), section: 4 (over y).
Axes of the slice: x: 4, y: 4, z: 8, core: 2. Of those that a mesh axis runs over, the one named last changes fastest.
Arguments:
- hidden: bfloat16 [4, 128, 8192], P('section', 'kvp'), may hold values from -15 to 15
- norm_gain: bfloat16 [4, 8192], P('section'), may hold values from 0.099609375 to 1.8984375
- w_query: bfloat16 [4, 8192, 8192], P('section', None, 'kvp'), may hold values from -0.0625 to 0.0625
- w_kv: bfloat16 [4, 8192, 2048], P('section', None, 'kvp'), may hold values from -0.3125 to 0.3125
- w_out: bfloat16 [4, 8192, 8192], P('section', 'kvp'), may hold values from -0.0625 to 0.0625
- doc_cache: bfloat16 [4, 256, 128, 2048], P('section', 'kvp'), may hold values from -470 to 470
- page_table: int32 [4, 64, 4], P('section', 'kvp'), may hold values from 0 to 3, as said below
- page_count: int32 [4, 64], P('section', 'kvp'), may hold values from 1 to 4, as said below
Outputs:
- next_hidden: bfloat16 [4, 128, 8192], P('section', 'kvp')
The draws below stay inside these ranges and needn't reach their ends.
Inputs may be any that keep to these rules, and one draw needn't show every extreme that they name: Each row page_table[s, k] is an ordering of all slots 0 to 3 of that device's pool. `page_count`: in every section one device has all 4 pages live; the others have 1 to 4, unevenly.
All inputs are finite; a program needn't handle non-finite values.
Results may differ from the reference program's by a relative error of at most 0.027.
The reference program's roundings to bfloat16 on the way count: a program that leaves them out, or rounds other values in their place, can miss the bound.
Values may be sent and summed in bfloat16 or wider, within the bound.
A program may use at most 128 MiB of HBM per device.

```python
import math
import jax
import jax.numpy as jnp
from jax import lax

D = 8192
HEADS = 64
KVH = 8
HD = 128
PAGE = 128
PAGES_DEV = 4
SPAN = 128
SECTIONS = 4
N_KVP = 64


def draw_hidden(key, part):
    key = jax.random.fold_in(key, 3)
    base_key, row_key, column_key = jax.random.split(key, 3)
    shape = (SECTIONS, SPAN, D)
    base = jnp.clip(jax.random.normal(base_key, shape, jnp.float32), -5.0, 5.0)
    row_scale = jnp.exp(jax.random.uniform(row_key, (SECTIONS, SPAN, 1), jnp.float32, math.log(0.1), math.log(1.0)))
    column_scale = jnp.exp(jax.random.uniform(column_key, (1, 1, D), jnp.float32, math.log(0.3), math.log(3.0)))
    return (base * row_scale * column_scale).astype(jnp.bfloat16)


def draw_doc_cache(key, part):
    key = jax.random.fold_in(key, 7)
    key_part, value_part = jax.random.split(key, 2)
    lead = (SECTIONS, N_KVP * PAGES_DEV, PAGE)
    half_width = KVH * HD
    doc_keys = 3.0 * jnp.clip(jax.random.normal(key_part, lead + (half_width,), jnp.float32), -6.0, 6.0)
    doc_values = jnp.clip(jax.random.normal(value_part, lead + (half_width,), jnp.float32), -6.0, 6.0)
    return jnp.concatenate([doc_keys, doc_values], axis=-1).astype(jnp.bfloat16)


def shuffle_row(row_key):
    return jax.random.permutation(row_key, PAGES_DEV)


def draw_page_table(key, part):
    key = jax.random.fold_in(key, 5)
    row_keys = jax.random.split(key, SECTIONS * N_KVP)
    ordering = jax.vmap(shuffle_row)(row_keys)
    return ordering.reshape(SECTIONS, N_KVP, PAGES_DEV).astype(jnp.int32)


def draw_page_count(key, part):
    key = jax.random.fold_in(key, 9)
    first_key, second_key, full_key = jax.random.split(key, 3)
    shape = (SECTIONS, N_KVP)
    first_draw = jax.random.randint(first_key, shape, 1, PAGES_DEV + 1)
    second_draw = jax.random.randint(second_key, shape, 1, PAGES_DEV + 1)
    counts = jnp.minimum(first_draw, second_draw)
    full_slot = jax.random.randint(full_key, (SECTIONS, 1), 0, N_KVP)
    devices = jnp.arange(N_KVP, dtype=jnp.int32)[None, :]
    return jnp.where(devices == full_slot, PAGES_DEV, counts).astype(jnp.int32)


def block_levels(stream_key, dims, cuts, least, top_value):
    def one(position, shards_of):
        steps = jax.random.uniform(jax.random.fold_in(jax.random.fold_in(stream_key, 6), position), (shards_of,), jnp.float32, least / len(cuts), top_value / len(cuts))
        return jnp.repeat(jnp.exp(steps), dims[position] // shards_of).reshape((-1,) + (1,) * (len(dims) - position - 1))

    gain = one(*cuts[0])
    for cut in cuts[1:]:
        gain = gain * one(*cut)
    return gain


def centred(stream_key, extent, width, most, shards=(), held_as=jnp.bfloat16):
    loudness = block_levels(stream_key, extent, shards, -0.22, 0.18) if shards else 1.0
    array = jax.random.normal(stream_key, extent, jnp.float32) * width * loudness
    return jnp.minimum(jnp.maximum(array, -most), most).astype(held_as)


def setup_inputs(seed: int = 0) -> dict:
    key_list = jax.random.split(jax.random.key(seed), 9)
    return {
        "hidden": draw_hidden(jax.random.fold_in(key_list[8], 71), 0),
        "norm_gain": jnp.clip(1.0 + 0.18 * jax.random.normal(key_list[1], (SECTIONS, D), jnp.float32), 0.099609375, 1.8984375).astype(jnp.bfloat16),
        "w_query": centred(key_list[2], (SECTIONS, D, HEADS * HD), D ** -0.5, 0.0625, ((0, 4), (2, 64))),
        "w_kv": centred(key_list[3], (SECTIONS, D, 2 * KVH * HD), (D // 20) ** -0.5, 0.3125, ((0, 4), (2, 64))),
        "w_out": centred(key_list[4], (SECTIONS, HEADS * HD, D), (HEADS * HD) ** -0.5, 0.0625, ((0, 4), (1, 64))),
        "doc_cache": draw_doc_cache(jax.random.fold_in(key_list[8], 71), 0),
        "page_table": draw_page_table(jax.random.fold_in(key_list[8], 71), 0),
        "page_count": draw_page_count(jax.random.fold_in(key_list[8], 71), 0),
    }


epsilon = 1e-05
masked_score = -1e+30

def normalize(incoming, gain_row):
    values = incoming.astype(jnp.float32)
    inv_rms = lax.rsqrt(lax.optimization_barrier(jnp.mean(values * values, axis=-1, keepdims=True)) + epsilon)
    return (values * inv_rms * gain_row.astype(jnp.float32)).astype(jnp.bfloat16)

def document_partial(grouped, pool, page_ids, live_count, blocks):
    block_pages = min(PAGES_DEV, max(1, 512 // PAGE))
    query_rows = grouped.shape[1]
    half_width = KVH * HD

    def block_step(block_index, state_now):
        run_max, run_sum, run_out = state_now
        first_slot = block_index * block_pages
        picked = lax.dynamic_slice_in_dim(page_ids, first_slot, block_pages, 0)
        slot_live = first_slot + jnp.arange(block_pages, dtype=jnp.int32) < live_count
        page_rows = jnp.take(pool, picked, axis=0).reshape(block_pages * PAGE, 2 * half_width)
        doc_keys = page_rows[:, :half_width].reshape(block_pages * PAGE, KVH, HD)
        doc_values = page_rows[:, half_width:].reshape(block_pages * PAGE, KVH, HD)
        key_live = jnp.repeat(slot_live, PAGE)[None, None, :]
        scores = jnp.einsum('kqd,nkd->kqn', grouped.astype(jnp.float32), doc_keys.astype(jnp.float32)) * HD ** (-0.5)
        scores = jnp.where(key_live, scores, masked_score)
        block_max = lax.optimization_barrier(jnp.max(scores, axis=-1))
        weights = jnp.where(key_live, jnp.exp(scores - block_max[..., None]), 0.0)
        block_sum = lax.optimization_barrier(jnp.sum(weights, axis=-1))
        rounded = lax.optimization_barrier(weights.astype(jnp.bfloat16)).astype(jnp.float32)
        block_out = jnp.einsum('kqn,nkd->kqd', rounded, doc_values.astype(jnp.float32))
        new_max = jnp.maximum(run_max, block_max)
        old_factor = jnp.exp(run_max - new_max)
        new_factor = jnp.exp(block_max - new_max)
        return (new_max, run_sum * old_factor + block_sum * new_factor, run_out * old_factor[..., None] + block_out * new_factor[..., None])
    initial = (jnp.full((KVH, query_rows), masked_score, jnp.float32), jnp.zeros((KVH, query_rows), jnp.float32), jnp.zeros((KVH, query_rows, HD), jnp.float32))
    return lax.fori_loop(0, blocks, block_step, initial)

def span_part(own_queries, own_keys, own_values):
    span_len = own_queries.shape[0]
    scores = jnp.einsum('thd,uhd->htu', own_queries.astype(jnp.float32), own_keys.astype(jnp.float32)) * HD ** (-0.5)
    causal = (jnp.arange(span_len)[:, None] >= jnp.arange(span_len)[None, :])[None]
    scores = jnp.where(causal, scores, masked_score)
    self_max = lax.optimization_barrier(jnp.max(scores, axis=-1))
    weights = jnp.where(causal, jnp.exp(scores - self_max[..., None]), 0.0)
    self_sum = lax.optimization_barrier(jnp.sum(weights, axis=-1))
    rounded = lax.optimization_barrier(weights.astype(jnp.bfloat16)).astype(jnp.float32)
    self_out = jnp.einsum('htu,uhd->htd', rounded, own_values.astype(jnp.float32))
    return (self_max, self_sum, self_out)

def reference(hidden, norm_gain, w_query, w_kv, w_out, doc_cache, page_table, page_count):
    group_size = HEADS // KVH
    block_pages = min(PAGES_DEV, max(1, 512 // PAGE))
    results = []
    for section_index in range(SECTIONS):
        incoming = hidden[section_index]
        normed = normalize(incoming, norm_gain[section_index])
        queries = jnp.dot(normed, w_query[section_index], preferred_element_type=jnp.float32).astype(jnp.bfloat16)
        fresh_rows = jnp.dot(normed, w_kv[section_index], preferred_element_type=jnp.float32).astype(jnp.bfloat16)
        grouped = queries.reshape(SPAN, KVH, group_size, HD).transpose(1, 2, 0, 3).reshape(KVH, group_size * SPAN, HD)
        section_pool = doc_cache[section_index]
        section_table = page_table[section_index]
        section_count = page_count[section_index]

        def shard_step(state_now, device):
            pool = lax.dynamic_slice_in_dim(section_pool, device * PAGES_DEV, PAGES_DEV, 0)
            part_max, part_sum, part_out = document_partial(grouped, pool, section_table[device], section_count[device], PAGES_DEV // block_pages)
            total_max, total_sum, total_out = state_now
            new_max = jnp.maximum(total_max, part_max)
            old_factor = jnp.exp(total_max - new_max)
            new_factor = jnp.exp(part_max - new_max)
            return ((new_max, total_sum * old_factor + part_sum * new_factor, total_out * old_factor[..., None] + part_out * new_factor[..., None]), None)
        initial = (jnp.full((KVH, group_size * SPAN), masked_score, jnp.float32), jnp.zeros((KVH, group_size * SPAN), jnp.float32), jnp.zeros((KVH, group_size * SPAN, HD), jnp.float32))
        merged, _ = lax.scan(shard_step, initial, jnp.arange(N_KVP, dtype=jnp.int32))
        doc_max = merged[0].reshape(HEADS, SPAN)
        doc_sum = merged[1].reshape(HEADS, SPAN)
        doc_out = merged[2].reshape(HEADS, SPAN, HD)
        new_keys = jnp.repeat(fresh_rows[:, :KVH * HD].reshape(SPAN, KVH, HD), group_size, axis=1)
        new_values = jnp.repeat(fresh_rows[:, KVH * HD:].reshape(SPAN, KVH, HD), group_size, axis=1)
        self_max, self_sum, self_out = span_part(queries.reshape(SPAN, HEADS, HD), new_keys, new_values)
        top = jnp.maximum(doc_max, self_max)
        doc_factor = jnp.exp(doc_max - top)
        self_factor = jnp.exp(self_max - top)
        combined = (doc_out * doc_factor[..., None] + self_out * self_factor[..., None]) / (doc_sum * doc_factor + self_sum * self_factor)[..., None]
        attention = combined.transpose(1, 0, 2).reshape(SPAN, HEADS * HD).astype(jnp.bfloat16)
        mixed = jnp.dot(attention, w_out[section_index], preferred_element_type=jnp.float32)
        results.append((incoming.astype(jnp.float32) + mixed).astype(jnp.bfloat16))
    return jnp.roll(jnp.stack(results), 1, axis=0)
```

```python
import functools
import math

import jax
import jax.numpy as jnp
from jax import lax
from jax.experimental import pallas as pl
from jax.experimental.pallas import tpu as pltpu
from jax.sharding import PartitionSpec as P

MESH = pl.DeviceIdType.MESH
F32 = jnp.float32
BF16 = jnp.bfloat16

HD = 128
CORES = 2
RINGX = 4
SPLIT = 4
EXTRA = 16
EPSILON = 1e-05
BIG = 1e30
LOG2E = 1.4426950408889634


def dot(a, b, dims=((1,), (0,))):
    return lax.dot_general(a, b, (dims, ((), ())), preferred_element_type=F32)


def row_order(rows, nz, inverse):
    pieces = rows // (2 * nz)
    out_row = lax.broadcasted_iota(jnp.int32, (rows, rows), 0)
    in_row = lax.broadcasted_iota(jnp.int32, (rows, rows), 1)
    if inverse:
        out_row, in_row = in_row, out_row
    r = out_row % 2
    z = (out_row // 2) % nz
    piece = out_row // (2 * nz)
    return jnp.where(in_row == (z * pieces + piece) * 2 + r, 1.0, 0.0).astype(BF16)


def merge(parts):
    top = parts[0][1]
    for _, level in parts[1:]:
        top = jnp.maximum(top, level)
    total = None
    mixed = None
    for value, level in parts:
        weight = jnp.exp2(level - top)
        total = weight if total is None else total + weight
        mixed = value * weight if mixed is None else mixed + value * weight
    return mixed / total, top + jnp.log(total) * LOG2E


def packed(value, level):
    high = level.astype(BF16).astype(F32)
    middle = (level - high).astype(BF16).astype(F32)
    low = level - high - middle
    row = lax.broadcasted_iota(jnp.int32, (EXTRA, level.shape[1]), 0)
    tail = jnp.where(row == 0, high, jnp.where(row == 1, middle, jnp.where(row == 2, low, 0.0)))
    return value.astype(BF16), tail.astype(BF16)


def unpacked(message):
    return message[:HD].astype(F32), jnp.sum(message[HD:].astype(F32), axis=0, keepdims=True)


def kernel(
    n,
    nz,
    nx,
    sections,
    hid,
    gain,
    wq_hbm,
    wkv_hbm,
    wout_hbm,
    pool_hbm,
    table,
    count,
    out,
    wq,
    wkv,
    wout,
    kv,
    vt,
    stage_x,
    stage_n,
    stage_o,
    gbuf,
    xbuf,
    qbuf,
    fown,
    fbuf,
    ocs,
    ocr,
    own_out,
    own_level,
    oxs,
    oxr,
    ozs,
    ozr,
    att,
    ycs,
    ycr,
    yown,
    yxs,
    yxr,
    yzs,
    yzr,
    fin,
    finr,
    load_sem,
    kv_sem,
    az_s,
    az_r,
    ax_s,
    ax_r,
    ac_s,
    ac_r,
    qz_s,
    qz_r,
    qx_s,
    qx_r,
    qc_s,
    qc_r,
    f_s,
    f_r,
    oc_s,
    oc_r,
    ox_s,
    ox_r,
    oz_s,
    oz_r,
    yc_s,
    yc_r,
    yx_s,
    yx_r,
    yz_s,
    yz_r,
    sec_s,
    sec_r,
):
    kvh = nz
    span = 2 * n
    model = hid.shape[-1]
    wide = model // SPLIT
    thin = wide // 8
    pages = pool_hbm.shape[1]
    scale = HD ** (-0.5) * LOG2E

    me = lax.axis_index("kvp")
    section = lax.axis_index("section")
    c = me % CORES
    x = (me // CORES) % nx
    z = me // (CORES * nx)
    half = n // 2
    fresh_head = (me % half) // nx
    fresh_piece = (me // half) * nx + me % nx

    def at(zz, xx, cc):
        return (zz * nx + xx) * CORES + cc

    def remote(src, dst, send, recv, target):
        return pltpu.make_async_remote_copy(
            src_ref=src,
            dst_ref=dst,
            send_sem=send,
            recv_sem=recv,
            device_id={"kvp": target},
            device_id_type=MESH,
        )

    def to_z(d):
        return at((z + d) % nz, x, c)

    def to_x(d):
        return at(z, (x + d) % nx, c)

    peer = at(z, x, 1 - c)

    loads = [
        pltpu.make_async_copy(wq_hbm.at[0], wq, load_sem.at[0]),
        pltpu.make_async_copy(wkv_hbm.at[0], wkv, load_sem.at[1]),
        pltpu.make_async_copy(wout_hbm.at[0], wout, load_sem.at[2]),
    ]
    kv_loads = [
        pltpu.make_async_copy(pool_hbm.at[0, :, :, pl.ds(i * HD, HD)], kv.at[i], kv_sem.at[i])
        for i in range(2 * kvh)
    ]
    for load in loads[:2] + kv_loads + loads[2:]:
        load.start()

    barrier = pltpu.get_barrier_semaphore()

    def greet(target):
        pl.semaphore_signal(barrier, inc=1, device_id={"kvp": target}, device_id_type=MESH)

    for d in range(1, nz):
        greet(to_z(d))
    for d in range(1, nx):
        greet(to_x(d))
    greet(peer)
    for i in range(2 * nx):
        source = (i // nx) * half + z * nx + i % nx

        @pl.when(source != me)
        def _():
            greet(source)

    pl.semaphore_signal(
        barrier,
        inc=1,
        device_id={"section": (section + sections - 1) % sections},
        device_id_type=MESH,
    )

    values = hid[0].astype(F32)
    inv_rms = lax.rsqrt(jnp.mean(values * values, axis=-1, keepdims=True) + EPSILON)
    normed = (values * inv_rms * gain[...].astype(F32)).astype(BF16).astype(F32)
    for q in range(SPLIT):
        for j in range(8):
            start = q * wide + j * thin
            stage_n[q, 2 * j : 2 * j + 2, :] = normed[:, start : start + thin]
            stage_x[q, 2 * j : 2 * j + 2, :] = values[:, start : start + thin]
    for q in range(SPLIT):
        gbuf[q, z] = stage_n[q].astype(BF16)

    own_target = jnp.where(fresh_head == z, 1, 0)
    pl.semaphore_wait(barrier, (nz - 1) + (nx - 1) + 1 + 2 * nx + 1 - own_target)

    def az(q, d):
        return remote(gbuf.at[q, z], gbuf.at[q, z], az_s.at[q, d - 1], az_r.at[q, d - 1], to_z(d))

    def az_in(q, d):
        slot = gbuf.at[q, (z + nz - d) % nz]
        return remote(slot, slot, az_s.at[q, d - 1], az_r.at[q, d - 1], to_z(d))

    def ax(q, d):
        slot = xbuf.at[q, c, x]
        return remote(slot, slot, ax_s.at[q, d - 1], ax_r.at[q, d - 1], to_x(d))

    def ax_in(q, d):
        slot = xbuf.at[q, c, (x + nx - d) % nx]
        return remote(slot, slot, ax_s.at[q, d - 1], ax_r.at[q, d - 1], to_x(d))

    def ac(q):
        return remote(xbuf.at[q, c], xbuf.at[q, c], ac_s.at[q], ac_r.at[q], peer)

    def ac_in(q):
        return remote(xbuf.at[q, 1 - c], xbuf.at[q, 1 - c], ac_s.at[q], ac_r.at[q], peer)

    for q in range(SPLIT):
        for d in range(1, nz):
            az(q, d).start()

    for load in kv_loads:
        load.wait()

    @pl.loop(0, kvh)
    def _(g):
        vt[g] = kv[kvh + g].reshape(pages * HD, HD).T

    spread = row_order(16 * nz, nz, False)
    gather = row_order(16 * nz, nz, True)
    loads[0].wait()
    loads[1].wait()

    query = jnp.zeros((span, HD), F32)
    fresh = jnp.zeros((wkv.shape[0], span), F32)
    for t in range(SPLIT + 2):
        if t < SPLIT:
            for d in range(1, nz):
                az_in(t, d).wait_recv()
            rows = dot(spread, gbuf[t].reshape(16 * nz, thin)).astype(BF16)
            for j in range(8):
                xbuf[t, c, x, :, j * thin : (j + 1) * thin] = rows[j * 2 * nz : (j + 1) * 2 * nz]
            for d in range(1, nx):
                ax(t, d).start()
        if 1 <= t <= SPLIT:
            for d in range(1, nx):
                ax_in(t - 1, d).wait_recv()
            ac(t - 1).start()
        if t >= 2:
            q = t - 2
            ac_in(q).wait_recv()
            block = xbuf[q].reshape(span, wide)
            query = query + dot(block, wq[q * wide : (q + 1) * wide])
            fresh = fresh + dot(wkv[:, q * wide : (q + 1) * wide], block, ((1,), (1,)))

    qbuf[z, c, x] = query.T.astype(BF16)
    fown[...] = fresh.astype(BF16)

    def qz(d):
        slot = qbuf.at[z, c, x]
        return remote(slot, slot, qz_s.at[d - 1], qz_r.at[d - 1], to_z(d))

    def qz_in(g, d):
        slot = qbuf.at[g, c, x]
        return remote(slot, slot, qz_s.at[d - 1], qz_r.at[d - 1], to_z(d))

    def qx(g, d):
        slot = qbuf.at[g, c, x]
        return remote(slot, slot, qx_s.at[g, d - 1], qx_r.at[g, d - 1], to_x(d))

    def qx_in(g, d):
        slot = qbuf.at[g, c, (x + nx - d) % nx]
        return remote(slot, slot, qx_s.at[g, d - 1], qx_r.at[g, d - 1], to_x(d))

    def qc(g):
        return remote(qbuf.at[g, c], qbuf.at[g, c], qc_s.at[g], qc_r.at[g], peer)

    def qc_in(g):
        return remote(qbuf.at[g, 1 - c], qbuf.at[g, 1 - c], qc_s.at[g], qc_r.at[g], peer)

    def fresh_out(i):
        return remote(
            fown,
            fbuf.at[fresh_piece],
            f_s.at[i],
            f_r.at[fresh_piece],
            fresh_head * CORES * nx + i,
        )

    for d in range(1, nz):
        qz(d).start()
    for i in range(2 * nx):
        target = fresh_head * CORES * nx + i

        @pl.when(target != me)
        def _():
            fresh_out(i).start()

        @pl.when(target == me)
        def _():
            pltpu.make_async_copy(fown, fbuf.at[fresh_piece], f_r.at[fresh_piece]).start()

    bounds = []
    for slot in range(pages):
        bound = jnp.float32(BIG)
        for j in range(pages):
            named = jnp.logical_and(table[0, 0, j] == slot, j < count[0, 0])
            bound = jnp.where(named, jnp.float32(-BIG), bound)
        bounds.append(bound)

    def attend(g, side):
        cols = jnp.concatenate([qbuf[g, side, i] for i in range(nx)], axis=1)
        scores = dot(kv[g].reshape(pages * HD, HD), cols)
        parts = [scores[p * HD : (p + 1) * HD] for p in range(pages)]
        top = None
        for part, bound in zip(parts, bounds):
            here = jnp.minimum(jnp.max(part, axis=0, keepdims=True), -bound)
            top = here if top is None else jnp.maximum(top, here)
        total = None
        weights = []
        for part, bound in zip(parts, bounds):
            weight = jnp.exp2((part - jnp.maximum(top, bound)) * scale)
            add = jnp.sum(weight, axis=0, keepdims=True)
            total = add if total is None else total + add
            weights.append(weight.astype(BF16))
        mixed = dot(vt[g], jnp.concatenate(weights, axis=0))
        return mixed / total, top * scale + jnp.log(total) * LOG2E

    def oc(g):
        return remote(ocs.at[g], ocr.at[g], oc_s.at[g], oc_r.at[g], peer)

    def ox(g, d):
        return remote(
            oxs.at[g, (x + d) % nx], oxr.at[g, x], ox_s.at[g, d - 1], ox_r.at[g, d - 1], to_x(d)
        )

    def ox_in(g, d):
        slot = (x + nx - d) % nx
        return remote(
            oxs.at[g, slot], oxr.at[g, slot], ox_s.at[g, d - 1], ox_r.at[g, d - 1], to_x(d)
        )

    def oz(g, d):
        return remote(ozs.at[g], ozr.at[z], oz_s.at[d - 1], oz_r.at[d - 1], at(g, x, c))

    def oz_in(d):
        slot = (z + nz - d) % nz
        return remote(ozs.at[slot], ozr.at[slot], oz_s.at[d - 1], oz_r.at[d - 1], to_z(d))

    def offset(s):
        return (nz + ((s + 1) // 2) * (2 * (s % 2) - 1)) % nz

    @pl.loop(0, nz + 4)
    def _(t):
        @pl.when(t < nz)
        def _():
            d = offset(t)
            g = (z + d) % nz

            @pl.when(t > 0)
            def _():
                qz_in(g, nz - d).wait_recv()

            for e in range(1, nx):
                qx(g, e).start()

        @pl.when(jnp.logical_and(t >= 1, t < nz + 1))
        def _():
            g = (z + offset(t - 1)) % nz
            for e in range(1, nx):
                qx_in(g, e).wait_recv()
            qc(g).start()

        @pl.when(t >= 4)
        def _():
            d = offset(t - 4)
            g = (z + d) % nz
            for e in range(1, nx):
                ox_in(g, e).wait_recv()
            parts = [unpacked(oxs[g, x])]
            for e in range(1, nx):
                parts.append(unpacked(oxr[g, (x + e) % nx]))
            value, tail = packed(*merge(parts))
            ozs[g, :HD] = value
            ozs[g, HD:] = tail

            @pl.when(t > 4)
            def _():
                oz(g, d).start()

        @pl.when(jnp.logical_and(t >= 3, t < nz + 3))
        def _():
            g = (z + offset(t - 3)) % nz
            remote(ocs.at[g], ocr.at[g], oc_s.at[g], oc_r.at[g], peer).wait_recv()
            for i in range(nx):
                here = (own_out[:, i * span : (i + 1) * span], own_level[:, i * span : (i + 1) * span])
                value, tail = packed(*merge([here, unpacked(ocr[g, i])]))
                oxs[g, i, :HD] = value
                oxs[g, i, HD:] = tail
            for e in range(1, nx):
                ox(g, e).start()

        @pl.when(jnp.logical_and(t >= 2, t < nz + 2))
        def _():
            g = (z + offset(t - 2)) % nz
            qc_in(g).wait_recv()
            mixed, level = attend(g, 1 - c)
            for i in range(nx):
                value, tail = packed(
                    mixed[:, i * span : (i + 1) * span], level[:, i * span : (i + 1) * span]
                )
                ocs[g, i, :HD] = value
                ocs[g, i, HD:] = tail
            oc(g).start()
            mixed, level = attend(g, c)
            own_out[...] = mixed
            own_level[...] = level

    for i in range(2 * nx):
        remote(fown, fbuf.at[i], f_s.at[i], f_r.at[i], peer).wait_recv()
    new_keys = fbuf[:nx].reshape(HD, span)
    new_values = fbuf[nx:].reshape(HD, span)

    def token(axis):
        row = lax.broadcasted_iota(jnp.int32, (span, span), axis)
        r = row % 2
        tz = (row // 2) % nz
        tx = (row // (2 * nz)) % nx
        tc = row // (2 * nz * nx)
        return ((tz * nx + tx) * CORES + tc) * 2 + r

    causal = token(0) <= token(1)
    scores = dot(new_keys.T, qbuf[z, c, x])
    scores = jnp.where(causal, scores, -BIG)
    top = jnp.max(scores, axis=0, keepdims=True)
    weights = jnp.where(causal, jnp.exp2((scores - top) * scale), 0.0)
    total = jnp.sum(weights, axis=0, keepdims=True)
    own = dot(new_values, weights.astype(BF16)) / total
    parts = [(own, top * scale + jnp.log(total) * LOG2E), unpacked(ozs[z])]
    for d in range(1, nz):
        oz_in(d).wait_recv()
        parts.append(unpacked(ozr[(z + nz - d) % nz]))
    attention, _ = merge(parts)
    att[...] = attention.T.astype(BF16).reshape(CORES, span // CORES, HD)

    loads[2].wait()

    def yc(q):
        return remote(ycs.at[q], ycr.at[q], yc_s.at[q], yc_r.at[q], peer)

    def yx(q, d):
        return remote(
            yxs.at[q, (x + d) % nx], yxr.at[q, x], yx_s.at[q, d - 1], yx_r.at[q, d - 1], to_x(d)
        )

    def yx_in(q, d):
        slot = (x + nx - d) % nx
        return remote(
            yxs.at[q, slot], yxr.at[q, slot], yx_s.at[q, d - 1], yx_r.at[q, d - 1], to_x(d)
        )

    def yz(q, d):
        return remote(
            yzs.at[q, (z + d) % nz], yzr.at[q, z], yz_s.at[q, d - 1], yz_r.at[q, d - 1], to_z(d)
        )

    def yz_in(q, d):
        slot = (z + nz - d) % nz
        return remote(
            yzs.at[q, slot], yzr.at[q, slot], yz_s.at[q, d - 1], yz_r.at[q, d - 1], to_z(d)
        )

    def final(q):
        return pltpu.make_async_remote_copy(
            src_ref=fin.at[q],
            dst_ref=finr.at[q],
            send_sem=sec_s.at[q],
            recv_sem=sec_r.at[q],
            device_id={"section": (section + 1) % sections},
            device_id_type=MESH,
        )

    for t in range(SPLIT + 3):
        if t < SPLIT:
            weight = wout[:, t * wide : (t + 1) * wide]
            ycs[t] = dot(att[1 - c], weight).astype(BF16)
            yc(t).start()
            yown[t] = dot(att[c], weight)
        if 1 <= t <= SPLIT:
            q = t - 1
            yc(q).wait_recv()
            sums = yown[q] + ycr[q].astype(F32)
            yown[q] = sums
            yxs[q] = sums.astype(BF16).reshape(nx, 2 * nz, wide)
            for d in range(1, nx):
                yx(q, d).start()
        if 2 <= t <= SPLIT + 1:
            q = t - 2
            sums = yown[q, pl.ds(pl.multiple_of(x * 2 * nz, 2 * nz), 2 * nz)]
            for d in range(1, nx):
                yx_in(q, d).wait_recv()
                sums = sums + yxr[q, (x + nx - d) % nx].astype(F32)
            sums = sums.astype(BF16)
            rows = jnp.concatenate([sums[:, j * thin : (j + 1) * thin] for j in range(8)], axis=0)
            yzs[q] = dot(gather, rows).astype(BF16).reshape(nz, 16, thin)
            for d in range(1, nz):
                yz(q, d).start()
        if t >= 3:
            q = t - 3
            sums = yzs[q, z].astype(F32)
            for d in range(1, nz):
                yz_in(q, d).wait_recv()
                sums = sums + yzr[q, (z + nz - d) % nz].astype(F32)
            fin[q] = (stage_x[q] + sums).astype(BF16)
            final(q).start()

    for q in range(SPLIT):
        final(q).wait_recv()
        stage_o[...] = finr[q].astype(F32)
        for j in range(8):
            start = q * wide + j * thin
            out[0, :, start : start + thin] = stage_o[2 * j : 2 * j + 2, :].astype(BF16)

    for q in range(SPLIT):
        for d in range(1, nz):
            az(q, d).wait_send()
            yz(q, d).wait_send()
        for d in range(1, nx):
            ax(q, d).wait_send()
            yx(q, d).wait_send()
        ac(q).wait_send()
        yc(q).wait_send()
        final(q).wait_send()
    for d in range(1, nz):
        qz(d).wait_send()
        oz((z + d) % nz, d).wait_send()
    for g in range(nz):
        for d in range(1, nx):
            qx(g, d).wait_send()
            ox(g, d).wait_send()
        qc(g).wait_send()
        oc(g).wait_send()
    for i in range(2 * nx):

        @pl.when(fresh_head * CORES * nx + i != me)
        def _():
            fresh_out(i).wait_send()


def local(n, nx, sections, hidden, norm_gain, w_query, w_kv, w_out, doc_cache, page_table, page_count):
    nz = n // (CORES * nx)
    span = 2 * n
    model = hidden.shape[-1]
    wide = model // SPLIT
    thin = wide // 8
    fresh_rows = w_kv.shape[-1]
    pages = doc_cache.shape[1]
    tall = HD + EXTRA
    vmem = pl.BlockSpec(memory_space=pltpu.VMEM)
    smem = pl.BlockSpec(memory_space=pltpu.SMEM)
    anywhere = pl.BlockSpec(memory_space=pl.ANY)
    dma = pltpu.SemaphoreType.DMA

    def pair(*shape):
        return [dma(shape), dma(shape)]

    scratch = [
        pltpu.VMEM((model, HD), BF16),
        pltpu.VMEM((fresh_rows, model), BF16),
        pltpu.VMEM((HD, model), BF16),
        pltpu.VMEM((2 * nz, pages, HD, HD), BF16),
        pltpu.VMEM((nz, HD, pages * HD), BF16),
        pltpu.VMEM((SPLIT, 16, thin), F32),
        pltpu.VMEM((SPLIT, 16, thin), F32),
        pltpu.VMEM((16, thin), F32),
        pltpu.VMEM((SPLIT, nz, 16, thin), BF16),
        pltpu.VMEM((SPLIT, CORES, nx, 2 * nz, wide), BF16),
        pltpu.VMEM((nz, CORES, nx, HD, span), BF16),
        pltpu.VMEM((fresh_rows, span), BF16),
        pltpu.VMEM((2 * nx, fresh_rows, span), BF16),
        pltpu.VMEM((nz, nx, tall, span), BF16),
        pltpu.VMEM((nz, nx, tall, span), BF16),
        pltpu.VMEM((HD, nx * span), F32),
        pltpu.VMEM((1, nx * span), F32),
        pltpu.VMEM((nz, nx, tall, span), BF16),
        pltpu.VMEM((nz, nx, tall, span), BF16),
        pltpu.VMEM((nz, tall, span), BF16),
        pltpu.VMEM((nz, tall, span), BF16),
        pltpu.VMEM((CORES, span // CORES, HD), BF16),
        pltpu.VMEM((SPLIT, span // CORES, wide), BF16),
        pltpu.VMEM((SPLIT, span // CORES, wide), BF16),
        pltpu.VMEM((SPLIT, span // CORES, wide), F32),
        pltpu.VMEM((SPLIT, nx, 2 * nz, wide), BF16),
        pltpu.VMEM((SPLIT, nx, 2 * nz, wide), BF16),
        pltpu.VMEM((SPLIT, nz, 16, thin), BF16),
        pltpu.VMEM((SPLIT, nz, 16, thin), BF16),
        pltpu.VMEM((SPLIT, 16, thin), BF16),
        pltpu.VMEM((SPLIT, 16, thin), BF16),
        dma((3,)),
        dma((2 * nz,)),
        *pair(SPLIT, nz - 1),
        *pair(SPLIT, nx - 1),
        *pair(SPLIT),
        *pair(nz - 1),
        *pair(nz, nx - 1),
        *pair(nz),
        *pair(2 * nx),
        *pair(nz),
        *pair(nz, nx - 1),
        *pair(nz - 1),
        *pair(SPLIT),
        *pair(SPLIT, nx - 1),
        *pair(SPLIT, nz - 1),
        *pair(SPLIT),
    ]
    return pl.pallas_call(
        functools.partial(kernel, n, nz, nx, sections),
        out_shape=jax.ShapeDtypeStruct(hidden.shape, BF16),
        in_specs=[vmem, vmem, anywhere, anywhere, anywhere, anywhere, smem, smem],
        out_specs=vmem,
        scratch_shapes=scratch,
        compiler_params=pltpu.CompilerParams(
            collective_id=0, has_side_effects=True, vmem_limit_bytes=56 * 1024 * 1024
        ),
    )(hidden, norm_gain, w_query, jnp.swapaxes(w_kv, 1, 2), w_out, doc_cache, page_table, page_count)


def solution(mesh):
    placed = (
        P("section", "kvp", None),
        P("section", None),
        P("section", None, "kvp"),
        P("section", None, "kvp"),
        P("section", "kvp", None),
        P("section", "kvp", None, None),
        P("section", "kvp", None),
        P("section", "kvp"),
    )
    n = mesh.shape["kvp"]
    nx = RINGX if n >= 32 else 2
    return jax.shard_map(
        functools.partial(local, n, nx, mesh.shape["section"]),
        mesh=mesh,
        in_specs=placed,
        out_specs=P("section", "kvp", None),
        check_vma=False,
    )
```

```python
import functools
import math

import jax
import jax.numpy as jnp
from jax import lax
from jax.experimental import pallas as pl
from jax.experimental.pallas import tpu as pltpu
from jax.sharding import PartitionSpec as P

MESH = pl.DeviceIdType.MESH
F32 = jnp.float32
BF16 = jnp.bfloat16

HD = 128
CORES = 2
RINGX = 4
SPLIT = 4
EXTRA = 16
EPSILON = 1e-05
BIG = 1e30
LOG2E = 1.4426950408889634
LAG = 5


def dot(a, b, dims=((1,), (0,))):
    return lax.dot_general(a, b, (dims, ((), ())), preferred_element_type=F32)


def row_order(rows, nz, inverse):
    pieces = rows // (2 * nz)
    out_row = lax.broadcasted_iota(jnp.int32, (rows, rows), 0)
    in_row = lax.broadcasted_iota(jnp.int32, (rows, rows), 1)
    if inverse:
        out_row, in_row = in_row, out_row
    r = out_row % 2
    z = (out_row // 2) % nz
    piece = out_row // (2 * nz)
    return jnp.where(in_row == (z * pieces + piece) * 2 + r, 1.0, 0.0).astype(BF16)


def merge(parts):
    top = parts[0][1]
    for _, level in parts[1:]:
        top = jnp.maximum(top, level)
    total = None
    mixed = None
    for value, level in parts:
        weight = jnp.exp2(level - top)
        total = weight if total is None else total + weight
        mixed = value * weight if mixed is None else mixed + value * weight
    return mixed / total, top + jnp.log(total) * LOG2E


def packed(value, level):
    high = level.astype(BF16).astype(F32)
    middle = (level - high).astype(BF16).astype(F32)
    low = level - high - middle
    row = lax.broadcasted_iota(jnp.int32, (EXTRA, level.shape[1]), 0)
    tail = jnp.where(row == 0, high, jnp.where(row == 1, middle, jnp.where(row == 2, low, 0.0)))
    return value.astype(BF16), tail.astype(BF16)


def unpacked(message):
    return message[:HD].astype(F32), jnp.sum(message[HD:].astype(F32), axis=0, keepdims=True)


def kernel(
    n,
    nz,
    nx,
    sections,
    hid,
    gain,
    wq_hbm,
    wkv_hbm,
    wout_hbm,
    pool_hbm,
    table,
    count,
    out,
    wq,
    wkv,
    wout,
    kv,
    vt,
    stage_x,
    stage_n,
    stage_o,
    gbuf,
    xbuf,
    qbuf,
    fown,
    fbuf,
    ocs,
    ocr,
    own_out,
    own_level,
    oxs,
    oxr,
    ozs,
    ozr,
    att,
    ycs,
    ycr,
    yown,
    yxs,
    yxr,
    yzs,
    yzr,
    fin,
    finr,
    load_sem,
    kv_sem,
    az_s,
    az_r,
    ax_s,
    ax_r,
    ac_s,
    ac_r,
    qz_s,
    qz_r,
    qx_s,
    qx_r,
    qc_s,
    qc_r,
    f_s,
    f_r,
    oc_s,
    oc_r,
    ox_s,
    ox_r,
    oz_s,
    oz_r,
    yc_s,
    yc_r,
    yx_s,
    yx_r,
    yz_s,
    yz_r,
    sec_s,
    sec_r,
):
    kvh = nz
    span = 2 * n
    model = hid.shape[-1]
    wide = model // SPLIT
    thin = wide // 8
    pages = pool_hbm.shape[1]
    scale = HD ** (-0.5) * LOG2E

    me = lax.axis_index("kvp")
    section = lax.axis_index("section")
    c = me % CORES
    x = (me // CORES) % nx
    z = me // (CORES * nx)
    half = n // 2
    fresh_head = (me % half) // nx
    fresh_piece = (me // half) * nx + me % nx

    def at(zz, xx, cc):
        return (zz * nx + xx) * CORES + cc

    def remote(src, dst, send, recv, target):
        return pltpu.make_async_remote_copy(
            src_ref=src,
            dst_ref=dst,
            send_sem=send,
            recv_sem=recv,
            device_id={"kvp": target},
            device_id_type=MESH,
        )

    def to_z(d):
        return at((z + d) % nz, x, c)

    def to_x(d):
        return at(z, (x + d) % nx, c)

    peer = at(z, x, 1 - c)

    loads = [
        pltpu.make_async_copy(wq_hbm.at[0], wq, load_sem.at[0]),
        pltpu.make_async_copy(wkv_hbm.at[0], wkv, load_sem.at[1]),
        pltpu.make_async_copy(wout_hbm.at[0], wout, load_sem.at[2]),
    ]
    kv_loads = [
        pltpu.make_async_copy(pool_hbm.at[0, :, :, pl.ds(i * HD, HD)], kv.at[i], kv_sem.at[i])
        for i in range(2 * kvh)
    ]
    for load in loads[:2] + kv_loads + loads[2:]:
        load.start()

    barrier = pltpu.get_barrier_semaphore()

    def greet(target):
        pl.semaphore_signal(barrier, inc=1, device_id={"kvp": target}, device_id_type=MESH)

    for d in range(1, nz):
        greet(to_z(d))
    for d in range(1, nx):
        greet(to_x(d))
    greet(peer)
    for i in range(2 * nx):
        source = (i // nx) * half + z * nx + i % nx

        @pl.when(source != me)
        def _():
            greet(source)

    before = (section + sections - 1) % sections
    after = (section + 1) % sections
    for d in range(nz):
        pl.semaphore_signal(
            barrier, inc=1, device_id={"kvp": to_z(d), "section": before}, device_id_type=MESH
        )

    values = hid[0].astype(F32)
    inv_rms = lax.rsqrt(jnp.mean(values * values, axis=-1, keepdims=True) + EPSILON)
    normed = (values * inv_rms * gain[...].astype(F32)).astype(BF16).astype(F32)
    for q in range(SPLIT):
        for j in range(8):
            start = q * wide + j * thin
            stage_n[q, 2 * j : 2 * j + 2, :] = normed[:, start : start + thin]
            stage_x[q, 2 * j : 2 * j + 2, :] = values[:, start : start + thin]
    for q in range(SPLIT):
        gbuf[q, z] = stage_n[q].astype(BF16)
        fin[q] = stage_x[q].astype(BF16)

    own_target = jnp.where(fresh_head == z, 1, 0)
    pl.semaphore_wait(barrier, (nz - 1) + (nx - 1) + 1 + 2 * nx + nz - own_target)

    def residual():
        return pltpu.make_async_remote_copy(
            src_ref=fin,
            dst_ref=finr,
            send_sem=sec_s.at[0],
            recv_sem=sec_r.at[0],
            device_id={"section": after},
            device_id_type=MESH,
        )

    def az(q, d):
        return remote(gbuf.at[q, z], gbuf.at[q, z], az_s.at[q, d - 1], az_r.at[q, d - 1], to_z(d))

    def az_in(q, d):
        slot = gbuf.at[q, (z + nz - d) % nz]
        return remote(slot, slot, az_s.at[q, d - 1], az_r.at[q, d - 1], to_z(d))

    def ax(q, d):
        slot = xbuf.at[q, c, x]
        return remote(slot, slot, ax_s.at[q, d - 1], ax_r.at[q, d - 1], to_x(d))

    def ax_in(q, d):
        slot = xbuf.at[q, c, (x + nx - d) % nx]
        return remote(slot, slot, ax_s.at[q, d - 1], ax_r.at[q, d - 1], to_x(d))

    def ac(q):
        return remote(xbuf.at[q, c], xbuf.at[q, c], ac_s.at[q], ac_r.at[q], peer)

    def ac_in(q):
        return remote(xbuf.at[q, 1 - c], xbuf.at[q, 1 - c], ac_s.at[q], ac_r.at[q], peer)

    for q in range(SPLIT):
        for d in range(1, nz):
            az(q, d).start()

    residual().start()

    for load in kv_loads:
        load.wait()

    @pl.loop(0, kvh)
    def _(g):
        vt[g] = kv[kvh + g].reshape(pages * HD, HD).T

    spread = row_order(16 * nz, nz, False)
    gather = row_order(16 * nz, nz, True)
    loads[0].wait()
    loads[1].wait()

    query = jnp.zeros((span, HD), F32)
    fresh = jnp.zeros((wkv.shape[0], span), F32)
    for t in range(SPLIT + 2):
        if t < SPLIT:
            for d in range(1, nz):
                az_in(t, d).wait_recv()
            rows = dot(spread, gbuf[t].reshape(16 * nz, thin)).astype(BF16)
            for j in range(8):
                xbuf[t, c, x, :, j * thin : (j + 1) * thin] = rows[j * 2 * nz : (j + 1) * 2 * nz]
            for d in range(1, nx):
                ax(t, d).start()
        if 1 <= t <= SPLIT:
            for d in range(1, nx):
                ax_in(t - 1, d).wait_recv()
            ac(t - 1).start()
        if t >= 2:
            q = t - 2
            ac_in(q).wait_recv()
            block = xbuf[q].reshape(span, wide)
            query = query + dot(block, wq[q * wide : (q + 1) * wide])
            fresh = fresh + dot(wkv[:, q * wide : (q + 1) * wide], block, ((1,), (1,)))

    qbuf[z, c, x] = query.T.astype(BF16)
    fown[...] = fresh.astype(BF16)

    def qz(d):
        slot = qbuf.at[z, c, x]
        return remote(slot, slot, qz_s.at[d - 1], qz_r.at[d - 1], to_z(d))

    def qz_in(g, d):
        slot = qbuf.at[g, c, x]
        return remote(slot, slot, qz_s.at[d - 1], qz_r.at[d - 1], to_z(d))

    def qx(g, d):
        slot = qbuf.at[g, c, x]
        return remote(slot, slot, qx_s.at[g, d - 1], qx_r.at[g, d - 1], to_x(d))

    def qx_in(g, d):
        slot = qbuf.at[g, c, (x + nx - d) % nx]
        return remote(slot, slot, qx_s.at[g, d - 1], qx_r.at[g, d - 1], to_x(d))

    def qc(g):
        return remote(qbuf.at[g, c], qbuf.at[g, c], qc_s.at[g], qc_r.at[g], peer)

    def qc_in(g):
        return remote(qbuf.at[g, 1 - c], qbuf.at[g, 1 - c], qc_s.at[g], qc_r.at[g], peer)

    def fresh_out(i):
        return remote(
            fown,
            fbuf.at[fresh_piece],
            f_s.at[i],
            f_r.at[fresh_piece],
            fresh_head * CORES * nx + i,
        )

    for d in range(1, nz):
        qz(d).start()
    for i in range(2 * nx):
        target = fresh_head * CORES * nx + i

        @pl.when(target != me)
        def _():
            fresh_out(i).start()

        @pl.when(target == me)
        def _():
            pltpu.make_async_copy(fown, fbuf.at[fresh_piece], f_r.at[fresh_piece]).start()

    bounds = []
    for slot in range(pages):
        bound = jnp.float32(BIG)
        for j in range(pages):
            named = jnp.logical_and(table[0, 0, j] == slot, j < count[0, 0])
            bound = jnp.where(named, jnp.float32(-BIG), bound)
        bounds.append(bound)

    def attend(g, side):
        cols = jnp.concatenate([qbuf[g, side, i] for i in range(nx)], axis=1)
        scores = dot(kv[g].reshape(pages * HD, HD), cols)
        parts = [scores[p * HD : (p + 1) * HD] for p in range(pages)]
        top = None
        for part, bound in zip(parts, bounds):
            here = jnp.minimum(jnp.max(part, axis=0, keepdims=True), -bound)
            top = here if top is None else jnp.maximum(top, here)
        total = None
        weights = []
        for part, bound in zip(parts, bounds):
            weight = jnp.exp2((part - jnp.maximum(top, bound)) * scale)
            add = jnp.sum(weight, axis=0, keepdims=True)
            total = add if total is None else total + add
            weights.append(weight.astype(BF16))
        mixed = dot(vt[g], jnp.concatenate(weights, axis=0))
        return mixed / total, top * scale + jnp.log(total) * LOG2E

    def oc(g):
        return remote(ocs.at[g], ocr.at[g], oc_s.at[g], oc_r.at[g], peer)

    def ox(g, d):
        return remote(
            oxs.at[g, (x + d) % nx], oxr.at[g, x], ox_s.at[g, d - 1], ox_r.at[g, d - 1], to_x(d)
        )

    def ox_in(g, d):
        slot = (x + nx - d) % nx
        return remote(
            oxs.at[g, slot], oxr.at[g, slot], ox_s.at[g, d - 1], ox_r.at[g, d - 1], to_x(d)
        )

    def oz(g, d):
        return remote(ozs.at[g], ozr.at[z], oz_s.at[d - 1], oz_r.at[d - 1], at(g, x, c))

    def oz_in(d):
        slot = (z + nz - d) % nz
        return remote(ozs.at[slot], ozr.at[slot], oz_s.at[d - 1], oz_r.at[d - 1], to_z(d))

    def offset(s):
        return (nz + ((s + 1) // 2) * (2 * (s % 2) - 1)) % nz

    @pl.loop(0, nz)
    def _(t):
        d = offset(t)
        g = (z + d) % nz

        @pl.when(t > 0)
        def _():
            qz_in(g, nz - d).wait_recv()

        for e in range(1, nx):
            qx(g, e).start()

    @pl.loop(0, nz + LAG)
    def _(t):
        @pl.when(t < nz)
        def _():
            g = (z + offset(t)) % nz
            for e in range(1, nx):
                qx_in(g, e).wait_recv()
            qc(g).start()

        @pl.when(jnp.logical_and(t >= 2, t < nz + 2))
        def _():
            g = (z + offset(t - 2)) % nz
            oc(g).wait_recv()
            for i in range(nx):
                here = (own_out[:, i * span : (i + 1) * span], own_level[:, i * span : (i + 1) * span])
                value, tail = packed(*merge([here, unpacked(ocr[g, i])]))
                oxs[g, i, :HD] = value
                oxs[g, i, HD:] = tail
            for e in range(1, nx):
                ox(g, e).start()

        @pl.when(jnp.logical_and(t >= 1, t < nz + 1))
        def _():
            g = (z + offset(t - 1)) % nz
            qc_in(g).wait_recv()
            mixed, level = attend(g, 1 - c)
            for i in range(nx):
                value, tail = packed(
                    mixed[:, i * span : (i + 1) * span], level[:, i * span : (i + 1) * span]
                )
                ocs[g, i, :HD] = value
                ocs[g, i, HD:] = tail
            oc(g).start()
            mixed, level = attend(g, c)
            own_out[...] = mixed
            own_level[...] = level

        @pl.when(t >= LAG)
        def _():
            d = offset(t - LAG)
            g = (z + d) % nz
            for e in range(1, nx):
                ox_in(g, e).wait_recv()
            parts = [unpacked(oxs[g, x])]
            for e in range(1, nx):
                parts.append(unpacked(oxr[g, (x + e) % nx]))
            value, tail = packed(*merge(parts))
            ozs[g, :HD] = value
            ozs[g, HD:] = tail

            @pl.when(t > LAG)
            def _():
                oz(g, d).start()

    for i in range(2 * nx):
        remote(fown, fbuf.at[i], f_s.at[i], f_r.at[i], peer).wait_recv()
    new_keys = fbuf[:nx].reshape(HD, span)
    new_values = fbuf[nx:].reshape(HD, span)

    def token(axis):
        row = lax.broadcasted_iota(jnp.int32, (span, span), axis)
        r = row % 2
        tz = (row // 2) % nz
        tx = (row // (2 * nz)) % nx
        tc = row // (2 * nz * nx)
        return ((tz * nx + tx) * CORES + tc) * 2 + r

    causal = token(0) <= token(1)
    scores = dot(new_keys.T, qbuf[z, c, x])
    scores = jnp.where(causal, scores, -BIG)
    top = jnp.max(scores, axis=0, keepdims=True)
    weights = jnp.where(causal, jnp.exp2((scores - top) * scale), 0.0)
    total = jnp.sum(weights, axis=0, keepdims=True)
    own = dot(new_values, weights.astype(BF16)) / total
    parts = [(own, top * scale + jnp.log(total) * LOG2E), unpacked(ozs[z])]
    for d in range(1, nz):
        oz_in(d).wait_recv()
        parts.append(unpacked(ozr[(z + nz - d) % nz]))
    attention, _ = merge(parts)
    att[...] = attention.T.astype(BF16).reshape(CORES, span // CORES, HD)

    loads[2].wait()

    def yc(q):
        return remote(ycs.at[q], ycr.at[q], yc_s.at[q], yc_r.at[q], peer)

    def yx(q, d):
        return remote(
            yxs.at[q, (x + d) % nx], yxr.at[q, x], yx_s.at[q, d - 1], yx_r.at[q, d - 1], to_x(d)
        )

    def yx_in(q, d):
        slot = (x + nx - d) % nx
        return remote(
            yxs.at[q, slot], yxr.at[q, slot], yx_s.at[q, d - 1], yx_r.at[q, d - 1], to_x(d)
        )

    def yz(q, d):
        return pltpu.make_async_remote_copy(
            src_ref=yzs.at[q, (z + d) % nz],
            dst_ref=yzr.at[q, z],
            send_sem=yz_s.at[q, d],
            recv_sem=yz_r.at[q, d],
            device_id={"kvp": to_z(d), "section": after},
            device_id_type=MESH,
        )

    def yz_in(q, d):
        slot = (z + nz - d) % nz
        return remote(yzs.at[q, slot], yzr.at[q, slot], yz_s.at[q, d], yz_r.at[q, d], peer)

    for t in range(SPLIT + 2):
        if t < SPLIT:
            weight = wout[:, t * wide : (t + 1) * wide]
            ycs[t] = dot(att[1 - c], weight).astype(BF16)
            yc(t).start()
            yown[t] = dot(att[c], weight)
        if 1 <= t <= SPLIT:
            q = t - 1
            yc(q).wait_recv()
            sums = yown[q] + ycr[q].astype(F32)
            yown[q] = sums
            yxs[q] = sums.astype(BF16).reshape(nx, 2 * nz, wide)
            for d in range(1, nx):
                yx(q, d).start()
        if 2 <= t <= SPLIT + 1:
            q = t - 2
            sums = yown[q, pl.ds(pl.multiple_of(x * 2 * nz, 2 * nz), 2 * nz)]
            for d in range(1, nx):
                yx_in(q, d).wait_recv()
                sums = sums + yxr[q, (x + nx - d) % nx].astype(F32)
            sums = sums.astype(BF16)
            rows = jnp.concatenate([sums[:, j * thin : (j + 1) * thin] for j in range(8)], axis=0)
            yzs[q] = dot(gather, rows).astype(BF16).reshape(nz, 16, thin)
            for d in range(nz):
                yz(q, (d + 1) % nz).start()

    residual().wait_recv()
    for q in range(SPLIT):
        sums = finr[q].astype(F32)
        for d in range(nz):
            yz_in(q, d).wait_recv()
            sums = sums + yzr[q, (z + nz - d) % nz].astype(F32)
        stage_o[...] = sums
        for j in range(8):
            start = q * wide + j * thin
            out[0, :, start : start + thin] = stage_o[2 * j : 2 * j + 2, :].astype(BF16)

    for q in range(SPLIT):
        for d in range(1, nz):
            az(q, d).wait_send()
        for d in range(nz):
            yz(q, d).wait_send()
        for d in range(1, nx):
            ax(q, d).wait_send()
            yx(q, d).wait_send()
        ac(q).wait_send()
        yc(q).wait_send()
    residual().wait_send()
    for d in range(1, nz):
        qz(d).wait_send()
        oz((z + d) % nz, d).wait_send()
    for g in range(nz):
        for d in range(1, nx):
            qx(g, d).wait_send()
            ox(g, d).wait_send()
        qc(g).wait_send()
        oc(g).wait_send()
    for i in range(2 * nx):

        @pl.when(fresh_head * CORES * nx + i != me)
        def _():
            fresh_out(i).wait_send()


def local(n, nx, sections, hidden, norm_gain, w_query, w_kv, w_out, doc_cache, page_table, page_count):
    nz = n // (CORES * nx)
    span = 2 * n
    model = hidden.shape[-1]
    wide = model // SPLIT
    thin = wide // 8
    fresh_rows = w_kv.shape[-1]
    pages = doc_cache.shape[1]
    tall = HD + EXTRA
    vmem = pl.BlockSpec(memory_space=pltpu.VMEM)
    smem = pl.BlockSpec(memory_space=pltpu.SMEM)
    anywhere = pl.BlockSpec(memory_space=pl.ANY)
    dma = pltpu.SemaphoreType.DMA

    def pair(*shape):
        return [dma(shape), dma(shape)]

    scratch = [
        pltpu.VMEM((model, HD), BF16),
        pltpu.VMEM((fresh_rows, model), BF16),
        pltpu.VMEM((HD, model), BF16),
        pltpu.VMEM((2 * nz, pages, HD, HD), BF16),
        pltpu.VMEM((nz, HD, pages * HD), BF16),
        pltpu.VMEM((SPLIT, 16, thin), F32),
        pltpu.VMEM((SPLIT, 16, thin), F32),
        pltpu.VMEM((16, thin), F32),
        pltpu.VMEM((SPLIT, nz, 16, thin), BF16),
        pltpu.VMEM((SPLIT, CORES, nx, 2 * nz, wide), BF16),
        pltpu.VMEM((nz, CORES, nx, HD, span), BF16),
        pltpu.VMEM((fresh_rows, span), BF16),
        pltpu.VMEM((2 * nx, fresh_rows, span), BF16),
        pltpu.VMEM((nz, nx, tall, span), BF16),
        pltpu.VMEM((nz, nx, tall, span), BF16),
        pltpu.VMEM((HD, nx * span), F32),
        pltpu.VMEM((1, nx * span), F32),
        pltpu.VMEM((nz, nx, tall, span), BF16),
        pltpu.VMEM((nz, nx, tall, span), BF16),
        pltpu.VMEM((nz, tall, span), BF16),
        pltpu.VMEM((nz, tall, span), BF16),
        pltpu.VMEM((CORES, span // CORES, HD), BF16),
        pltpu.VMEM((SPLIT, span // CORES, wide), BF16),
        pltpu.VMEM((SPLIT, span // CORES, wide), BF16),
        pltpu.VMEM((SPLIT, span // CORES, wide), F32),
        pltpu.VMEM((SPLIT, nx, 2 * nz, wide), BF16),
        pltpu.VMEM((SPLIT, nx, 2 * nz, wide), BF16),
        pltpu.VMEM((SPLIT, nz, 16, thin), BF16),
        pltpu.VMEM((SPLIT, nz, 16, thin), BF16),
        pltpu.VMEM((SPLIT, 16, thin), BF16),
        pltpu.VMEM((SPLIT, 16, thin), BF16),
        dma((3,)),
        dma((2 * nz,)),
        *pair(SPLIT, nz - 1),
        *pair(SPLIT, nx - 1),
        *pair(SPLIT),
        *pair(nz - 1),
        *pair(nz, nx - 1),
        *pair(nz),
        *pair(2 * nx),
        *pair(nz),
        *pair(nz, nx - 1),
        *pair(nz - 1),
        *pair(SPLIT),
        *pair(SPLIT, nx - 1),
        *pair(SPLIT, nz),
        *pair(1),
    ]
    return pl.pallas_call(
        functools.partial(kernel, n, nz, nx, sections),
        out_shape=jax.ShapeDtypeStruct(hidden.shape, BF16),
        in_specs=[vmem, vmem, anywhere, anywhere, anywhere, anywhere, smem, smem],
        out_specs=vmem,
        scratch_shapes=scratch,
        compiler_params=pltpu.CompilerParams(
            collective_id=0, has_side_effects=True, vmem_limit_bytes=56 * 1024 * 1024
        ),
    )(hidden, norm_gain, w_query, jnp.swapaxes(w_kv, 1, 2), w_out, doc_cache, page_table, page_count)


def solution(mesh):
    placed = (
        P("section", "kvp", None),
        P("section", None),
        P("section", None, "kvp"),
        P("section", None, "kvp"),
        P("section", "kvp", None),
        P("section", "kvp", None, None),
        P("section", "kvp", None),
        P("section", "kvp"),
    )
    n = mesh.shape["kvp"]
    nx = RINGX if n >= 32 else 2
    return jax.shard_map(
        functools.partial(local, n, nx, mesh.shape["section"]),
        mesh=mesh,
        in_specs=placed,
        out_specs=P("section", "kvp", None),
        check_vma=False,
    )
```

```python
import functools
import math

import jax
import jax.numpy as jnp
from jax import lax
from jax.experimental import pallas as pl
from jax.experimental.pallas import tpu as pltpu
from jax.sharding import PartitionSpec as P

MESH = pl.DeviceIdType.MESH
F32 = jnp.float32
BF16 = jnp.bfloat16

HD = 128
CORES = 2
RINGX = 4
SPLIT = 4
MAIN = 96
EPSILON = 1e-05
BIG = 1e30
LOG2E = 1.4426950408889634
AHEAD = 3
PASS = 3
LAG = 8


def dot(a, b, dims=((1,), (0,))):
    return lax.dot_general(a, b, (dims, ((), ())), preferred_element_type=F32)


def row_order(rows, nz, inverse):
    pieces = rows // (2 * nz)
    out_row = lax.broadcasted_iota(jnp.int32, (rows, rows), 0)
    in_row = lax.broadcasted_iota(jnp.int32, (rows, rows), 1)
    if inverse:
        out_row, in_row = in_row, out_row
    r = out_row % 2
    z = (out_row // 2) % nz
    piece = out_row // (2 * nz)
    return jnp.where(in_row == (z * pieces + piece) * 2 + r, 1.0, 0.0).astype(BF16)


def merge(parts):
    top = parts[0][1]
    for _, level in parts[1:]:
        top = jnp.maximum(top, level)
    total = None
    mixed = None
    for value, level in parts:
        weight = jnp.exp2(level - top)
        total = weight if total is None else total + weight
        mixed = value * weight if mixed is None else mixed + value * weight
    return mixed * (1.0 / total), top + jnp.log(total) * LOG2E


def kernel(
    n,
    nz,
    nx,
    sections,
    hid,
    gain,
    wq_hbm,
    wkv_hbm,
    wout_hbm,
    pool_hbm,
    table,
    count,
    out,
    wq,
    wkv,
    wout,
    kv,
    vt,
    stage_x,
    stage_n,
    stage_o,
    gbuf,
    hbuf,
    xbuf,
    qbuf,
    fown,
    fbuf,
    ocs,
    ocr,
    lcs,
    lcr,
    own_out,
    own_level,
    oxs,
    oxr,
    lxs,
    lxr,
    ozs,
    ozr,
    lzs,
    lzr,
    pzs,
    pzr,
    mzs,
    mzr,
    pxs,
    pxr,
    mxs,
    mxr,
    att,
    ycs,
    ycr,
    yown,
    yxs,
    yxr,
    yzs,
    yzr,
    vzs,
    vzr,
    vxs,
    vxr,
    fin,
    finr,
    load_sem,
    kv_sem,
    az_s,
    az_r,
    ax_s,
    ax_r,
    ac_s,
    ac_r,
    hx_s,
    hx_r,
    hz_s,
    hz_r,
    qz_s,
    qz_r,
    qx_s,
    qx_r,
    qc_s,
    qc_r,
    rx_s,
    rx_r,
    rz_s,
    rz_r,
    f_s,
    f_r,
    oc_s,
    oc_r,
    lc_s,
    lc_r,
    ox_s,
    ox_r,
    lx_s,
    lx_r,
    oz_s,
    oz_r,
    lz_s,
    lz_r,
    pz_s,
    pz_r,
    mz_s,
    mz_r,
    px_s,
    px_r,
    mx_s,
    mx_r,
    yc_s,
    yc_r,
    yx_s,
    yx_r,
    yz_s,
    yz_r,
    vz_s,
    vz_r,
    vx_s,
    vx_r,
    sec_s,
    sec_r,
):
    kvh = nz
    span = 2 * n
    model = hid.shape[-1]
    wide = model // SPLIT
    thin = wide // 8
    pages = pool_hbm.shape[1]
    scale = HD ** (-0.5) * LOG2E

    me = lax.axis_index("kvp")
    section = lax.axis_index("section")
    c = me % CORES
    x = (me // CORES) % nx
    z = me // (CORES * nx)
    half = n // 2
    fresh_head = (me % half) // nx
    fresh_piece = (me // half) * nx + me % nx

    def at(zz, xx, cc):
        return (zz * nx + xx) * CORES + cc

    peer = at(z, x, 1 - c)

    def remote(src, dst, send, recv, target):
        return pltpu.make_async_remote_copy(
            src_ref=src,
            dst_ref=dst,
            send_sem=send,
            recv_sem=recv,
            device_id={"kvp": target},
            device_id_type=MESH,
        )

    def arrived(region, sem):
        remote(region, region, sem, sem, peer).wait_recv()

    def left(region, sem):
        remote(region, region, sem, sem, peer).wait_send()

    def to_z(d):
        return at((z + d) % nz, x, c)

    def to_x(d):
        return at(z, (x + d) % nx, c)

    loads = [
        pltpu.make_async_copy(wq_hbm.at[0], wq, load_sem.at[0]),
        pltpu.make_async_copy(wkv_hbm.at[0], wkv, load_sem.at[1]),
        pltpu.make_async_copy(wout_hbm.at[0], wout, load_sem.at[2]),
    ]
    kv_loads = [
        pltpu.make_async_copy(pool_hbm.at[0, :, :, pl.ds(i * HD, HD)], kv.at[i], kv_sem.at[0])
        for i in range(2 * kvh)
    ]
    for load in loads[:2] + kv_loads + loads[2:]:
        load.start()

    barrier = pltpu.get_barrier_semaphore()

    def greet(target):
        pl.semaphore_signal(barrier, inc=1, device_id={"kvp": target}, device_id_type=MESH)

    for d in range(1, nz):
        greet(to_z(d))
    for d in range(1, nx):
        greet(to_x(d))
    greet(peer)
    before = (section + sections - 1) % sections
    after = (section + 1) % sections
    pl.semaphore_signal(barrier, inc=1, device_id={"section": before}, device_id_type=MESH)

    values = hid[0].astype(F32)
    inv_rms = lax.rsqrt(jnp.mean(values * values, axis=-1, keepdims=True) + EPSILON)
    normed = (values * inv_rms * gain[...].astype(F32)).astype(BF16).astype(F32)
    for q in range(SPLIT):
        for j in range(8):
            start = q * wide + j * thin
            stage_n[q, 2 * j : 2 * j + 2, :] = normed[:, start : start + thin]
            stage_x[q, 2 * j : 2 * j + 2, :] = values[:, start : start + thin]
    for q in range(SPLIT):
        if q > 0:
            gbuf[q, z] = stage_n[q].astype(BF16)
        else:
            hbuf[z, x] = stage_n[q].astype(BF16)
        fin[q] = stage_x[q].astype(BF16)

    pl.semaphore_wait(barrier, (nz - 1) + (nx - 1) + 1 + 1)

    def residual():
        return pltpu.make_async_remote_copy(
            src_ref=fin,
            dst_ref=finr,
            send_sem=sec_s.at[0],
            recv_sem=sec_r.at[0],
            device_id={"section": after},
            device_id_type=MESH,
        )

    def az(q, d):
        return remote(gbuf.at[q, z], gbuf.at[q, z], az_s.at[0], az_r.at[q], to_z(d))

    def ax(q, d):
        slot = xbuf.at[q, c, x]
        return remote(slot, slot, ax_s.at[0], ax_r.at[q], to_x(d))

    def ac(q):
        return remote(xbuf.at[q, c], xbuf.at[q, c], ac_s.at[0], ac_r.at[q], peer)

    def hx(d):
        return remote(hbuf.at[z, x], hbuf.at[z, x], hx_s.at[0], hx_r.at[0], to_x(d))

    def hz(d):
        return remote(hbuf.at[z], hbuf.at[z], hz_s.at[0], hz_r.at[0], to_z(d))

    for d in range(1, nx):
        hx(d).start()
    for q in range(1, SPLIT):
        for d in range(1, nz):
            az(q, d).start()
    arrived(hbuf.at[0, pl.ds(0, nx - 1)], hx_r.at[0])
    for d in range(1, nz):
        hz(d).start()
    residual().start()

    pltpu.make_async_copy(kv, kv, kv_sem.at[0]).wait()

    @pl.loop(0, kvh)
    def _(g):
        vt[g] = kv[kvh + g].reshape(pages * HD, HD).T

    spread = row_order(16 * nz, nz, False)
    gather = row_order(16 * nz, nz, True)
    loads[0].wait()
    loads[1].wait()

    query = jnp.zeros((span, HD), F32)
    fresh = jnp.zeros((wkv.shape[0], span), F32)
    order = [*range(1, SPLIT), 0]
    for t in range(SPLIT + 2):
        if t < SPLIT - 1:
            q = order[t]
            arrived(gbuf.at[q, pl.ds(0, nz - 1)], az_r.at[q])
            rows = dot(spread, gbuf[q].reshape(16 * nz, thin)).astype(BF16)
            for j in range(8):
                xbuf[q, c, x, :, j * thin : (j + 1) * thin] = rows[j * 2 * nz : (j + 1) * 2 * nz]
            for d in range(1, nx):
                ax(q, d).start()
        elif t == SPLIT - 1:
            arrived(hbuf.at[pl.ds(0, nz - 1)], hz_r.at[0])
            for i in range(nx):
                block = jnp.concatenate([hbuf[k, i] for k in range(nz)], axis=0)
                rows = dot(spread, block).astype(BF16)
                for j in range(8):
                    xbuf[0, c, i, :, j * thin : (j + 1) * thin] = rows[j * 2 * nz : (j + 1) * 2 * nz]
            ac(0).start()
        if 1 <= t <= SPLIT - 1:
            q = order[t - 1]
            arrived(xbuf.at[q, 0, pl.ds(0, nx - 1)], ax_r.at[q])
            ac(q).start()
        if t >= 2:
            q = order[t - 2]
            arrived(xbuf.at[q, 0], ac_r.at[q])
            block = xbuf[q].reshape(span, wide)
            query = query + dot(block, wq[q * wide : (q + 1) * wide])
            fresh = fresh + dot(wkv[:, q * wide : (q + 1) * wide], block, ((1,), (1,)))

    qbuf[z, c, x] = query.T.astype(BF16)
    fown[...] = fresh.astype(BF16)

    def qz(d):
        slot = qbuf.at[z, c, x, pl.ds(0, MAIN)]
        return remote(slot, slot, qz_s.at[0], qz_r.at[d - 1], to_z(d))

    def qx(g, d):
        slot = qbuf.at[g, c, x, pl.ds(0, MAIN)]
        return remote(slot, slot, qx_s.at[0], qx_r.at[g], to_x(d))

    def rx(d):
        slot = qbuf.at[z, c, x, pl.ds(MAIN, HD - MAIN)]
        return remote(slot, slot, rx_s.at[0], rx_r.at[0], to_x(d))

    def rz(d):
        slot = qbuf.at[z, c, :, pl.ds(MAIN, HD - MAIN)]
        return remote(slot, slot, rz_s.at[0], rz_r.at[d - 1], to_z(d))

    def qc(g):
        return remote(qbuf.at[g, c], qbuf.at[g, c], qc_s.at[0], qc_r.at[g], peer)

    def fresh_out(i):
        return remote(
            fown,
            fbuf.at[fresh_piece],
            f_s.at[0],
            f_r.at[0],
            fresh_head * CORES * nx + i,
        )

    for d in range(1, nx):
        rx(d).start()
    for d in range(1, nz):
        qz(d).start()
    for d in range(1, nx):
        qx(z, d).start()
    for i in range(2 * nx):
        target = fresh_head * CORES * nx + i

        @pl.when(target != me)
        def _():
            fresh_out(i).start()

        @pl.when(target == me)
        def _():
            pltpu.make_async_copy(fown, fbuf.at[fresh_piece], f_r.at[0]).start()

    bounds = []
    for slot in range(pages):
        bound = jnp.float32(BIG)
        for j in range(pages):
            named = jnp.logical_and(table[0, 0, j] == slot, j < count[0, 0])
            bound = jnp.where(named, jnp.float32(-BIG), bound)
        bounds.append(bound)

    def attend(g, side):
        cols = jnp.concatenate([qbuf[g, side, i] for i in range(nx)], axis=1)
        scores = dot(kv[g].reshape(pages * HD, HD), cols)
        parts = [scores[p * HD : (p + 1) * HD] for p in range(pages)]
        top = None
        for part, bound in zip(parts, bounds):
            here = jnp.minimum(jnp.max(part, axis=0, keepdims=True), -bound)
            top = here if top is None else jnp.maximum(top, here)
        total = None
        weights = []
        for part, bound in zip(parts, bounds):
            weight = jnp.exp2((part - jnp.maximum(top, bound)) * scale)
            add = jnp.sum(weight, axis=0, keepdims=True)
            total = add if total is None else total + add
            weights.append(weight.astype(BF16))
        mixed = dot(vt[g], jnp.concatenate(weights, axis=0)) * (1.0 / total)
        return mixed, top * scale + jnp.log(total) * LOG2E

    def oc(g):
        return remote(ocs.at[g], ocr.at[g], oc_s.at[0], oc_r.at[g], peer)

    def lc(g):
        return remote(lcs.at[g], lcr.at[g], lc_s.at[0], lc_r.at[g], peer)

    def along_x(send, recv, send_sem, recv_sem):
        def out_copy(g, d):
            return remote(
                send.at[g, (x + d) % nx], recv.at[g, x], send_sem.at[0], recv_sem.at[g], to_x(d)
            )

        return out_copy, lambda g: arrived(recv.at[g, pl.ds(0, nx - 1)], recv_sem.at[g])

    def along_z(send, recv, send_sem, recv_sem):
        def out_copy(g):
            return remote(send.at[g], recv.at[z], send_sem.at[0], recv_sem.at[0], at(g, x, c))

        return out_copy, lambda: arrived(recv.at[pl.ds(0, nz - 1)], recv_sem.at[0])

    ox, ox_in = along_x(oxs, oxr, ox_s, ox_r)
    lx, lx_in = along_x(lxs, lxr, lx_s, lx_r)
    oz, oz_in = along_z(ozs, ozr, oz_s, oz_r)
    lz, lz_in = along_z(lzs, lzr, lz_s, lz_r)
    pz, pz_in = along_z(pzs, pzr, pz_s, pz_r)
    mz, mz_in = along_z(mzs, mzr, mz_s, mz_r)
    px, px_in = along_x(pxs, pxr, px_s, px_r)
    mx, mx_in = along_x(mxs, mxr, mx_s, mx_r)

    def offset(s):
        return (nz + ((s + 1) // 2) * (2 * (s % 2) - 1)) % nz

    def forward(s):
        d = offset(s)
        g = (z + d) % nz
        arrived(qbuf.at[g, 0, 0, pl.ds(0, MAIN)], qz_r.at[nz - d - 1])
        for e in range(1, nx):
            qx(g, e).start()

    arrived(qbuf.at[0, 0, pl.ds(0, nx - 1), pl.ds(MAIN, HD - MAIN)], rx_r.at[0])
    for d in range(1, nz):
        rz(d).start()
    for s in range(1, min(AHEAD, nz)):
        forward(s)

    @pl.loop(0, nz + LAG)
    def _(t):
        @pl.when(t < nz)
        def _():
            d = offset(t)
            g = (z + d) % nz
            arrived(qbuf.at[g, 0, pl.ds(0, nx - 1), pl.ds(0, MAIN)], qx_r.at[g])

            @pl.when(t > 0)
            def _():
                arrived(qbuf.at[g, 0, :, pl.ds(MAIN, HD - MAIN)], rz_r.at[nz - d - 1])

            qc(g).start()

        @pl.when(t < nz - AHEAD)
        def _():
            forward(t + AHEAD)

        @pl.when(jnp.logical_and(t >= PASS, t < nz + PASS))
        def _():
            d = offset(t - PASS)
            g = (z + d) % nz
            slot = (t - PASS) % (PASS - 1)
            arrived(ocr.at[g], oc_r.at[g])
            arrived(lcr.at[g], lc_r.at[g])
            for i in range(nx):
                cols = slice(i * span, (i + 1) * span)
                here = (own_out[slot, :, cols], own_level[slot, :, cols])
                value, level = merge([here, (ocr[g, i].astype(F32), lcr[g, i])])
                oxs[g, i] = value[:MAIN].astype(BF16)
                lxs[g, i] = level
                pzs[g, i] = value[MAIN:].astype(BF16)
                mzs[g, i] = level
            for e in range(1, nx):
                ox(g, e).start()
                lx(g, e).start()

            @pl.when(t > PASS)
            def _():
                pz(g).start()
                mz(g).start()

        @pl.when(jnp.logical_and(t >= 1, t < nz + 1))
        def _():
            g = (z + offset(t - 1)) % nz
            slot = (t - 1) % (PASS - 1)
            arrived(qbuf.at[g, 0], qc_r.at[g])
            mixed, level = attend(g, 1 - c)
            for i in range(nx):
                cols = slice(i * span, (i + 1) * span)
                ocs[g, i] = mixed[:, cols].astype(BF16)
                lcs[g, i] = level[:, cols]
            oc(g).start()
            lc(g).start()
            mixed, level = attend(g, c)
            own_out[slot] = mixed
            own_level[slot] = level

        @pl.when(t >= LAG)
        def _():
            d = offset(t - LAG)
            g = (z + d) % nz
            ox_in(g)
            lx_in(g)
            parts = [(oxs[g, x].astype(F32), lxs[g, x])]
            for e in range(1, nx):
                slot = (x + e) % nx
                parts.append((oxr[g, slot].astype(F32), lxr[g, slot]))
            value, level = merge(parts)
            ozs[g] = value.astype(BF16)
            lzs[g] = level

            @pl.when(t > LAG)
            def _():
                oz(g).start()
                lz(g).start()

    pz_in()
    mz_in()
    for i in range(nx):
        parts = [(pzs[z, i].astype(F32), mzs[z, i])]
        for d in range(1, nz):
            slot = (z + nz - d) % nz
            parts.append((pzr[slot, i].astype(F32), mzr[slot, i]))
        value, level = merge(parts)
        pxs[0, i] = value.astype(BF16)
        mxs[0, i] = level
    for e in range(1, nx):
        px(0, e).start()
        mx(0, e).start()

    arrived(fbuf, f_r.at[0])
    new_keys = fbuf[:nx].reshape(HD, span)
    new_values = fbuf[nx:].reshape(HD, span)

    def token(axis):
        row = lax.broadcasted_iota(jnp.int32, (span, span), axis)
        r = row % 2
        tz = (row // 2) % nz
        tx = (row // (2 * nz)) % nx
        tc = row // (2 * nz * nx)
        return ((tz * nx + tx) * CORES + tc) * 2 + r

    causal = token(0) <= token(1)
    scores = dot(new_keys.T, qbuf[z, c, x])
    scores = jnp.where(causal, scores, -BIG)
    top = jnp.max(scores, axis=0, keepdims=True)
    weights = jnp.where(causal, jnp.exp2((scores - top) * scale), 0.0)
    total = jnp.sum(weights, axis=0, keepdims=True)
    own = dot(new_values, weights.astype(BF16)) * (1.0 / total)
    own_lsum = top * scale + jnp.log(total) * LOG2E
    parts = [(own[:MAIN], own_lsum), (ozs[z].astype(F32), lzs[z])]
    oz_in()
    lz_in()
    for d in range(1, nz):
        slot = (z + nz - d) % nz
        parts.append((ozr[slot].astype(F32), lzr[slot]))
    first_rows, _ = merge(parts)
    parts = [(own[MAIN:], own_lsum), (pxs[0, x].astype(F32), mxs[0, x])]
    px_in(0)
    mx_in(0)
    for e in range(1, nx):
        slot = (x + nx - e) % nx
        parts.append((pxr[0, slot].astype(F32), mxr[0, slot]))
    last_rows, _ = merge(parts)
    attention = jnp.concatenate([first_rows, last_rows], axis=0)
    att[...] = attention.T.astype(BF16).reshape(CORES, span // CORES, HD)

    loads[2].wait()

    def yc(q):
        return remote(ycs.at[q], ycr.at[q], yc_s.at[0], yc_r.at[q], peer)

    def yx(q, d):
        return remote(
            yxs.at[q, (x + d) % nx], yxr.at[q, x], yx_s.at[0], yx_r.at[q], to_x(d)
        )

    def yz(q, d):
        return pltpu.make_async_remote_copy(
            src_ref=yzs.at[q, (z + d) % nz],
            dst_ref=yzr.at[q, z],
            send_sem=yz_s.at[0],
            recv_sem=yz_r.at[q],
            device_id={"kvp": to_z(d), "section": after},
            device_id_type=MESH,
        )

    def vz(d):
        return remote(vzs.at[(z + d) % nz], vzr.at[z], vz_s.at[0], vz_r.at[0], to_z(d))

    def vx(d):
        return pltpu.make_async_remote_copy(
            src_ref=vxs.at[(x + d) % nx],
            dst_ref=vxr.at[x],
            send_sem=vx_s.at[0],
            recv_sem=vx_r.at[0],
            device_id={"kvp": to_x(d), "section": after},
            device_id_type=MESH,
        )

    def by_owner(sums):
        rows = jnp.concatenate([sums[:, j * thin : (j + 1) * thin] for j in range(8)], axis=0)
        return dot(gather, rows).astype(BF16).reshape(nz, 16, thin)

    def sum_x(q):
        sums = yown[q, pl.ds(pl.multiple_of(x * 2 * nz, 2 * nz), 2 * nz)]
        arrived(yxr.at[q, pl.ds(0, nx - 1)], yx_r.at[q])
        for d in range(1, nx):
            sums = sums + yxr[q, (x + nx - d) % nx].astype(F32)
        yzs[q] = by_owner(sums.astype(BF16))
        for d in range(nz):
            yz(q, (d + 1) % nz).start()

    for t in range(SPLIT + 1):
        if t < SPLIT:
            weight = wout[:, t * wide : (t + 1) * wide]
            ycs[t] = dot(att[1 - c], weight).astype(BF16)
            yc(t).start()
            yown[t] = dot(att[c], weight)
        if t >= 1:
            q = t - 1
            arrived(ycr.at[q], yc_r.at[q])
            sums = yown[q] + ycr[q].astype(F32)
            blocks = sums.astype(BF16).reshape(nx, 2 * nz, wide)
            if q > 0:
                yown[q] = sums
                yxs[q] = blocks
                for d in range(1, nx):
                    yx(q, d).start()
            else:
                for i in range(nx):
                    vzs[:, i] = by_owner(blocks[i])
                for d in range(1, nz):
                    vz(d).start()
        if t >= 3:
            sum_x(t - 2)
    arrived(vzr.at[pl.ds(0, nz - 1)], vz_r.at[0])
    for i in range(nx):
        sums = vzs[z, i].astype(F32)
        for d in range(1, nz):
            sums = sums + vzr[(z + nz - d) % nz, i].astype(F32)
        vxs[i] = sums.astype(BF16)
    for d in range(nx):
        vx((d + 1) % nx).start()
    sum_x(SPLIT - 1)

    residual().wait_recv()
    for q in [*range(1, SPLIT - 1), 0, SPLIT - 1]:
        sums = finr[q].astype(F32)
        if q > 0:
            arrived(yzr.at[q], yz_r.at[q])
            for d in range(nz):
                sums = sums + yzr[q, (z + nz - d) % nz].astype(F32)
        else:
            arrived(vxr, vx_r.at[0])
            for d in range(nx):
                sums = sums + vxr[(x + nx - d) % nx].astype(F32)
        stage_o[...] = sums
        for j in range(8):
            start = q * wide + j * thin
            out[0, :, start : start + thin] = stage_o[2 * j : 2 * j + 2, :].astype(BF16)

    tail = pl.ds(1, SPLIT - 1)
    near_x = pl.ds(0, nx - 1)
    near_z = pl.ds(0, nz - 1)
    main = pl.ds(0, MAIN)
    rest = pl.ds(MAIN, HD - MAIN)
    left(hbuf.at[0, near_x], hx_s.at[0])
    left(hbuf.at[near_z], hz_s.at[0])
    left(gbuf.at[tail, near_z], az_s.at[0])
    left(xbuf.at[tail, 0, near_x], ax_s.at[0])
    left(xbuf.at[:, 0], ac_s.at[0])
    left(qbuf.at[near_z, 0, 0, main], qz_s.at[0])
    left(qbuf.at[:, 0, near_x, main], qx_s.at[0])
    left(qbuf.at[0, 0, near_x, rest], rx_s.at[0])
    left(qbuf.at[near_z, 0, :, rest], rz_s.at[0])
    left(qbuf.at[:, 0], qc_s.at[0])
    left(ocs, oc_s.at[0])
    left(lcs, lc_s.at[0])
    left(oxs.at[:, near_x], ox_s.at[0])
    left(lxs.at[:, near_x], lx_s.at[0])
    left(ozs.at[near_z], oz_s.at[0])
    left(lzs.at[near_z], lz_s.at[0])
    left(pzs.at[near_z], pz_s.at[0])
    left(mzs.at[near_z], mz_s.at[0])
    left(pxs.at[0, near_x], px_s.at[0])
    left(mxs.at[0, near_x], mx_s.at[0])
    left(ycs, yc_s.at[0])
    left(yxs.at[tail, near_x], yx_s.at[0])
    left(yzs.at[tail], yz_s.at[0])
    left(vzs.at[near_z], vz_s.at[0])
    left(vxs, vx_s.at[0])
    left(fin, sec_s.at[0])

    @pl.when(fresh_head == z)
    def _():
        left(fbuf.at[pl.ds(0, 2 * nx - 1)], f_s.at[0])

    @pl.when(fresh_head != z)
    def _():
        left(fbuf, f_s.at[0])


def local(n, nx, sections, hidden, norm_gain, w_query, w_kv, w_out, doc_cache, page_table, page_count):
    nz = n // (CORES * nx)
    span = 2 * n
    model = hidden.shape[-1]
    wide = model // SPLIT
    thin = wide // 8
    fresh_rows = w_kv.shape[-1]
    pages = doc_cache.shape[1]
    rest = HD - MAIN
    vmem = pl.BlockSpec(memory_space=pltpu.VMEM)
    smem = pl.BlockSpec(memory_space=pltpu.SMEM)
    anywhere = pl.BlockSpec(memory_space=pl.ANY)
    dma = pltpu.SemaphoreType.DMA

    def pair(waits):
        return [dma((1,)), dma((waits,))]

    scratch = [
        pltpu.VMEM((model, HD), BF16),
        pltpu.VMEM((fresh_rows, model), BF16),
        pltpu.VMEM((HD, model), BF16),
        pltpu.VMEM((2 * nz, pages, HD, HD), BF16),
        pltpu.VMEM((nz, HD, pages * HD), BF16),
        pltpu.VMEM((SPLIT, 16, thin), F32),
        pltpu.VMEM((SPLIT, 16, thin), F32),
        pltpu.VMEM((16, thin), F32),
        pltpu.VMEM((SPLIT, nz, 16, thin), BF16),
        pltpu.VMEM((nz, nx, 16, thin), BF16),
        pltpu.VMEM((SPLIT, CORES, nx, 2 * nz, wide), BF16),
        pltpu.VMEM((nz, CORES, nx, HD, span), BF16),
        pltpu.VMEM((fresh_rows, span), BF16),
        pltpu.VMEM((2 * nx, fresh_rows, span), BF16),
        pltpu.VMEM((nz, nx, HD, span), BF16),
        pltpu.VMEM((nz, nx, HD, span), BF16),
        pltpu.VMEM((nz, nx, 1, span), F32),
        pltpu.VMEM((nz, nx, 1, span), F32),
        pltpu.VMEM((PASS - 1, HD, nx * span), F32),
        pltpu.VMEM((PASS - 1, 1, nx * span), F32),
        pltpu.VMEM((nz, nx, MAIN, span), BF16),
        pltpu.VMEM((nz, nx, MAIN, span), BF16),
        pltpu.VMEM((nz, nx, 1, span), F32),
        pltpu.VMEM((nz, nx, 1, span), F32),
        pltpu.VMEM((nz, MAIN, span), BF16),
        pltpu.VMEM((nz, MAIN, span), BF16),
        pltpu.VMEM((nz, 1, span), F32),
        pltpu.VMEM((nz, 1, span), F32),
        pltpu.VMEM((nz, nx, rest, span), BF16),
        pltpu.VMEM((nz, nx, rest, span), BF16),
        pltpu.VMEM((nz, nx, 1, span), F32),
        pltpu.VMEM((nz, nx, 1, span), F32),
        pltpu.VMEM((1, nx, rest, span), BF16),
        pltpu.VMEM((1, nx, rest, span), BF16),
        pltpu.VMEM((1, nx, 1, span), F32),
        pltpu.VMEM((1, nx, 1, span), F32),
        pltpu.VMEM((CORES, span // CORES, HD), BF16),
        pltpu.VMEM((SPLIT, span // CORES, wide), BF16),
        pltpu.VMEM((SPLIT, span // CORES, wide), BF16),
        pltpu.VMEM((SPLIT, span // CORES, wide), F32),
        pltpu.VMEM((SPLIT, nx, 2 * nz, wide), BF16),
        pltpu.VMEM((SPLIT, nx, 2 * nz, wide), BF16),
        pltpu.VMEM((SPLIT, nz, 16, thin), BF16),
        pltpu.VMEM((SPLIT, nz, 16, thin), BF16),
        pltpu.VMEM((nz, nx, 16, thin), BF16),
        pltpu.VMEM((nz, nx, 16, thin), BF16),
        pltpu.VMEM((nx, 16, thin), BF16),
        pltpu.VMEM((nx, 16, thin), BF16),
        pltpu.VMEM((SPLIT, 16, thin), BF16),
        pltpu.VMEM((SPLIT, 16, thin), BF16),
        dma((3,)),
        dma((1,)),
        *pair(SPLIT),
        *pair(SPLIT),
        *pair(SPLIT),
        *pair(1),
        *pair(1),
        *pair(nz - 1),
        *pair(nz),
        *pair(nz),
        *pair(1),
        *pair(nz - 1),
        *pair(1),
        *pair(nz),
        *pair(nz),
        *pair(nz),
        *pair(nz),
        *pair(1),
        *pair(1),
        *pair(1),
        *pair(1),
        *pair(1),
        *pair(1),
        *pair(SPLIT),
        *pair(SPLIT),
        *pair(SPLIT),
        *pair(1),
        *pair(1),
        *pair(1),
    ]
    return pl.pallas_call(
        functools.partial(kernel, n, nz, nx, sections),
        out_shape=jax.ShapeDtypeStruct(hidden.shape, BF16),
        in_specs=[vmem, vmem, anywhere, anywhere, anywhere, anywhere, smem, smem],
        out_specs=vmem,
        scratch_shapes=scratch,
        compiler_params=pltpu.CompilerParams(
            collective_id=0, has_side_effects=True, vmem_limit_bytes=56 * 1024 * 1024
        ),
    )(hidden, norm_gain, w_query, jnp.swapaxes(w_kv, 1, 2), w_out, doc_cache, page_table, page_count)


def solution(mesh):
    placed = (
        P("section", "kvp", None),
        P("section", None),
        P("section", None, "kvp"),
        P("section", None, "kvp"),
        P("section", "kvp", None),
        P("section", "kvp", None, None),
        P("section", "kvp", None),
        P("section", "kvp"),
    )
    n = mesh.shape["kvp"]
    nx = RINGX if n >= 32 else 2
    return jax.shard_map(
        functools.partial(local, n, nx, mesh.shape["section"]),
        mesh=mesh,
        in_specs=placed,
        out_specs=P("section", "kvp", None),
        check_vma=False,
    )
```

```python
import functools
import math

import jax
import jax.numpy as jnp
from jax import lax
from jax.experimental import pallas as pl
from jax.experimental.pallas import tpu as pltpu
from jax.sharding import PartitionSpec as P

MESH = pl.DeviceIdType.MESH
F32 = jnp.float32
BF16 = jnp.bfloat16

HD = 128
CORES = 2
RINGX = 4
SPLIT = 4
MAIN = 96
EPSILON = 1e-05
BIG = 1e30
LOG2E = 1.4426950408889634
AHEAD = 5
LAG = 6


def dot(a, b, dims=((1,), (0,))):
    return lax.dot_general(a, b, (dims, ((), ())), preferred_element_type=F32)


def row_order(rows, nz, inverse):
    pieces = rows // (2 * nz)
    out_row = lax.broadcasted_iota(jnp.int32, (rows, rows), 0)
    in_row = lax.broadcasted_iota(jnp.int32, (rows, rows), 1)
    if inverse:
        out_row, in_row = in_row, out_row
    r = out_row % 2
    z = (out_row // 2) % nz
    piece = out_row // (2 * nz)
    return jnp.where(in_row == (z * pieces + piece) * 2 + r, 1.0, 0.0).astype(BF16)


def merge(parts):
    top = parts[0][1]
    for _, level in parts[1:]:
        top = jnp.maximum(top, level)
    total = None
    mixed = None
    for value, level in parts:
        weight = jnp.exp2(level - top)
        total = weight if total is None else total + weight
        mixed = value * weight if mixed is None else mixed + value * weight
    return mixed * (1.0 / total), top + jnp.log(total) * LOG2E


def kernel(
    n,
    nz,
    nx,
    sections,
    hid,
    gain,
    wq_hbm,
    wkv_hbm,
    wout_hbm,
    pool_hbm,
    table,
    count,
    out,
    wq,
    wkv,
    wout,
    kv,
    vt,
    limits,
    stage_x,
    stage_n,
    stage_o,
    gbuf,
    hbuf,
    xbuf,
    qbuf,
    fown,
    fbuf,
    oxs,
    oxr,
    lxs,
    lxr,
    ozs,
    ozr,
    lzs,
    lzr,
    pzs,
    pzr,
    mzs,
    mzr,
    pxs,
    pxr,
    mxs,
    mxr,
    att,
    pair_att,
    yown,
    yxs,
    yxr,
    yzs,
    yzr,
    vzs,
    vzr,
    vxs,
    vxr,
    fin,
    finr,
    load_sem,
    kv_sem,
    kc_s,
    kc_r,
    bc_s,
    bc_r,
    az_s,
    az_r,
    ax_s,
    ax_r,
    ac_s,
    ac_r,
    hx_s,
    hx_r,
    hz_s,
    hz_r,
    qz_s,
    qz_r,
    qx_s,
    qx_r,
    rx_s,
    rx_r,
    rz_s,
    rz_r,
    f_s,
    f_r,
    ox_s,
    ox_r,
    lx_s,
    lx_r,
    oz_s,
    oz_r,
    lz_s,
    lz_r,
    pz_s,
    pz_r,
    mz_s,
    mz_r,
    px_s,
    px_r,
    mx_s,
    mx_r,
    wc_s,
    wc_r,
    tc_s,
    tc_r,
    yx_s,
    yx_r,
    yz_s,
    yz_r,
    vz_s,
    vz_r,
    vx_s,
    vx_r,
    sec_s,
    sec_r,
):
    kvh = nz
    span = 2 * n
    model = hid.shape[-1]
    wide = model // SPLIT
    thin = wide // 8
    pages = pool_hbm.shape[1]
    scale = HD ** (-0.5) * LOG2E

    me = lax.axis_index("kvp")
    section = lax.axis_index("section")
    c = me % CORES
    x = (me // CORES) % nx
    z = me // (CORES * nx)
    half = n // 2
    fresh_head = (me % half) // nx
    fresh_piece = (me // half) * nx + me % nx

    def at(zz, xx, cc):
        return (zz * nx + xx) * CORES + cc

    peer = at(z, x, 1 - c)

    def remote(src, dst, send, recv, target):
        return pltpu.make_async_remote_copy(
            src_ref=src,
            dst_ref=dst,
            send_sem=send,
            recv_sem=recv,
            device_id={"kvp": target},
            device_id_type=MESH,
        )

    def arrived(region, sem):
        remote(region, region, sem, sem, peer).wait_recv()

    def left(region, sem):
        remote(region, region, sem, sem, peer).wait_send()

    near_first = sorted(range(1, nz), key=lambda d: min(d, nz - d))
    far_first = sorted(range(1, nz), key=lambda d: -min(d, nz - d))

    def to_z(d):
        return at((z + d) % nz, x, c)

    def to_x(d):
        return at(z, (x + d) % nx, c)

    loads = [
        pltpu.make_async_copy(wq_hbm.at[0], wq, load_sem.at[0]),
        pltpu.make_async_copy(wkv_hbm.at[0], wkv, load_sem.at[1]),
        pltpu.make_async_copy(wout_hbm.at[0], wout.at[c], load_sem.at[2]),
    ]
    kv_loads = [
        pltpu.make_async_copy(pool_hbm.at[0, :, :, pl.ds(i * HD, HD)], kv.at[c, i], kv_sem.at[0])
        for i in range(2 * kvh)
    ]
    for load in loads[:2] + kv_loads + loads[2:]:
        load.start()

    barrier = pltpu.get_barrier_semaphore()

    def greet(target):
        pl.semaphore_signal(barrier, inc=1, device_id={"kvp": target}, device_id_type=MESH)

    for d in range(1, nz):
        greet(to_z(d))
    for d in range(1, nx):
        greet(to_x(d))
    greet(peer)
    before = (section + sections - 1) % sections
    after = (section + 1) % sections
    pl.semaphore_signal(barrier, inc=1, device_id={"section": before}, device_id_type=MESH)

    values = hid[0].astype(F32)
    inv_rms = lax.rsqrt(jnp.mean(values * values, axis=-1, keepdims=True) + EPSILON)
    normed = (values * inv_rms * gain[...].astype(F32)).astype(BF16).astype(F32)
    for q in range(SPLIT):
        for j in range(8):
            start = q * wide + j * thin
            stage_n[q, 2 * j : 2 * j + 2, :] = normed[:, start : start + thin]
            stage_x[q, 2 * j : 2 * j + 2, :] = values[:, start : start + thin]
    for q in range(SPLIT):
        if q > 0:
            gbuf[q, z] = stage_n[q].astype(BF16)
        else:
            hbuf[z, x] = stage_n[q].astype(BF16)
        fin[q] = stage_x[q].astype(BF16)

    pl.semaphore_wait(barrier, (nz - 1) + (nx - 1) + 1 + 1)

    def residual():
        return pltpu.make_async_remote_copy(
            src_ref=fin,
            dst_ref=finr,
            send_sem=sec_s.at[0],
            recv_sem=sec_r.at[0],
            device_id={"section": after},
            device_id_type=MESH,
        )

    def az(q, d):
        return remote(gbuf.at[q, z], gbuf.at[q, z], az_s.at[0], az_r.at[q], to_z(d))

    def ax(q, d):
        slot = xbuf.at[q, c, x]
        return remote(slot, slot, ax_s.at[0], ax_r.at[q], to_x(d))

    def ac(q):
        return remote(xbuf.at[q, c], xbuf.at[q, c], ac_s.at[0], ac_r.at[q], peer)

    def hx(d):
        return remote(hbuf.at[z, x], hbuf.at[z, x], hx_s.at[0], hx_r.at[0], to_x(d))

    def hz(d):
        return remote(hbuf.at[z], hbuf.at[z], hz_s.at[0], hz_r.at[0], to_z(d))

    for d in range(1, nx):
        hx(d).start()
    for q in range(1, SPLIT):
        for d in far_first:
            az(q, d).start()
    arrived(hbuf.at[0, pl.ds(0, nx - 1)], hx_r.at[0])
    for d in far_first:
        hz(d).start()
    residual().start()

    row = lax.broadcasted_iota(jnp.int32, (8, span), 0)
    bounds = jnp.zeros((8, span), F32)
    for slot in range(pages):
        bound = jnp.float32(BIG)
        for j in range(pages):
            named = jnp.logical_and(table[0, 0, j] == slot, j < count[0, 0])
            bound = jnp.where(named, jnp.float32(-BIG), bound)
        bounds = jnp.where(row == slot, bound, bounds)
    limits[c] = bounds

    pltpu.make_async_copy(kv.at[c], kv.at[c], kv_sem.at[0]).wait()
    remote(kv.at[c], kv.at[c], kc_s.at[0], kc_r.at[0], peer).start()
    remote(limits.at[c], limits.at[c], bc_s.at[0], bc_r.at[0], peer).start()
    loads[2].wait()
    remote(wout.at[c], wout.at[c], wc_s.at[0], wc_r.at[0], peer).start()

    def transpose_values(core):
        @pl.loop(0, kvh)
        def _(g):
            vt[core, g] = kv[core, kvh + g].reshape(pages * HD, HD).T

    transpose_values(c)
    spread = row_order(16 * nz, nz, False)
    gather = row_order(16 * nz, nz, True)
    loads[0].wait()
    loads[1].wait()

    query = jnp.zeros((span, HD), F32)
    fresh = jnp.zeros((wkv.shape[0], span), F32)
    order = [*range(1, SPLIT), 0]
    for t in range(SPLIT + 2):
        if t < SPLIT - 1:
            q = order[t]
            arrived(gbuf.at[q, pl.ds(0, nz - 1)], az_r.at[q])
            rows = dot(spread, gbuf[q].reshape(16 * nz, thin)).astype(BF16)
            for j in range(8):
                xbuf[q, c, x, :, j * thin : (j + 1) * thin] = rows[j * 2 * nz : (j + 1) * 2 * nz]
            for d in range(1, nx):
                ax(q, d).start()
        elif t == SPLIT - 1:
            arrived(hbuf.at[pl.ds(0, nz - 1)], hz_r.at[0])
            for i in range(nx):
                block = jnp.concatenate([hbuf[k, i] for k in range(nz)], axis=0)
                rows = dot(spread, block).astype(BF16)
                for j in range(8):
                    xbuf[0, c, i, :, j * thin : (j + 1) * thin] = rows[j * 2 * nz : (j + 1) * 2 * nz]
            ac(0).start()
        if t == 1:
            arrived(kv.at[0], kc_r.at[0])
            arrived(limits.at[0], bc_r.at[0])
            transpose_values(1 - c)
        if 1 <= t <= SPLIT - 1:
            q = order[t - 1]
            arrived(xbuf.at[q, 0, pl.ds(0, nx - 1)], ax_r.at[q])
            ac(q).start()
        if t >= 2:
            q = order[t - 2]
            arrived(xbuf.at[q, 0], ac_r.at[q])
            block = xbuf[q].reshape(span, wide)
            query = query + dot(block, wq[q * wide : (q + 1) * wide])
            fresh = fresh + dot(wkv[:, q * wide : (q + 1) * wide], block, ((1,), (1,)))

    qbuf[z, x] = query.T.astype(BF16)
    fown[...] = fresh.astype(BF16)

    def qz(d):
        slot = qbuf.at[z, x, pl.ds(0, MAIN)]
        return remote(slot, slot, qz_s.at[0], qz_r.at[d - 1], to_z(d))

    def qx(g, d):
        slot = qbuf.at[g, x, pl.ds(0, MAIN)]
        return remote(slot, slot, qx_s.at[0], qx_r.at[g], to_x(d))

    def rx(d):
        slot = qbuf.at[z, x, pl.ds(MAIN, HD - MAIN)]
        return remote(slot, slot, rx_s.at[0], rx_r.at[0], to_x(d))

    def rz(d):
        slot = qbuf.at[z, :, pl.ds(MAIN, HD - MAIN)]
        return remote(slot, slot, rz_s.at[0], rz_r.at[d - 1], to_z(d))

    def fresh_out(i):
        return remote(
            fown,
            fbuf.at[fresh_piece],
            f_s.at[0],
            f_r.at[0],
            fresh_head * CORES * nx + i,
        )

    for d in range(1, nx):
        rx(d).start()
    for d in near_first:
        qz(d).start()
    for d in range(1, nx):
        qx(z, d).start()
    for i in range(2 * nx):
        target = fresh_head * CORES * nx + i

        @pl.when(target != me)
        def _():
            fresh_out(i).start()

        @pl.when(target == me)
        def _():
            pltpu.make_async_copy(fown, fbuf.at[fresh_piece], f_r.at[0]).start()

    def attend(g):
        cols = jnp.concatenate([qbuf[g, i] for i in range(nx)], axis=1)
        parts = []
        bounds = []
        for core in range(CORES):
            scores = dot(kv[core, g].reshape(pages * HD, HD), cols)
            parts += [scores[p * HD : (p + 1) * HD] for p in range(pages)]
            bounds += [jnp.concatenate([limits[core, p : p + 1]] * nx, axis=1) for p in range(pages)]
        top = None
        for part, bound in zip(parts, bounds):
            here = jnp.minimum(jnp.max(part, axis=0, keepdims=True), -bound)
            top = here if top is None else jnp.maximum(top, here)
        total = None
        weights = []
        for part, bound in zip(parts, bounds):
            weight = jnp.exp2((part - jnp.maximum(top, bound)) * scale)
            add = jnp.sum(weight, axis=0, keepdims=True)
            total = add if total is None else total + add
            weights.append(weight.astype(BF16))
        mixed = None
        for core in range(CORES):
            here = jnp.concatenate(weights[core * pages : (core + 1) * pages], axis=0)
            here = dot(vt[core, g], here)
            mixed = here if mixed is None else mixed + here
        return mixed * (1.0 / total), top * scale + jnp.log(total) * LOG2E

    def along_x(send, recv, send_sem, recv_sem):
        def out_copy(g, d):
            return remote(
                send.at[g, (x + d) % nx], recv.at[g, x], send_sem.at[0], recv_sem.at[g], to_x(d)
            )

        return out_copy, lambda g: arrived(recv.at[g, pl.ds(0, nx - 1)], recv_sem.at[g])

    def along_z(send, recv, send_sem, recv_sem):
        def out_copy(g):
            return remote(send.at[g], recv.at[z], send_sem.at[0], recv_sem.at[0], at(g, x, c))

        return out_copy, lambda: arrived(recv.at[pl.ds(0, nz - 1)], recv_sem.at[0])

    ox, ox_in = along_x(oxs, oxr, ox_s, ox_r)
    lx, lx_in = along_x(lxs, lxr, lx_s, lx_r)
    oz, oz_in = along_z(ozs, ozr, oz_s, oz_r)
    lz, lz_in = along_z(lzs, lzr, lz_s, lz_r)
    pz, pz_in = along_z(pzs, pzr, pz_s, pz_r)
    mz, mz_in = along_z(mzs, mzr, mz_s, mz_r)
    px, px_in = along_x(pxs, pxr, px_s, px_r)
    mx, mx_in = along_x(mxs, mxr, mx_s, mx_r)

    def offset(s):
        return (nz + ((s + 1) // 2) * (2 * (s % 2) - 1)) % nz

    def forward(s):
        d = offset(s)
        g = (z + d) % nz
        arrived(qbuf.at[g, 0, pl.ds(0, MAIN)], qz_r.at[nz - d - 1])
        for e in range(1, nx):
            qx(g, e).start()

    arrived(qbuf.at[0, pl.ds(0, nx - 1), pl.ds(MAIN, HD - MAIN)], rx_r.at[0])
    for d in near_first:
        rz(d).start()
    for s in range(1, min(AHEAD, nz)):
        forward(s)

    @pl.loop(0, nz + LAG)
    def _(t):
        @pl.when(t < nz - AHEAD)
        def _():
            forward(t + AHEAD)

        @pl.when(t < nz)
        def _():
            d = offset(t)
            g = (z + d) % nz
            arrived(qbuf.at[g, pl.ds(0, nx - 1), pl.ds(0, MAIN)], qx_r.at[g])

            @pl.when(t > 0)
            def _():
                arrived(qbuf.at[g, :, pl.ds(MAIN, HD - MAIN)], rz_r.at[nz - d - 1])

            mixed, level = attend(g)
            for i in range(nx):
                cols = slice(i * span, (i + 1) * span)
                oxs[g, i] = mixed[:MAIN, cols].astype(BF16)
                pzs[g, i] = mixed[MAIN:, cols].astype(BF16)
                lxs[g, i] = level[:, cols]
                mzs[g, i] = level[:, cols]
            for e in range(1, nx):
                ox(g, e).start()
                lx(g, e).start()

            @pl.when(t > 0)
            def _():
                pz(g).start()
                mz(g).start()

        @pl.when(t >= LAG)
        def _():
            d = offset(t - LAG)
            g = (z + d) % nz
            ox_in(g)
            lx_in(g)
            parts = [(oxs[g, x].astype(F32), lxs[g, x])]
            for e in range(1, nx):
                slot = (x + e) % nx
                parts.append((oxr[g, slot].astype(F32), lxr[g, slot]))
            value, level = merge(parts)
            ozs[g] = value.astype(BF16)
            lzs[g] = level

            @pl.when(t > LAG)
            def _():
                oz(g).start()
                lz(g).start()

    pz_in()
    mz_in()
    for i in range(nx):
        parts = [(pzs[z, i].astype(F32), mzs[z, i])]
        for d in range(1, nz):
            slot = (z + nz - d) % nz
            parts.append((pzr[slot, i].astype(F32), mzr[slot, i]))
        value, level = merge(parts)
        pxs[0, i] = value.astype(BF16)
        mxs[0, i] = level
    for e in range(1, nx):
        px(0, e).start()
        mx(0, e).start()

    arrived(fbuf, f_r.at[0])
    new_keys = fbuf[:nx].reshape(HD, span)
    new_values = fbuf[nx:].reshape(HD, span)

    def token(axis):
        row = lax.broadcasted_iota(jnp.int32, (span, span), axis)
        r = row % 2
        tz = (row // 2) % nz
        tx = (row // (2 * nz)) % nx
        tc = row // (2 * nz * nx)
        return ((tz * nx + tx) * CORES + tc) * 2 + r

    causal = token(0) <= token(1)
    scores = dot(new_keys.T, qbuf[z, x])
    scores = jnp.where(causal, scores, -BIG)
    top = jnp.max(scores, axis=0, keepdims=True)
    weights = jnp.where(causal, jnp.exp2((scores - top) * scale), 0.0)
    total = jnp.sum(weights, axis=0, keepdims=True)
    own = dot(new_values, weights.astype(BF16)) * (1.0 / total)
    own_lsum = top * scale + jnp.log(total) * LOG2E
    parts = [(own[:MAIN], own_lsum), (ozs[z].astype(F32), lzs[z])]
    oz_in()
    lz_in()
    for d in range(1, nz):
        slot = (z + nz - d) % nz
        parts.append((ozr[slot].astype(F32), lzr[slot]))
    first_rows, _ = merge(parts)
    parts = [(own[MAIN:], own_lsum), (pxs[0, x].astype(F32), mxs[0, x])]
    px_in(0)
    mx_in(0)
    for e in range(1, nx):
        slot = (x + nx - e) % nx
        parts.append((pxr[0, slot].astype(F32), mxr[0, slot]))
    last_rows, _ = merge(parts)
    attention = jnp.concatenate([first_rows, last_rows], axis=0)
    att[...] = attention.T.astype(BF16).reshape(CORES, span // CORES, HD)
    remote(att.at[1 - c], pair_att.at[c], tc_s.at[0], tc_r.at[0], peer).start()
    pair_att[c] = att[c]
    arrived(wout.at[0], wc_r.at[0])
    arrived(pair_att.at[0], tc_r.at[0])
    both = jnp.concatenate([pair_att[0], pair_att[1]], axis=1)


    def yx(q, d):
        return remote(
            yxs.at[q, (x + d) % nx], yxr.at[q, x], yx_s.at[0], yx_r.at[q], to_x(d)
        )

    def yz(q, d):
        return pltpu.make_async_remote_copy(
            src_ref=yzs.at[q, (z + d) % nz],
            dst_ref=yzr.at[q, z],
            send_sem=yz_s.at[0],
            recv_sem=yz_r.at[q],
            device_id={"kvp": to_z(d), "section": after},
            device_id_type=MESH,
        )

    def vz(d):
        return remote(vzs.at[(z + d) % nz], vzr.at[z], vz_s.at[0], vz_r.at[0], to_z(d))

    def vx(d):
        return pltpu.make_async_remote_copy(
            src_ref=vxs.at[(x + d) % nx],
            dst_ref=vxr.at[x],
            send_sem=vx_s.at[0],
            recv_sem=vx_r.at[0],
            device_id={"kvp": to_x(d), "section": after},
            device_id_type=MESH,
        )

    def by_owner(sums):
        rows = jnp.concatenate([sums[:, j * thin : (j + 1) * thin] for j in range(8)], axis=0)
        return dot(gather, rows).astype(BF16).reshape(nz, 16, thin)

    def sum_x(q):
        sums = yown[q, pl.ds(pl.multiple_of(x * 2 * nz, 2 * nz), 2 * nz)]
        arrived(yxr.at[q, pl.ds(0, nx - 1)], yx_r.at[q])
        for d in range(1, nx):
            sums = sums + yxr[q, (x + nx - d) % nx].astype(F32)
        yzs[q] = by_owner(sums.astype(BF16))
        for d in [*far_first, 0]:
            yz(q, d).start()

    for q in range(SPLIT):
        sums = dot(both, wout[:, :, q * wide : (q + 1) * wide].reshape(CORES * HD, wide))
        blocks = sums.astype(BF16).reshape(nx, 2 * nz, wide)
        if q > 0:
            yown[q] = sums
            yxs[q] = blocks
            for d in range(1, nx):
                yx(q, d).start()
        else:
            for i in range(nx):
                vzs[:, i] = by_owner(blocks[i])
            for d in far_first:
                vz(d).start()
    for q in range(1, SPLIT - 1):
        sum_x(q)
    arrived(vzr.at[pl.ds(0, nz - 1)], vz_r.at[0])
    for i in range(nx):
        sums = vzs[z, i].astype(F32)
        for d in range(1, nz):
            sums = sums + vzr[(z + nz - d) % nz, i].astype(F32)
        vxs[i] = sums.astype(BF16)
    for d in range(nx):
        vx((d + 1) % nx).start()
    sum_x(SPLIT - 1)

    residual().wait_recv()
    for q in [*range(1, SPLIT - 1), 0, SPLIT - 1]:
        sums = finr[q].astype(F32)
        if q > 0:
            arrived(yzr.at[q], yz_r.at[q])
            for d in range(nz):
                sums = sums + yzr[q, (z + nz - d) % nz].astype(F32)
        else:
            arrived(vxr, vx_r.at[0])
            for d in range(nx):
                sums = sums + vxr[(x + nx - d) % nx].astype(F32)
        stage_o[...] = sums
        for j in range(8):
            start = q * wide + j * thin
            out[0, :, start : start + thin] = stage_o[2 * j : 2 * j + 2, :].astype(BF16)

    tail = pl.ds(1, SPLIT - 1)
    near_x = pl.ds(0, nx - 1)
    near_z = pl.ds(0, nz - 1)
    main = pl.ds(0, MAIN)
    rest = pl.ds(MAIN, HD - MAIN)
    left(hbuf.at[0, near_x], hx_s.at[0])
    left(hbuf.at[near_z], hz_s.at[0])
    left(gbuf.at[tail, near_z], az_s.at[0])
    left(xbuf.at[tail, 0, near_x], ax_s.at[0])
    left(xbuf.at[:, 0], ac_s.at[0])
    left(kv.at[0], kc_s.at[0])
    left(limits.at[0], bc_s.at[0])
    left(qbuf.at[near_z, 0, main], qz_s.at[0])
    left(qbuf.at[:, near_x, main], qx_s.at[0])
    left(qbuf.at[0, near_x, rest], rx_s.at[0])
    left(qbuf.at[near_z, :, rest], rz_s.at[0])
    left(oxs.at[:, near_x], ox_s.at[0])
    left(lxs.at[:, near_x], lx_s.at[0])
    left(ozs.at[near_z], oz_s.at[0])
    left(lzs.at[near_z], lz_s.at[0])
    left(pzs.at[near_z], pz_s.at[0])
    left(mzs.at[near_z], mz_s.at[0])
    left(pxs.at[0, near_x], px_s.at[0])
    left(mxs.at[0, near_x], mx_s.at[0])
    left(wout.at[0], wc_s.at[0])
    left(att.at[0], tc_s.at[0])
    left(yxs.at[tail, near_x], yx_s.at[0])
    left(yzs.at[tail], yz_s.at[0])
    left(vzs.at[near_z], vz_s.at[0])
    left(vxs, vx_s.at[0])
    left(fin, sec_s.at[0])

    @pl.when(fresh_head == z)
    def _():
        left(fbuf.at[pl.ds(0, 2 * nx - 1)], f_s.at[0])

    @pl.when(fresh_head != z)
    def _():
        left(fbuf, f_s.at[0])


def local(n, nx, sections, hidden, norm_gain, w_query, w_kv, w_out, doc_cache, page_table, page_count):
    nz = n // (CORES * nx)
    span = 2 * n
    model = hidden.shape[-1]
    wide = model // SPLIT
    thin = wide // 8
    fresh_rows = w_kv.shape[-1]
    pages = doc_cache.shape[1]
    rest = HD - MAIN
    vmem = pl.BlockSpec(memory_space=pltpu.VMEM)
    smem = pl.BlockSpec(memory_space=pltpu.SMEM)
    anywhere = pl.BlockSpec(memory_space=pl.ANY)
    dma = pltpu.SemaphoreType.DMA

    def pair(waits):
        return [dma((1,)), dma((waits,))]

    scratch = [
        pltpu.VMEM((model, HD), BF16),
        pltpu.VMEM((fresh_rows, model), BF16),
        pltpu.VMEM((CORES, HD, model), BF16),
        pltpu.VMEM((CORES, 2 * nz, pages, HD, HD), BF16),
        pltpu.VMEM((CORES, nz, HD, pages * HD), BF16),
        pltpu.VMEM((CORES, 8, span), F32),
        pltpu.VMEM((SPLIT, 16, thin), F32),
        pltpu.VMEM((SPLIT, 16, thin), F32),
        pltpu.VMEM((16, thin), F32),
        pltpu.VMEM((SPLIT, nz, 16, thin), BF16),
        pltpu.VMEM((nz, nx, 16, thin), BF16),
        pltpu.VMEM((SPLIT, CORES, nx, 2 * nz, wide), BF16),
        pltpu.VMEM((nz, nx, HD, span), BF16),
        pltpu.VMEM((fresh_rows, span), BF16),
        pltpu.VMEM((2 * nx, fresh_rows, span), BF16),
        pltpu.VMEM((nz, nx, MAIN, span), BF16),
        pltpu.VMEM((nz, nx, MAIN, span), BF16),
        pltpu.VMEM((nz, nx, 1, span), F32),
        pltpu.VMEM((nz, nx, 1, span), F32),
        pltpu.VMEM((nz, MAIN, span), BF16),
        pltpu.VMEM((nz, MAIN, span), BF16),
        pltpu.VMEM((nz, 1, span), F32),
        pltpu.VMEM((nz, 1, span), F32),
        pltpu.VMEM((nz, nx, rest, span), BF16),
        pltpu.VMEM((nz, nx, rest, span), BF16),
        pltpu.VMEM((nz, nx, 1, span), F32),
        pltpu.VMEM((nz, nx, 1, span), F32),
        pltpu.VMEM((1, nx, rest, span), BF16),
        pltpu.VMEM((1, nx, rest, span), BF16),
        pltpu.VMEM((1, nx, 1, span), F32),
        pltpu.VMEM((1, nx, 1, span), F32),
        pltpu.VMEM((CORES, span // CORES, HD), BF16),
        pltpu.VMEM((CORES, span // CORES, HD), BF16),
        pltpu.VMEM((SPLIT, span // CORES, wide), F32),
        pltpu.VMEM((SPLIT, nx, 2 * nz, wide), BF16),
        pltpu.VMEM((SPLIT, nx, 2 * nz, wide), BF16),
        pltpu.VMEM((SPLIT, nz, 16, thin), BF16),
        pltpu.VMEM((SPLIT, nz, 16, thin), BF16),
        pltpu.VMEM((nz, nx, 16, thin), BF16),
        pltpu.VMEM((nz, nx, 16, thin), BF16),
        pltpu.VMEM((nx, 16, thin), BF16),
        pltpu.VMEM((nx, 16, thin), BF16),
        pltpu.VMEM((SPLIT, 16, thin), BF16),
        pltpu.VMEM((SPLIT, 16, thin), BF16),
        dma((3,)),
        dma((1,)),
        *pair(1),
        *pair(1),
        *pair(SPLIT),
        *pair(SPLIT),
        *pair(SPLIT),
        *pair(1),
        *pair(1),
        *pair(nz - 1),
        *pair(nz),
        *pair(1),
        *pair(nz - 1),
        *pair(1),
        *pair(nz),
        *pair(nz),
        *pair(1),
        *pair(1),
        *pair(1),
        *pair(1),
        *pair(1),
        *pair(1),
        *pair(1),
        *pair(1),
        *pair(SPLIT),
        *pair(SPLIT),
        *pair(1),
        *pair(1),
        *pair(1),
    ]
    return pl.pallas_call(
        functools.partial(kernel, n, nz, nx, sections),
        out_shape=jax.ShapeDtypeStruct(hidden.shape, BF16),
        in_specs=[vmem, vmem, anywhere, anywhere, anywhere, anywhere, smem, smem],
        out_specs=vmem,
        scratch_shapes=scratch,
        compiler_params=pltpu.CompilerParams(
            collective_id=0, has_side_effects=True, vmem_limit_bytes=56 * 1024 * 1024
        ),
    )(hidden, norm_gain, w_query, jnp.swapaxes(w_kv, 1, 2), w_out, doc_cache, page_table, page_count)


def solution(mesh):
    placed = (
        P("section", "kvp", None),
        P("section", None),
        P("section", None, "kvp"),
        P("section", None, "kvp"),
        P("section", "kvp", None),
        P("section", "kvp", None, None),
        P("section", "kvp", None),
        P("section", "kvp"),
    )
    n = mesh.shape["kvp"]
    nx = RINGX if n >= 32 else 2
    return jax.shard_map(
        functools.partial(local, n, nx, mesh.shape["section"]),
        mesh=mesh,
        in_specs=placed,
        out_specs=P("section", "kvp", None),
        check_vma=False,
    )
```

```python
import functools
import math

import jax
import jax.numpy as jnp
from jax import lax
from jax.experimental import pallas as pl
from jax.experimental.pallas import tpu as pltpu
from jax.sharding import PartitionSpec as P

MESH = pl.DeviceIdType.MESH
F32 = jnp.float32
BF16 = jnp.bfloat16

HD = 128
CORES = 2
RINGX = 4
SPLIT = 4
MAIN = 96
EPSILON = 1e-05
BIG = 1e30
LOG2E = 1.4426950408889634
AHEAD = 5
LAG = 6


def dot(a, b, dims=((1,), (0,))):
    return lax.dot_general(a, b, (dims, ((), ())), preferred_element_type=F32)


def row_order(rows, nz, inverse):
    pieces = rows // (2 * nz)
    out_row = lax.broadcasted_iota(jnp.int32, (rows, rows), 0)
    in_row = lax.broadcasted_iota(jnp.int32, (rows, rows), 1)
    if inverse:
        out_row, in_row = in_row, out_row
    r = out_row % 2
    z = (out_row // 2) % nz
    piece = out_row // (2 * nz)
    return jnp.where(in_row == (z * pieces + piece) * 2 + r, 1.0, 0.0).astype(BF16)


def merge(parts):
    top = parts[0][1]
    for _, level in parts[1:]:
        top = jnp.maximum(top, level)
    total = None
    mixed = None
    for value, level in parts:
        weight = jnp.exp2(level - top)
        total = weight if total is None else total + weight
        mixed = value * weight if mixed is None else mixed + value * weight
    return mixed * (1.0 / total), top + jnp.log(total) * LOG2E


def kernel(
    n,
    nz,
    nx,
    sections,
    hid,
    gain,
    wq_hbm,
    wkv_hbm,
    wout_hbm,
    pool_hbm,
    table,
    count,
    out,
    wq,
    wkv,
    wout,
    kv,
    vt,
    limits,
    stage_x,
    stage_n,
    stage_o,
    gbuf,
    hbuf,
    xbuf,
    qbuf,
    fpair,
    fturn,
    fown,
    fbuf,
    oxs,
    oxr,
    lxs,
    lxr,
    ozs,
    ozr,
    lzs,
    lzr,
    pzs,
    pzr,
    mzs,
    mzr,
    pxs,
    pxr,
    mxs,
    mxr,
    yown,
    yxs,
    yxr,
    yzs,
    yzr,
    vzs,
    vzr,
    vxs,
    vxr,
    fin,
    finr,
    load_sem,
    kv_sem,
    kc_s,
    kc_r,
    bc_s,
    bc_r,
    az_s,
    az_r,
    ax_s,
    ax_r,
    dc_s,
    dc_r,
    ec_s,
    ec_r,
    fc_s,
    fc_r,
    hx_s,
    hx_r,
    hz_s,
    hz_r,
    qz_s,
    qz_r,
    qx_s,
    qx_r,
    rx_s,
    rx_r,
    rz_s,
    rz_r,
    f_s,
    f_r,
    ox_s,
    ox_r,
    lx_s,
    lx_r,
    oz_s,
    oz_r,
    lz_s,
    lz_r,
    pz_s,
    pz_r,
    mz_s,
    mz_r,
    px_s,
    px_r,
    mx_s,
    mx_r,
    wc_s,
    wc_r,
    yx_s,
    yx_r,
    yz_s,
    yz_r,
    vz_s,
    vz_r,
    vx_s,
    vx_r,
    sec_s,
    sec_r,
):
    kvh = nz
    span = 2 * n
    half_span = span // CORES
    model = hid.shape[-1]
    wide = model // SPLIT
    thin = wide // 8
    pages = pool_hbm.shape[1]
    scale = HD ** (-0.5) * LOG2E

    me = lax.axis_index("kvp")
    section = lax.axis_index("section")
    c = me % CORES
    x = (me // CORES) % nx
    z = me // (CORES * nx)
    half = n // 2
    fresh_head = (me % half) // nx
    fresh_piece = (me // half) * nx + me % nx

    def at(zz, xx, cc):
        return (zz * nx + xx) * CORES + cc

    peer = at(z, x, 1 - c)

    def remote(src, dst, send, recv, target):
        return pltpu.make_async_remote_copy(
            src_ref=src,
            dst_ref=dst,
            send_sem=send,
            recv_sem=recv,
            device_id={"kvp": target},
            device_id_type=MESH,
        )

    def arrived(region, sem):
        remote(region, region, sem, sem, peer).wait_recv()

    def left(region, sem):
        remote(region, region, sem, sem, peer).wait_send()

    near_first = sorted(range(1, nz), key=lambda d: min(d, nz - d))
    far_first = sorted(range(1, nz), key=lambda d: -min(d, nz - d))

    def to_z(d):
        return at((z + d) % nz, x, c)

    def to_x(d):
        return at(z, (x + d) % nx, c)

    loads = [
        pltpu.make_async_copy(wq_hbm.at[0], wq.at[c], load_sem.at[0]),
        pltpu.make_async_copy(wkv_hbm.at[0], wkv.at[c], load_sem.at[1]),
        pltpu.make_async_copy(wout_hbm.at[0], wout.at[c], load_sem.at[2]),
    ]
    kv_loads = [
        pltpu.make_async_copy(pool_hbm.at[0, :, :, pl.ds(i * HD, HD)], kv.at[c, i], kv_sem.at[0])
        for i in range(2 * kvh)
    ]
    for load in loads[:2] + kv_loads + loads[2:]:
        load.start()

    barrier = pltpu.get_barrier_semaphore()

    def greet(target):
        pl.semaphore_signal(barrier, inc=1, device_id={"kvp": target}, device_id_type=MESH)

    for d in range(1, nz):
        greet(to_z(d))
    for d in range(1, nx):
        greet(to_x(d))
    greet(peer)
    before = (section + sections - 1) % sections
    after = (section + 1) % sections
    pl.semaphore_signal(barrier, inc=1, device_id={"section": before}, device_id_type=MESH)

    values = hid[0].astype(F32)
    inv_rms = lax.rsqrt(jnp.mean(values * values, axis=-1, keepdims=True) + EPSILON)
    normed = (values * inv_rms * gain[...].astype(F32)).astype(BF16).astype(F32)
    for q in range(SPLIT):
        for j in range(8):
            start = q * wide + j * thin
            stage_n[q, 2 * j : 2 * j + 2, :] = normed[:, start : start + thin]
            stage_x[q, 2 * j : 2 * j + 2, :] = values[:, start : start + thin]
    for q in range(SPLIT):
        if q > 0:
            gbuf[q, z] = stage_n[q].astype(BF16)
        else:
            hbuf[z, x] = stage_n[q].astype(BF16)
        fin[q] = stage_x[q].astype(BF16)

    pl.semaphore_wait(barrier, (nz - 1) + (nx - 1) + 1 + 1)

    def residual():
        return pltpu.make_async_remote_copy(
            src_ref=fin,
            dst_ref=finr,
            send_sem=sec_s.at[0],
            recv_sem=sec_r.at[0],
            device_id={"section": after},
            device_id_type=MESH,
        )

    def az(q, d):
        return remote(gbuf.at[q, z], gbuf.at[q, z], az_s.at[0], az_r.at[q], to_z(d))

    def ax(q, d):
        slot = xbuf.at[q, x]
        return remote(slot, slot, ax_s.at[0], ax_r.at[q], to_x(d))

    def hx(d):
        return remote(hbuf.at[z, x], hbuf.at[z, x], hx_s.at[0], hx_r.at[0], to_x(d))

    def hz(d):
        return remote(hbuf.at[z], hbuf.at[z], hz_s.at[0], hz_r.at[0], to_z(d))

    for d in range(1, nx):
        hx(d).start()
    for q in range(1, SPLIT):
        for d in far_first:
            az(q, d).start()
    arrived(hbuf.at[0, pl.ds(0, nx - 1)], hx_r.at[0])
    for d in far_first:
        hz(d).start()
    residual().start()

    row = lax.broadcasted_iota(jnp.int32, (8, span), 0)
    bounds = jnp.zeros((8, span), F32)
    for slot in range(pages):
        bound = jnp.float32(BIG)
        for j in range(pages):
            named = jnp.logical_and(table[0, 0, j] == slot, j < count[0, 0])
            bound = jnp.where(named, jnp.float32(-BIG), bound)
        bounds = jnp.where(row == slot, bound, bounds)
    limits[c] = bounds

    if wkv.shape[0] > CORES:
        wkv[CORES:] = jnp.zeros((wkv.shape[0] - CORES, *wkv.shape[1:]), BF16)
    loads[0].wait()
    remote(wq.at[c], wq.at[c], dc_s.at[0], dc_r.at[0], peer).start()
    loads[1].wait()
    remote(wkv.at[c], wkv.at[c], ec_s.at[0], ec_r.at[0], peer).start()
    pltpu.make_async_copy(kv.at[c], kv.at[c], kv_sem.at[0]).wait()
    remote(kv.at[c], kv.at[c], kc_s.at[0], kc_r.at[0], peer).start()
    remote(limits.at[c], limits.at[c], bc_s.at[0], bc_r.at[0], peer).start()
    loads[2].wait()
    remote(wout.at[c], wout.at[c], wc_s.at[0], wc_r.at[0], peer).start()

    def transpose_values(core):
        @pl.loop(0, kvh)
        def _(g):
            vt[core, g] = kv[core, kvh + g].reshape(pages * HD, HD).T

    transpose_values(c)
    spread = row_order(16 * nz, nz, False)
    gather = row_order(16 * nz, nz, True)

    queries = [jnp.zeros((half_span, HD), F32) for _ in range(CORES)]
    fresh = jnp.zeros((half_span, HD), F32)
    order = [*range(1, SPLIT), 0]
    for t in range(SPLIT + 1):
        if t < SPLIT - 1:
            q = order[t]
            arrived(gbuf.at[q, pl.ds(0, nz - 1)], az_r.at[q])
            rows = dot(spread, gbuf[q].reshape(16 * nz, thin)).astype(BF16)
            for j in range(8):
                xbuf[q, x, :, j * thin : (j + 1) * thin] = rows[j * 2 * nz : (j + 1) * 2 * nz]
            for d in range(1, nx):
                ax(q, d).start()
        elif t == SPLIT - 1:
            arrived(hbuf.at[pl.ds(0, nz - 1)], hz_r.at[0])
            for i in range(nx):
                block = jnp.concatenate([hbuf[k, i] for k in range(nz)], axis=0)
                rows = dot(spread, block).astype(BF16)
                for j in range(8):
                    xbuf[0, i, :, j * thin : (j + 1) * thin] = rows[j * 2 * nz : (j + 1) * 2 * nz]
        if t == 1:
            arrived(kv.at[0], kc_r.at[0])
            arrived(limits.at[0], bc_r.at[0])
            transpose_values(1 - c)
            arrived(wq.at[0], dc_r.at[0])
            arrived(wkv.at[0], ec_r.at[0])
        if t >= 1:
            q = order[t - 1]
            if q > 0:
                arrived(xbuf.at[q, pl.ds(0, nx - 1)], ax_r.at[q])
            block = xbuf[q].reshape(half_span, wide)
            cols = slice(q * wide, (q + 1) * wide)
            queries = [queries[h] + dot(block, wq[h, cols]) for h in range(CORES)]
            fresh = fresh + dot(block, wkv[:, :, cols].reshape(HD, wide), ((1,), (1,)))

    qbuf[z, x] = jnp.concatenate(queries, axis=0).T.astype(BF16)
    fpair[c] = fresh.astype(BF16)
    remote(fpair.at[c], fpair.at[c], fc_s.at[0], fc_r.at[0], peer).start()

    def qz(d):
        slot = qbuf.at[z, x, pl.ds(0, MAIN)]
        return remote(slot, slot, qz_s.at[0], qz_r.at[d - 1], to_z(d))

    def qx(g, d):
        slot = qbuf.at[g, x, pl.ds(0, MAIN)]
        return remote(slot, slot, qx_s.at[0], qx_r.at[g], to_x(d))

    def rx(d):
        slot = qbuf.at[z, x, pl.ds(MAIN, HD - MAIN)]
        return remote(slot, slot, rx_s.at[0], rx_r.at[0], to_x(d))

    def rz(d):
        slot = qbuf.at[z, :, pl.ds(MAIN, HD - MAIN)]
        return remote(slot, slot, rz_s.at[0], rz_r.at[d - 1], to_z(d))

    def fresh_out(i):
        return remote(
            fown,
            fbuf.at[fresh_piece],
            f_s.at[0],
            f_r.at[0],
            fresh_head * CORES * nx + i,
        )

    for d in range(1, nx):
        rx(d).start()
    for d in near_first:
        qz(d).start()
    for d in range(1, nx):
        qx(z, d).start()
    def attend(g):
        cols = jnp.concatenate([qbuf[g, i] for i in range(nx)], axis=1)
        parts = []
        bounds = []
        for core in range(CORES):
            scores = dot(kv[core, g].reshape(pages * HD, HD), cols)
            parts += [scores[p * HD : (p + 1) * HD] for p in range(pages)]
            bounds += [jnp.concatenate([limits[core, p : p + 1]] * nx, axis=1) for p in range(pages)]
        top = None
        for part, bound in zip(parts, bounds):
            here = jnp.minimum(jnp.max(part, axis=0, keepdims=True), -bound)
            top = here if top is None else jnp.maximum(top, here)
        total = None
        weights = []
        for part, bound in zip(parts, bounds):
            weight = jnp.exp2((part - jnp.maximum(top, bound)) * scale)
            add = jnp.sum(weight, axis=0, keepdims=True)
            total = add if total is None else total + add
            weights.append(weight.astype(BF16))
        mixed = None
        for core in range(CORES):
            here = jnp.concatenate(weights[core * pages : (core + 1) * pages], axis=0)
            here = dot(vt[core, g], here)
            mixed = here if mixed is None else mixed + here
        return mixed * (1.0 / total), top * scale + jnp.log(total) * LOG2E

    def along_x(send, recv, send_sem, recv_sem):
        def out_copy(g, d):
            return remote(
                send.at[g, (x + d) % nx], recv.at[g, x], send_sem.at[0], recv_sem.at[g], to_x(d)
            )

        return out_copy, lambda g: arrived(recv.at[g, pl.ds(0, nx - 1)], recv_sem.at[g])

    def along_z(send, recv, send_sem, recv_sem):
        def out_copy(g):
            return remote(send.at[g], recv.at[z], send_sem.at[0], recv_sem.at[0], at(g, x, c))

        return out_copy, lambda: arrived(recv.at[pl.ds(0, nz - 1)], recv_sem.at[0])

    ox, ox_in = along_x(oxs, oxr, ox_s, ox_r)
    lx, lx_in = along_x(lxs, lxr, lx_s, lx_r)
    oz, oz_in = along_z(ozs, ozr, oz_s, oz_r)
    lz, lz_in = along_z(lzs, lzr, lz_s, lz_r)
    pz, pz_in = along_z(pzs, pzr, pz_s, pz_r)
    mz, mz_in = along_z(mzs, mzr, mz_s, mz_r)
    px, px_in = along_x(pxs, pxr, px_s, px_r)
    mx, mx_in = along_x(mxs, mxr, mx_s, mx_r)

    def offset(s):
        return (nz + ((s + 1) // 2) * (2 * (s % 2) - 1)) % nz

    def forward(s):
        d = offset(s)
        g = (z + d) % nz
        arrived(qbuf.at[g, 0, pl.ds(0, MAIN)], qz_r.at[nz - d - 1])
        for e in range(1, nx):
            qx(g, e).start()

    arrived(qbuf.at[0, pl.ds(0, nx - 1), pl.ds(MAIN, HD - MAIN)], rx_r.at[0])
    for d in near_first:
        rz(d).start()
    for s in range(1, min(AHEAD, nz)):
        forward(s)

    arrived(fpair.at[0], fc_r.at[0])
    fturn[...] = fpair[...].astype(F32).reshape(span, HD).T.astype(BF16).reshape(fturn.shape)
    fown[...] = fturn[c]
    for i in range(2 * nx):
        target = fresh_head * CORES * nx + i

        @pl.when(target != me)
        def _():
            fresh_out(i).start()

        @pl.when(target == me)
        def _():
            pltpu.make_async_copy(fown, fbuf.at[fresh_piece], f_r.at[0]).start()

    @pl.loop(0, nz + LAG)
    def _(t):
        @pl.when(t < nz - AHEAD)
        def _():
            forward(t + AHEAD)

        @pl.when(t < nz)
        def _():
            d = offset(t)
            g = (z + d) % nz
            arrived(qbuf.at[g, pl.ds(0, nx - 1), pl.ds(0, MAIN)], qx_r.at[g])

            @pl.when(t > 0)
            def _():
                arrived(qbuf.at[g, :, pl.ds(MAIN, HD - MAIN)], rz_r.at[nz - d - 1])

            mixed, level = attend(g)
            for i in range(nx):
                cols = slice(i * span, (i + 1) * span)
                oxs[g, i] = mixed[:MAIN, cols].astype(BF16)
                pzs[g, i] = mixed[MAIN:, cols].astype(BF16)
                lxs[g, i] = level[:, cols]
                mzs[g, i] = level[:, cols]
            for e in range(1, nx):
                ox(g, e).start()
                lx(g, e).start()

            @pl.when(t > 0)
            def _():
                pz(g).start()
                mz(g).start()

        @pl.when(t >= LAG)
        def _():
            d = offset(t - LAG)
            g = (z + d) % nz
            ox_in(g)
            lx_in(g)
            parts = [(oxs[g, x].astype(F32), lxs[g, x])]
            for e in range(1, nx):
                slot = (x + e) % nx
                parts.append((oxr[g, slot].astype(F32), lxr[g, slot]))
            value, level = merge(parts)
            ozs[g] = value.astype(BF16)
            lzs[g] = level

            @pl.when(t > LAG)
            def _():
                oz(g).start()
                lz(g).start()

    pz_in()
    mz_in()
    for i in range(nx):
        parts = [(pzs[z, i].astype(F32), mzs[z, i])]
        for d in range(1, nz):
            slot = (z + nz - d) % nz
            parts.append((pzr[slot, i].astype(F32), mzr[slot, i]))
        value, level = merge(parts)
        pxs[0, i] = value.astype(BF16)
        mxs[0, i] = level
    for e in range(1, nx):
        px(0, e).start()
        mx(0, e).start()

    arrived(fbuf, f_r.at[0])
    new_keys = fbuf[:nx].reshape(HD, span)
    new_values = fbuf[nx:].reshape(HD, span)

    def token(row):
        r = row % 2
        tz = (row // 2) % nz
        tx = (row // (2 * nz)) % nx
        tc = row // (2 * nz * nx)
        return ((tz * nx + tx) * CORES + tc) * 2 + r

    key_row = lax.broadcasted_iota(jnp.int32, (span, span), 0)
    query_lane = lax.broadcasted_iota(jnp.int32, (span, span), 1)
    causal = token(key_row) <= token(c * half_span + query_lane % half_span)
    scores = dot(new_keys.T, qbuf[z, x])
    scores = jnp.where(causal, scores, -BIG)
    top = jnp.max(scores, axis=0, keepdims=True)
    weights = jnp.where(causal, jnp.exp2((scores - top) * scale), 0.0)
    total = jnp.sum(weights, axis=0, keepdims=True)
    own = dot(new_values, weights.astype(BF16)) * (1.0 / total)
    own_lsum = top * scale + jnp.log(total) * LOG2E
    parts = [(own[:MAIN], own_lsum), (ozs[z].astype(F32), lzs[z])]
    oz_in()
    lz_in()
    for d in range(1, nz):
        slot = (z + nz - d) % nz
        parts.append((ozr[slot].astype(F32), lzr[slot]))
    first_rows, _ = merge(parts)
    parts = [(own[MAIN:], own_lsum), (pxs[0, x].astype(F32), mxs[0, x])]
    px_in(0)
    mx_in(0)
    for e in range(1, nx):
        slot = (x + nx - e) % nx
        parts.append((pxr[0, slot].astype(F32), mxr[0, slot]))
    last_rows, _ = merge(parts)
    attention = jnp.concatenate([first_rows, last_rows], axis=0)
    attention = attention.T.astype(BF16)
    both = jnp.concatenate([attention[:half_span], attention[half_span:]], axis=1)
    arrived(wout.at[0], wc_r.at[0])


    def yx(q, d):
        return remote(
            yxs.at[q, (x + d) % nx], yxr.at[q, x], yx_s.at[0], yx_r.at[q], to_x(d)
        )

    def yz(q, d):
        return pltpu.make_async_remote_copy(
            src_ref=yzs.at[q, (z + d) % nz],
            dst_ref=yzr.at[q, z],
            send_sem=yz_s.at[0],
            recv_sem=yz_r.at[q],
            device_id={"kvp": to_z(d), "section": after},
            device_id_type=MESH,
        )

    def vz(d):
        return remote(vzs.at[(z + d) % nz], vzr.at[z], vz_s.at[0], vz_r.at[0], to_z(d))

    def vx(d):
        return pltpu.make_async_remote_copy(
            src_ref=vxs.at[(x + d) % nx],
            dst_ref=vxr.at[x],
            send_sem=vx_s.at[0],
            recv_sem=vx_r.at[0],
            device_id={"kvp": to_x(d), "section": after},
            device_id_type=MESH,
        )

    def by_owner(sums):
        rows = jnp.concatenate([sums[:, j * thin : (j + 1) * thin] for j in range(8)], axis=0)
        return dot(gather, rows).astype(BF16).reshape(nz, 16, thin)

    def sum_x(q):
        sums = yown[q, pl.ds(pl.multiple_of(x * 2 * nz, 2 * nz), 2 * nz)]
        arrived(yxr.at[q, pl.ds(0, nx - 1)], yx_r.at[q])
        for d in range(1, nx):
            sums = sums + yxr[q, (x + nx - d) % nx].astype(F32)
        yzs[q] = by_owner(sums.astype(BF16))
        for d in [*far_first, 0]:
            yz(q, d).start()

    for q in range(SPLIT):
        sums = dot(both, wout[:, :, q * wide : (q + 1) * wide].reshape(CORES * HD, wide))
        blocks = sums.astype(BF16).reshape(nx, 2 * nz, wide)
        if q > 0:
            yown[q] = sums
            yxs[q] = blocks
            for d in range(1, nx):
                yx(q, d).start()
        else:
            for i in range(nx):
                vzs[:, i] = by_owner(blocks[i])
            for d in far_first:
                vz(d).start()
    for q in range(1, SPLIT - 1):
        sum_x(q)
    arrived(vzr.at[pl.ds(0, nz - 1)], vz_r.at[0])
    for i in range(nx):
        sums = vzs[z, i].astype(F32)
        for d in range(1, nz):
            sums = sums + vzr[(z + nz - d) % nz, i].astype(F32)
        vxs[i] = sums.astype(BF16)
    for d in range(nx):
        vx((d + 1) % nx).start()
    sum_x(SPLIT - 1)

    residual().wait_recv()
    for q in [*range(1, SPLIT - 1), 0, SPLIT - 1]:
        sums = finr[q].astype(F32)
        if q > 0:
            arrived(yzr.at[q], yz_r.at[q])
            for d in range(nz):
                sums = sums + yzr[q, (z + nz - d) % nz].astype(F32)
        else:
            arrived(vxr, vx_r.at[0])
            for d in range(nx):
                sums = sums + vxr[(x + nx - d) % nx].astype(F32)
        stage_o[...] = sums
        for j in range(8):
            start = q * wide + j * thin
            out[0, :, start : start + thin] = stage_o[2 * j : 2 * j + 2, :].astype(BF16)

    tail = pl.ds(1, SPLIT - 1)
    near_x = pl.ds(0, nx - 1)
    near_z = pl.ds(0, nz - 1)
    main = pl.ds(0, MAIN)
    rest = pl.ds(MAIN, HD - MAIN)
    left(hbuf.at[0, near_x], hx_s.at[0])
    left(hbuf.at[near_z], hz_s.at[0])
    left(gbuf.at[tail, near_z], az_s.at[0])
    left(xbuf.at[tail, near_x], ax_s.at[0])
    left(wq.at[0], dc_s.at[0])
    left(wkv.at[0], ec_s.at[0])
    left(fpair.at[0], fc_s.at[0])
    left(kv.at[0], kc_s.at[0])
    left(limits.at[0], bc_s.at[0])
    left(qbuf.at[near_z, 0, main], qz_s.at[0])
    left(qbuf.at[:, near_x, main], qx_s.at[0])
    left(qbuf.at[0, near_x, rest], rx_s.at[0])
    left(qbuf.at[near_z, :, rest], rz_s.at[0])
    left(oxs.at[:, near_x], ox_s.at[0])
    left(lxs.at[:, near_x], lx_s.at[0])
    left(ozs.at[near_z], oz_s.at[0])
    left(lzs.at[near_z], lz_s.at[0])
    left(pzs.at[near_z], pz_s.at[0])
    left(mzs.at[near_z], mz_s.at[0])
    left(pxs.at[0, near_x], px_s.at[0])
    left(mxs.at[0, near_x], mx_s.at[0])
    left(wout.at[0], wc_s.at[0])
    left(yxs.at[tail, near_x], yx_s.at[0])
    left(yzs.at[tail], yz_s.at[0])
    left(vzs.at[near_z], vz_s.at[0])
    left(vxs, vx_s.at[0])
    left(fin, sec_s.at[0])

    @pl.when(fresh_head == z)
    def _():
        left(fbuf.at[pl.ds(0, 2 * nx - 1)], f_s.at[0])

    @pl.when(fresh_head != z)
    def _():
        left(fbuf, f_s.at[0])


def local(n, nx, sections, hidden, norm_gain, w_query, w_kv, w_out, doc_cache, page_table, page_count):
    nz = n // (CORES * nx)
    span = 2 * n
    model = hidden.shape[-1]
    wide = model // SPLIT
    thin = wide // 8
    fresh_rows = w_kv.shape[-1]
    pages = doc_cache.shape[1]
    rest = HD - MAIN
    vmem = pl.BlockSpec(memory_space=pltpu.VMEM)
    smem = pl.BlockSpec(memory_space=pltpu.SMEM)
    anywhere = pl.BlockSpec(memory_space=pl.ANY)
    dma = pltpu.SemaphoreType.DMA

    def pair(waits):
        return [dma((1,)), dma((waits,))]

    scratch = [
        pltpu.VMEM((CORES, model, HD), BF16),
        pltpu.VMEM((nx, fresh_rows, model), BF16),
        pltpu.VMEM((CORES, HD, model), BF16),
        pltpu.VMEM((CORES, 2 * nz, pages, HD, HD), BF16),
        pltpu.VMEM((CORES, nz, HD, pages * HD), BF16),
        pltpu.VMEM((CORES, 8, span), F32),
        pltpu.VMEM((SPLIT, 16, thin), F32),
        pltpu.VMEM((SPLIT, 16, thin), F32),
        pltpu.VMEM((16, thin), F32),
        pltpu.VMEM((SPLIT, nz, 16, thin), BF16),
        pltpu.VMEM((nz, nx, 16, thin), BF16),
        pltpu.VMEM((SPLIT, nx, 2 * nz, wide), BF16),
        pltpu.VMEM((nz, nx, HD, span), BF16),
        pltpu.VMEM((CORES, span // CORES, HD), BF16),
        pltpu.VMEM((nx, fresh_rows, span), BF16),
        pltpu.VMEM((fresh_rows, span), BF16),
        pltpu.VMEM((2 * nx, fresh_rows, span), BF16),
        pltpu.VMEM((nz, nx, MAIN, span), BF16),
        pltpu.VMEM((nz, nx, MAIN, span), BF16),
        pltpu.VMEM((nz, nx, 1, span), F32),
        pltpu.VMEM((nz, nx, 1, span), F32),
        pltpu.VMEM((nz, MAIN, span), BF16),
        pltpu.VMEM((nz, MAIN, span), BF16),
        pltpu.VMEM((nz, 1, span), F32),
        pltpu.VMEM((nz, 1, span), F32),
        pltpu.VMEM((nz, nx, rest, span), BF16),
        pltpu.VMEM((nz, nx, rest, span), BF16),
        pltpu.VMEM((nz, nx, 1, span), F32),
        pltpu.VMEM((nz, nx, 1, span), F32),
        pltpu.VMEM((1, nx, rest, span), BF16),
        pltpu.VMEM((1, nx, rest, span), BF16),
        pltpu.VMEM((1, nx, 1, span), F32),
        pltpu.VMEM((1, nx, 1, span), F32),
        pltpu.VMEM((SPLIT, span // CORES, wide), F32),
        pltpu.VMEM((SPLIT, nx, 2 * nz, wide), BF16),
        pltpu.VMEM((SPLIT, nx, 2 * nz, wide), BF16),
        pltpu.VMEM((SPLIT, nz, 16, thin), BF16),
        pltpu.VMEM((SPLIT, nz, 16, thin), BF16),
        pltpu.VMEM((nz, nx, 16, thin), BF16),
        pltpu.VMEM((nz, nx, 16, thin), BF16),
        pltpu.VMEM((nx, 16, thin), BF16),
        pltpu.VMEM((nx, 16, thin), BF16),
        pltpu.VMEM((SPLIT, 16, thin), BF16),
        pltpu.VMEM((SPLIT, 16, thin), BF16),
        dma((3,)),
        dma((1,)),
        *pair(1),
        *pair(1),
        *pair(SPLIT),
        *pair(SPLIT),
        *pair(1),
        *pair(1),
        *pair(1),
        *pair(1),
        *pair(1),
        *pair(nz - 1),
        *pair(nz),
        *pair(1),
        *pair(nz - 1),
        *pair(1),
        *pair(nz),
        *pair(nz),
        *pair(1),
        *pair(1),
        *pair(1),
        *pair(1),
        *pair(1),
        *pair(1),
        *pair(1),
        *pair(SPLIT),
        *pair(SPLIT),
        *pair(1),
        *pair(1),
        *pair(1),
    ]
    return pl.pallas_call(
        functools.partial(kernel, n, nz, nx, sections),
        out_shape=jax.ShapeDtypeStruct(hidden.shape, BF16),
        in_specs=[vmem, vmem, anywhere, anywhere, anywhere, anywhere, smem, smem],
        out_specs=vmem,
        scratch_shapes=scratch,
        compiler_params=pltpu.CompilerParams(
            collective_id=0, has_side_effects=True, vmem_limit_bytes=56 * 1024 * 1024
        ),
    )(hidden, norm_gain, w_query, jnp.swapaxes(w_kv, 1, 2), w_out, doc_cache, page_table, page_count)


def solution(mesh):
    placed = (
        P("section", "kvp", None),
        P("section", None),
        P("section", None, "kvp"),
        P("section", None, "kvp"),
        P("section", "kvp", None),
        P("section", "kvp", None, None),
        P("section", "kvp", None),
        P("section", "kvp"),
    )
    n = mesh.shape["kvp"]
    nx = RINGX if n >= 32 else 2
    return jax.shard_map(
        functools.partial(local, n, nx, mesh.shape["section"]),
        mesh=mesh,
        in_specs=placed,
        out_specs=P("section", "kvp", None),
        check_vma=False,
    )
```

```python
import functools
import math

import jax
import jax.numpy as jnp
from jax import lax
from jax.experimental import pallas as pl
from jax.experimental.pallas import tpu as pltpu
from jax.sharding import PartitionSpec as P

MESH = pl.DeviceIdType.MESH
F32 = jnp.float32
BF16 = jnp.bfloat16

HD = 128
CORES = 2
RINGX = 4
SPLIT = 4
MAIN = 96
EPSILON = 1e-05
BIG = 1e30
LOG2E = 1.4426950408889634
AHEAD = 5
LAG = 6


def dot(a, b, dims=((1,), (0,))):
    return lax.dot_general(a, b, (dims, ((), ())), preferred_element_type=F32)


def row_order(rows, nz, inverse):
    pieces = rows // (2 * nz)
    out_row = lax.broadcasted_iota(jnp.int32, (rows, rows), 0)
    in_row = lax.broadcasted_iota(jnp.int32, (rows, rows), 1)
    if inverse:
        out_row, in_row = in_row, out_row
    r = out_row % 2
    z = (out_row // 2) % nz
    piece = out_row // (2 * nz)
    return jnp.where(in_row == (z * pieces + piece) * 2 + r, 1.0, 0.0).astype(BF16)


def merge(parts):
    top = parts[0][1]
    for _, level in parts[1:]:
        top = jnp.maximum(top, level)
    total = None
    mixed = None
    for value, level in parts:
        weight = jnp.exp2(level - top)
        total = weight if total is None else total + weight
        mixed = value * weight if mixed is None else mixed + value * weight
    return mixed * (1.0 / total), top + jnp.log(total) * LOG2E


def kernel(
    n,
    nz,
    nx,
    sections,
    hid,
    gain,
    wq_hbm,
    wkv_hbm,
    wout_hbm,
    pool_hbm,
    table,
    count,
    out,
    wq,
    wkv,
    wout,
    kv,
    vt,
    limits,
    stage_x,
    stage_n,
    stage_o,
    gbuf,
    hbuf,
    xbuf,
    qbuf,
    fpair,
    fturn,
    fown,
    fbuf,
    oxs,
    oxr,
    lxs,
    lxr,
    ozs,
    ozr,
    lzs,
    lzr,
    pzs,
    pzr,
    mzs,
    mzr,
    pxs,
    pxr,
    mxs,
    mxr,
    yown,
    yxs,
    yxr,
    yzs,
    yzr,
    vzs,
    vzr,
    vxs,
    vxr,
    fin,
    finr,
    load_sem,
    kv_sem,
    kc_s,
    kc_r,
    bc_s,
    bc_r,
    az_s,
    az_r,
    ax_s,
    ax_r,
    dc_s,
    dc_r,
    ec_s,
    ec_r,
    fc_s,
    fc_r,
    hx_s,
    hx_r,
    hz_s,
    hz_r,
    qz_s,
    qz_r,
    qx_s,
    qx_r,
    rx_s,
    rx_r,
    rz_s,
    rz_r,
    f_s,
    f_r,
    ox_s,
    ox_r,
    lx_s,
    lx_r,
    oz_s,
    oz_r,
    lz_s,
    lz_r,
    pz_s,
    pz_r,
    mz_s,
    mz_r,
    px_s,
    px_r,
    mx_s,
    mx_r,
    wc_s,
    wc_r,
    yx_s,
    yx_r,
    yz_s,
    yz_r,
    vz_s,
    vz_r,
    vx_s,
    vx_r,
    sec_s,
    sec_r,
):
    kvh = nz
    span = 2 * n
    half_span = span // CORES
    model = hid.shape[-1]
    wide = model // SPLIT
    thin = wide // 8
    pages = pool_hbm.shape[1]
    scale = HD ** (-0.5) * LOG2E

    me = lax.axis_index("kvp")
    section = lax.axis_index("section")
    c = me % CORES
    x = (me // CORES) % nx
    z = me // (CORES * nx)
    half = n // 2
    fresh_head = (me % half) // nx
    fresh_piece = (me // half) * nx + me % nx

    def at(zz, xx, cc):
        return (zz * nx + xx) * CORES + cc

    peer = at(z, x, 1 - c)

    def remote(src, dst, send, recv, target):
        return pltpu.make_async_remote_copy(
            src_ref=src,
            dst_ref=dst,
            send_sem=send,
            recv_sem=recv,
            device_id={"kvp": target},
            device_id_type=MESH,
        )

    def arrived(region, sem):
        remote(region, region, sem, sem, peer).wait_recv()

    def left(region, sem):
        remote(region, region, sem, sem, peer).wait_send()

    across = sorted(range(1, nx), key=lambda d: -min(d, nx - d))
    near_first = sorted(range(1, nz), key=lambda d: min(d, nz - d))
    far_first = sorted(range(1, nz), key=lambda d: -min(d, nz - d))

    def to_z(d):
        return at((z + d) % nz, x, c)

    def to_x(d):
        return at(z, (x + d) % nx, c)

    loads = [
        pltpu.make_async_copy(wq_hbm.at[0], wq.at[c], load_sem.at[0]),
        pltpu.make_async_copy(wkv_hbm.at[0], wkv.at[c], load_sem.at[1]),
        pltpu.make_async_copy(wout_hbm.at[0], wout.at[c], load_sem.at[2]),
    ]
    kv_loads = [
        pltpu.make_async_copy(pool_hbm.at[0, :, :, pl.ds(i * HD, HD)], kv.at[c, i], kv_sem.at[0])
        for i in range(2 * kvh)
    ]
    for load in loads[:2] + kv_loads + loads[2:]:
        load.start()

    barrier = pltpu.get_barrier_semaphore()

    def greet(target):
        pl.semaphore_signal(barrier, inc=1, device_id={"kvp": target}, device_id_type=MESH)

    for d in range(1, nz):
        greet(to_z(d))
    for d in range(1, nx):
        greet(to_x(d))
    greet(peer)
    before = (section + sections - 1) % sections
    after = (section + 1) % sections
    pl.semaphore_signal(barrier, inc=1, device_id={"section": before}, device_id_type=MESH)

    values = hid[0].astype(F32)
    inv_rms = lax.rsqrt(jnp.mean(values * values, axis=-1, keepdims=True) + EPSILON)
    normed = (values * inv_rms * gain[...].astype(F32)).astype(BF16).astype(F32)
    for q in range(SPLIT):
        for j in range(8):
            start = q * wide + j * thin
            stage_n[q, 2 * j : 2 * j + 2, :] = normed[:, start : start + thin]
            stage_x[q, 2 * j : 2 * j + 2, :] = values[:, start : start + thin]
    for q in range(SPLIT):
        if q > 0:
            gbuf[q, z] = stage_n[q].astype(BF16)
        else:
            hbuf[z, x] = stage_n[q].astype(BF16)
        fin[q] = stage_x[q].astype(BF16)

    pl.semaphore_wait(barrier, (nz - 1) + (nx - 1) + 1 + 1)

    def residual():
        return pltpu.make_async_remote_copy(
            src_ref=fin,
            dst_ref=finr,
            send_sem=sec_s.at[0],
            recv_sem=sec_r.at[0],
            device_id={"section": after},
            device_id_type=MESH,
        )

    def az(q, d):
        return remote(gbuf.at[q, z], gbuf.at[q, z], az_s.at[0], az_r.at[q], to_z(d))

    def ax(q, d):
        slot = xbuf.at[q, x]
        return remote(slot, slot, ax_s.at[0], ax_r.at[q], to_x(d))

    def hx(d):
        return remote(hbuf.at[z, x], hbuf.at[z, x], hx_s.at[0], hx_r.at[0], to_x(d))

    def hz(d):
        return remote(hbuf.at[z], hbuf.at[z], hz_s.at[0], hz_r.at[0], to_z(d))

    for d in range(1, nx):
        hx(d).start()
    for q in range(1, SPLIT):
        for d in far_first:
            az(q, d).start()
    arrived(hbuf.at[0, pl.ds(0, nx - 1)], hx_r.at[0])
    for d in far_first:
        hz(d).start()
    residual().start()

    row = lax.broadcasted_iota(jnp.int32, (8, span), 0)
    bounds = jnp.zeros((8, span), F32)
    for slot in range(pages):
        bound = jnp.float32(BIG)
        for j in range(pages):
            named = jnp.logical_and(table[0, 0, j] == slot, j < count[0, 0])
            bound = jnp.where(named, jnp.float32(-BIG), bound)
        bounds = jnp.where(row == slot, bound, bounds)
    limits[c] = bounds

    if wkv.shape[0] > CORES:
        wkv[CORES:] = jnp.zeros((wkv.shape[0] - CORES, *wkv.shape[1:]), BF16)
    loads[0].wait()
    remote(wq.at[c], wq.at[c], dc_s.at[0], dc_r.at[0], peer).start()
    loads[1].wait()
    remote(wkv.at[c], wkv.at[c], ec_s.at[0], ec_r.at[0], peer).start()
    pltpu.make_async_copy(kv.at[c], kv.at[c], kv_sem.at[0]).wait()
    remote(kv.at[c], kv.at[c], kc_s.at[0], kc_r.at[0], peer).start()
    remote(limits.at[c], limits.at[c], bc_s.at[0], bc_r.at[0], peer).start()
    loads[2].wait()
    remote(wout.at[c], wout.at[c], wc_s.at[0], wc_r.at[0], peer).start()

    def transpose_values(core):
        @pl.loop(0, kvh)
        def _(g):
            vt[core, g] = kv[core, kvh + g].reshape(pages * HD, HD).T

    transpose_values(c)
    spread = row_order(16 * nz, nz, False)
    gather = row_order(16 * nz, nz, True)

    queries = [jnp.zeros((half_span, HD), F32) for _ in range(CORES)]
    fresh = jnp.zeros((half_span, HD), F32)
    order = [*range(1, SPLIT), 0]
    for t in range(SPLIT + 1):
        if t < SPLIT - 1:
            q = order[t]
            arrived(gbuf.at[q, pl.ds(0, nz - 1)], az_r.at[q])
            rows = dot(spread, gbuf[q].reshape(16 * nz, thin)).astype(BF16)
            for j in range(8):
                xbuf[q, x, :, j * thin : (j + 1) * thin] = rows[j * 2 * nz : (j + 1) * 2 * nz]
            for d in across:
                ax(q, d).start()
        elif t == SPLIT - 1:
            arrived(hbuf.at[pl.ds(0, nz - 1)], hz_r.at[0])
            for i in range(nx):
                block = jnp.concatenate([hbuf[k, i] for k in range(nz)], axis=0)
                rows = dot(spread, block).astype(BF16)
                for j in range(8):
                    xbuf[0, i, :, j * thin : (j + 1) * thin] = rows[j * 2 * nz : (j + 1) * 2 * nz]
        if t == 1:
            arrived(kv.at[0], kc_r.at[0])
            arrived(limits.at[0], bc_r.at[0])
            transpose_values(1 - c)
            arrived(wq.at[0], dc_r.at[0])
            arrived(wkv.at[0], ec_r.at[0])
        if t >= 1:
            q = order[t - 1]
            if q > 0:
                arrived(xbuf.at[q, pl.ds(0, nx - 1)], ax_r.at[q])
            block = xbuf[q].reshape(half_span, wide)
            cols = slice(q * wide, (q + 1) * wide)
            queries = [queries[h] + dot(block, wq[h, cols]) for h in range(CORES)]
            fresh = fresh + dot(block, wkv[:, :, cols].reshape(HD, wide), ((1,), (1,)))

    qbuf[z, x] = jnp.concatenate(queries, axis=0).T.astype(BF16)
    fpair[c] = fresh.astype(BF16)
    remote(fpair.at[c], fpair.at[c], fc_s.at[0], fc_r.at[0], peer).start()

    def qz(d):
        slot = qbuf.at[z, x, pl.ds(0, MAIN)]
        return remote(slot, slot, qz_s.at[0], qz_r.at[d - 1], to_z(d))

    def qx(g, d):
        slot = qbuf.at[g, x, pl.ds(0, MAIN)]
        return remote(slot, slot, qx_s.at[0], qx_r.at[g], to_x(d))

    def rx(d):
        slot = qbuf.at[z, x, pl.ds(MAIN, HD - MAIN)]
        return remote(slot, slot, rx_s.at[0], rx_r.at[0], to_x(d))

    def rz(d):
        slot = qbuf.at[z, :, pl.ds(MAIN, HD - MAIN)]
        return remote(slot, slot, rz_s.at[0], rz_r.at[d - 1], to_z(d))

    def fresh_out(i):
        return remote(
            fown,
            fbuf.at[fresh_piece],
            f_s.at[0],
            f_r.at[0],
            fresh_head * CORES * nx + i,
        )

    for d in range(1, nx):
        rx(d).start()
    for d in near_first:
        qz(d).start()
    for d in range(1, nx):
        qx(z, d).start()
    def attend(g):
        cols = jnp.concatenate([qbuf[g, i] for i in range(nx)], axis=1)
        parts = []
        bounds = []
        for core in range(CORES):
            scores = dot(kv[core, g].reshape(pages * HD, HD), cols)
            parts += [scores[p * HD : (p + 1) * HD] for p in range(pages)]
            bounds += [jnp.concatenate([limits[core, p : p + 1]] * nx, axis=1) for p in range(pages)]
        top = None
        for part, bound in zip(parts, bounds):
            here = jnp.minimum(jnp.max(part, axis=0, keepdims=True), -bound)
            top = here if top is None else jnp.maximum(top, here)
        total = None
        weights = []
        for part, bound in zip(parts, bounds):
            weight = jnp.exp2((part - jnp.maximum(top, bound)) * scale)
            add = jnp.sum(weight, axis=0, keepdims=True)
            total = add if total is None else total + add
            weights.append(weight.astype(BF16))
        mixed = None
        for core in range(CORES):
            here = jnp.concatenate(weights[core * pages : (core + 1) * pages], axis=0)
            here = dot(vt[core, g], here)
            mixed = here if mixed is None else mixed + here
        return mixed * (1.0 / total), top * scale + jnp.log(total) * LOG2E

    def along_x(send, recv, send_sem, recv_sem):
        def out_copy(g, d):
            return remote(
                send.at[g, (x + d) % nx], recv.at[g, x], send_sem.at[0], recv_sem.at[g], to_x(d)
            )

        return out_copy, lambda g: arrived(recv.at[g, pl.ds(0, nx - 1)], recv_sem.at[g])

    def along_z(send, recv, send_sem, recv_sem):
        def out_copy(g):
            return remote(send.at[g], recv.at[z], send_sem.at[0], recv_sem.at[0], at(g, x, c))

        return out_copy, lambda: arrived(recv.at[pl.ds(0, nz - 1)], recv_sem.at[0])

    ox, ox_in = along_x(oxs, oxr, ox_s, ox_r)
    lx, lx_in = along_x(lxs, lxr, lx_s, lx_r)
    oz, oz_in = along_z(ozs, ozr, oz_s, oz_r)
    lz, lz_in = along_z(lzs, lzr, lz_s, lz_r)
    pz, pz_in = along_z(pzs, pzr, pz_s, pz_r)
    mz, mz_in = along_z(mzs, mzr, mz_s, mz_r)
    px, px_in = along_x(pxs, pxr, px_s, px_r)
    mx, mx_in = along_x(mxs, mxr, mx_s, mx_r)

    def offset(s):
        return (nz + ((s + 1) // 2) * (2 * (s % 2) - 1)) % nz

    def forward(s):
        d = offset(s)
        g = (z + d) % nz
        arrived(qbuf.at[g, 0, pl.ds(0, MAIN)], qz_r.at[nz - d - 1])
        for e in across:
            qx(g, e).start()

    arrived(qbuf.at[0, pl.ds(0, nx - 1), pl.ds(MAIN, HD - MAIN)], rx_r.at[0])
    for d in near_first:
        rz(d).start()
    for s in range(1, min(AHEAD, nz)):
        forward(s)

    @pl.loop(0, nz + LAG)
    def _(t):
        @pl.when(t < nz - AHEAD)
        def _():
            forward(t + AHEAD)

        @pl.when(t < nz)
        def _():
            d = offset(t)
            g = (z + d) % nz
            arrived(qbuf.at[g, pl.ds(0, nx - 1), pl.ds(0, MAIN)], qx_r.at[g])

            @pl.when(t > 0)
            def _():
                arrived(qbuf.at[g, :, pl.ds(MAIN, HD - MAIN)], rz_r.at[nz - d - 1])

            mixed, level = attend(g)
            for i in range(nx):
                cols = slice(i * span, (i + 1) * span)
                oxs[g, i] = mixed[:MAIN, cols].astype(BF16)
                pzs[g, i] = mixed[MAIN:, cols].astype(BF16)
                lxs[g, i] = level[:, cols]
                mzs[g, i] = level[:, cols]
            for e in across:
                lx(g, e).start()
            for e in across:
                ox(g, e).start()

            @pl.when(t > 0)
            def _():
                mz(g).start()
                pz(g).start()

        @pl.when(t == 1)
        def _():
            arrived(fpair.at[0], fc_r.at[0])
            fturn[...] = fpair[...].astype(F32).reshape(span, HD).T.astype(BF16).reshape(fturn.shape)
            fown[...] = fturn[c]
            for i in range(2 * nx):
                target = fresh_head * CORES * nx + i

                @pl.when(target != me)
                def _():
                    fresh_out(i).start()

                @pl.when(target == me)
                def _():
                    pltpu.make_async_copy(fown, fbuf.at[fresh_piece], f_r.at[0]).start()


        @pl.when(t >= LAG)
        def _():
            d = offset(t - LAG)
            g = (z + d) % nz
            ox_in(g)
            lx_in(g)
            parts = [(oxs[g, x].astype(F32), lxs[g, x])]
            for e in range(1, nx):
                slot = (x + e) % nx
                parts.append((oxr[g, slot].astype(F32), lxr[g, slot]))
            value, level = merge(parts)
            ozs[g] = value.astype(BF16)
            lzs[g] = level

            @pl.when(t > LAG)
            def _():
                lz(g).start()
                oz(g).start()

    pz_in()
    mz_in()
    for i in range(nx):
        parts = [(pzs[z, i].astype(F32), mzs[z, i])]
        for d in range(1, nz):
            slot = (z + nz - d) % nz
            parts.append((pzr[slot, i].astype(F32), mzr[slot, i]))
        value, level = merge(parts)
        pxs[0, i] = value.astype(BF16)
        mxs[0, i] = level
    for e in range(1, nx):
        px(0, e).start()
        mx(0, e).start()

    arrived(fbuf, f_r.at[0])
    new_keys = fbuf[:nx].reshape(HD, span)
    new_values = fbuf[nx:].reshape(HD, span)

    def token(row):
        r = row % 2
        tz = (row // 2) % nz
        tx = (row // (2 * nz)) % nx
        tc = row // (2 * nz * nx)
        return ((tz * nx + tx) * CORES + tc) * 2 + r

    key_row = lax.broadcasted_iota(jnp.int32, (span, span), 0)
    query_lane = lax.broadcasted_iota(jnp.int32, (span, span), 1)
    causal = token(key_row) <= token(c * half_span + query_lane % half_span)
    scores = dot(new_keys.T, qbuf[z, x])
    scores = jnp.where(causal, scores, -BIG)
    top = jnp.max(scores, axis=0, keepdims=True)
    weights = jnp.where(causal, jnp.exp2((scores - top) * scale), 0.0)
    total = jnp.sum(weights, axis=0, keepdims=True)
    own = dot(new_values, weights.astype(BF16)) * (1.0 / total)
    own_lsum = top * scale + jnp.log(total) * LOG2E
    parts = [(own[:MAIN], own_lsum), (ozs[z].astype(F32), lzs[z])]
    oz_in()
    lz_in()
    for d in range(1, nz):
        slot = (z + nz - d) % nz
        parts.append((ozr[slot].astype(F32), lzr[slot]))
    first_rows, _ = merge(parts)
    parts = [(own[MAIN:], own_lsum), (pxs[0, x].astype(F32), mxs[0, x])]
    px_in(0)
    mx_in(0)
    for e in range(1, nx):
        slot = (x + nx - e) % nx
        parts.append((pxr[0, slot].astype(F32), mxr[0, slot]))
    last_rows, _ = merge(parts)
    attention = jnp.concatenate([first_rows, last_rows], axis=0)
    attention = attention.T.astype(BF16)
    both = jnp.concatenate([attention[:half_span], attention[half_span:]], axis=1)
    arrived(wout.at[0], wc_r.at[0])


    def yx(q, d):
        return remote(
            yxs.at[q, (x + d) % nx], yxr.at[q, x], yx_s.at[0], yx_r.at[q], to_x(d)
        )

    def yz(q, d):
        return pltpu.make_async_remote_copy(
            src_ref=yzs.at[q, (z + d) % nz],
            dst_ref=yzr.at[q, z],
            send_sem=yz_s.at[0],
            recv_sem=yz_r.at[q],
            device_id={"kvp": to_z(d), "section": after},
            device_id_type=MESH,
        )

    def vz(d):
        return remote(vzs.at[(z + d) % nz], vzr.at[z], vz_s.at[0], vz_r.at[0], to_z(d))

    def vx(d):
        return pltpu.make_async_remote_copy(
            src_ref=vxs.at[(x + d) % nx],
            dst_ref=vxr.at[x],
            send_sem=vx_s.at[0],
            recv_sem=vx_r.at[0],
            device_id={"kvp": to_x(d), "section": after},
            device_id_type=MESH,
        )

    def by_owner(sums):
        rows = jnp.concatenate([sums[:, j * thin : (j + 1) * thin] for j in range(8)], axis=0)
        return dot(gather, rows).astype(BF16).reshape(nz, 16, thin)

    def sum_x(q):
        sums = yown[q, pl.ds(pl.multiple_of(x * 2 * nz, 2 * nz), 2 * nz)]
        arrived(yxr.at[q, pl.ds(0, nx - 1)], yx_r.at[q])
        for d in range(1, nx):
            sums = sums + yxr[q, (x + nx - d) % nx].astype(F32)
        yzs[q] = by_owner(sums.astype(BF16))
        for d in [*far_first, 0]:
            yz(q, d).start()

    for q in [1, 0, *range(2, SPLIT)]:
        sums = dot(both, wout[:, :, q * wide : (q + 1) * wide].reshape(CORES * HD, wide))
        blocks = sums.astype(BF16).reshape(nx, 2 * nz, wide)
        if q > 0:
            yown[q] = sums
            yxs[q] = blocks
            for d in across:
                yx(q, d).start()
        else:
            for i in range(nx):
                vzs[:, i] = by_owner(blocks[i])
            for d in far_first:
                vz(d).start()
    for q in range(1, SPLIT - 1):
        sum_x(q)
    arrived(vzr.at[pl.ds(0, nz - 1)], vz_r.at[0])
    for i in range(nx):
        sums = vzs[z, i].astype(F32)
        for d in range(1, nz):
            sums = sums + vzr[(z + nz - d) % nz, i].astype(F32)
        vxs[i] = sums.astype(BF16)
    for d in range(nx):
        vx((d + 1) % nx).start()
    sum_x(SPLIT - 1)

    residual().wait_recv()
    for q in [*range(1, SPLIT - 1), 0, SPLIT - 1]:
        sums = finr[q].astype(F32)
        if q > 0:
            arrived(yzr.at[q], yz_r.at[q])
            for d in range(nz):
                sums = sums + yzr[q, (z + nz - d) % nz].astype(F32)
        else:
            arrived(vxr, vx_r.at[0])
            for d in range(nx):
                sums = sums + vxr[(x + nx - d) % nx].astype(F32)
        stage_o[...] = sums
        for j in range(8):
            start = q * wide + j * thin
            out[0, :, start : start + thin] = stage_o[2 * j : 2 * j + 2, :].astype(BF16)

    tail = pl.ds(1, SPLIT - 1)
    near_x = pl.ds(0, nx - 1)
    near_z = pl.ds(0, nz - 1)
    main = pl.ds(0, MAIN)
    rest = pl.ds(MAIN, HD - MAIN)
    left(hbuf.at[0, near_x], hx_s.at[0])
    left(hbuf.at[near_z], hz_s.at[0])
    left(gbuf.at[tail, near_z], az_s.at[0])
    left(xbuf.at[tail, near_x], ax_s.at[0])
    left(wq.at[0], dc_s.at[0])
    left(wkv.at[0], ec_s.at[0])
    left(fpair.at[0], fc_s.at[0])
    left(kv.at[0], kc_s.at[0])
    left(limits.at[0], bc_s.at[0])
    left(qbuf.at[near_z, 0, main], qz_s.at[0])
    left(qbuf.at[:, near_x, main], qx_s.at[0])
    left(qbuf.at[0, near_x, rest], rx_s.at[0])
    left(qbuf.at[near_z, :, rest], rz_s.at[0])
    left(oxs.at[:, near_x], ox_s.at[0])
    left(lxs.at[:, near_x], lx_s.at[0])
    left(ozs.at[near_z], oz_s.at[0])
    left(lzs.at[near_z], lz_s.at[0])
    left(pzs.at[near_z], pz_s.at[0])
    left(mzs.at[near_z], mz_s.at[0])
    left(pxs.at[0, near_x], px_s.at[0])
    left(mxs.at[0, near_x], mx_s.at[0])
    left(wout.at[0], wc_s.at[0])
    left(yxs.at[tail, near_x], yx_s.at[0])
    left(yzs.at[tail], yz_s.at[0])
    left(vzs.at[near_z], vz_s.at[0])
    left(vxs, vx_s.at[0])
    left(fin, sec_s.at[0])

    @pl.when(fresh_head == z)
    def _():
        left(fbuf.at[pl.ds(0, 2 * nx - 1)], f_s.at[0])

    @pl.when(fresh_head != z)
    def _():
        left(fbuf, f_s.at[0])


def local(n, nx, sections, hidden, norm_gain, w_query, w_kv, w_out, doc_cache, page_table, page_count):
    nz = n // (CORES * nx)
    span = 2 * n
    model = hidden.shape[-1]
    wide = model // SPLIT
    thin = wide // 8
    fresh_rows = w_kv.shape[-1]
    pages = doc_cache.shape[1]
    rest = HD - MAIN
    vmem = pl.BlockSpec(memory_space=pltpu.VMEM)
    smem = pl.BlockSpec(memory_space=pltpu.SMEM)
    anywhere = pl.BlockSpec(memory_space=pl.ANY)
    dma = pltpu.SemaphoreType.DMA

    def pair(waits):
        return [dma((1,)), dma((waits,))]

    scratch = [
        pltpu.VMEM((CORES, model, HD), BF16),
        pltpu.VMEM((nx, fresh_rows, model), BF16),
        pltpu.VMEM((CORES, HD, model), BF16),
        pltpu.VMEM((CORES, 2 * nz, pages, HD, HD), BF16),
        pltpu.VMEM((CORES, nz, HD, pages * HD), BF16),
        pltpu.VMEM((CORES, 8, span), F32),
        pltpu.VMEM((SPLIT, 16, thin), F32),
        pltpu.VMEM((SPLIT, 16, thin), F32),
        pltpu.VMEM((16, thin), F32),
        pltpu.VMEM((SPLIT, nz, 16, thin), BF16),
        pltpu.VMEM((nz, nx, 16, thin), BF16),
        pltpu.VMEM((SPLIT, nx, 2 * nz, wide), BF16),
        pltpu.VMEM((nz, nx, HD, span), BF16),
        pltpu.VMEM((CORES, span // CORES, HD), BF16),
        pltpu.VMEM((nx, fresh_rows, span), BF16),
        pltpu.VMEM((fresh_rows, span), BF16),
        pltpu.VMEM((2 * nx, fresh_rows, span), BF16),
        pltpu.VMEM((nz, nx, MAIN, span), BF16),
        pltpu.VMEM((nz, nx, MAIN, span), BF16),
        pltpu.VMEM((nz, nx, 1, span), F32),
        pltpu.VMEM((nz, nx, 1, span), F32),
        pltpu.VMEM((nz, MAIN, span), BF16),
        pltpu.VMEM((nz, MAIN, span), BF16),
        pltpu.VMEM((nz, 1, span), F32),
        pltpu.VMEM((nz, 1, span), F32),
        pltpu.VMEM((nz, nx, rest, span), BF16),
        pltpu.VMEM((nz, nx, rest, span), BF16),
        pltpu.VMEM((nz, nx, 1, span), F32),
        pltpu.VMEM((nz, nx, 1, span), F32),
        pltpu.VMEM((1, nx, rest, span), BF16),
        pltpu.VMEM((1, nx, rest, span), BF16),
        pltpu.VMEM((1, nx, 1, span), F32),
        pltpu.VMEM((1, nx, 1, span), F32),
        pltpu.VMEM((SPLIT, span // CORES, wide), F32),
        pltpu.VMEM((SPLIT, nx, 2 * nz, wide), BF16),
        pltpu.VMEM((SPLIT, nx, 2 * nz, wide), BF16),
        pltpu.VMEM((SPLIT, nz, 16, thin), BF16),
        pltpu.VMEM((SPLIT, nz, 16, thin), BF16),
        pltpu.VMEM((nz, nx, 16, thin), BF16),
        pltpu.VMEM((nz, nx, 16, thin), BF16),
        pltpu.VMEM((nx, 16, thin), BF16),
        pltpu.VMEM((nx, 16, thin), BF16),
        pltpu.VMEM((SPLIT, 16, thin), BF16),
        pltpu.VMEM((SPLIT, 16, thin), BF16),
        dma((3,)),
        dma((1,)),
        *pair(1),
        *pair(1),
        *pair(SPLIT),
        *pair(SPLIT),
        *pair(1),
        *pair(1),
        *pair(1),
        *pair(1),
        *pair(1),
        *pair(nz - 1),
        *pair(nz),
        *pair(1),
        *pair(nz - 1),
        *pair(1),
        *pair(nz),
        *pair(nz),
        *pair(1),
        *pair(1),
        *pair(1),
        *pair(1),
        *pair(1),
        *pair(1),
        *pair(1),
        *pair(SPLIT),
        *pair(SPLIT),
        *pair(1),
        *pair(1),
        *pair(1),
    ]
    return pl.pallas_call(
        functools.partial(kernel, n, nz, nx, sections),
        out_shape=jax.ShapeDtypeStruct(hidden.shape, BF16),
        in_specs=[vmem, vmem, anywhere, anywhere, anywhere, anywhere, smem, smem],
        out_specs=vmem,
        scratch_shapes=scratch,
        compiler_params=pltpu.CompilerParams(
            collective_id=0, has_side_effects=True, vmem_limit_bytes=56 * 1024 * 1024
        ),
    )(hidden, norm_gain, w_query, jnp.swapaxes(w_kv, 1, 2), w_out, doc_cache, page_table, page_count)


def solution(mesh):
    placed = (
        P("section", "kvp", None),
        P("section", None),
        P("section", None, "kvp"),
        P("section", None, "kvp"),
        P("section", "kvp", None),
        P("section", "kvp", None, None),
        P("section", "kvp", None),
        P("section", "kvp"),
    )
    n = mesh.shape["kvp"]
    nx = RINGX if n >= 32 else 2
    return jax.shard_map(
        functools.partial(local, n, nx, mesh.shape["section"]),
        mesh=mesh,
        in_specs=placed,
        out_specs=P("section", "kvp", None),
        check_vma=False,
    )
```

```python
import functools
import math

import jax
import jax.numpy as jnp
from jax import lax
from jax.experimental import pallas as pl
from jax.experimental.pallas import tpu as pltpu
from jax.sharding import PartitionSpec as P

MESH = pl.DeviceIdType.MESH
F32 = jnp.float32
BF16 = jnp.bfloat16

HD = 128
CORES = 2
RINGX = 4
SPLIT = 4
MAIN = 96
EPSILON = 1e-05
BIG = 1e30
LOG2E = 1.4426950408889634
AHEAD = 5
LAG = 6


def dot(a, b, dims=((1,), (0,))):
    return lax.dot_general(a, b, (dims, ((), ())), preferred_element_type=F32)


def row_order(rows, nz, inverse):
    pieces = rows // (2 * nz)
    out_row = lax.broadcasted_iota(jnp.int32, (rows, rows), 0)
    in_row = lax.broadcasted_iota(jnp.int32, (rows, rows), 1)
    if inverse:
        out_row, in_row = in_row, out_row
    r = out_row % 2
    z = (out_row // 2) % nz
    piece = out_row // (2 * nz)
    return jnp.where(in_row == (z * pieces + piece) * 2 + r, 1.0, 0.0).astype(BF16)


def merge(parts):
    top = parts[0][1]
    for _, level in parts[1:]:
        top = jnp.maximum(top, level)
    total = None
    mixed = None
    for value, level in parts:
        weight = jnp.exp2(level - top)
        total = weight if total is None else total + weight
        mixed = value * weight if mixed is None else mixed + value * weight
    return mixed * (1.0 / total), top + jnp.log(total) * LOG2E


def kernel(
    n,
    nz,
    nx,
    sections,
    hid,
    gain,
    wq_hbm,
    wkv_hbm,
    wout_hbm,
    pool_hbm,
    table,
    count,
    out,
    wq,
    wkv,
    wout,
    kv,
    vt,
    limits,
    stage_x,
    stage_n,
    stage_o,
    gbuf,
    hbuf,
    xbuf,
    qbuf,
    fpair,
    fturn,
    fown,
    fbuf,
    oxs,
    oxr,
    lxs,
    lxr,
    ozs,
    ozr,
    lzs,
    lzr,
    pzs,
    pzr,
    mzs,
    mzr,
    pxs,
    pxr,
    mxs,
    mxr,
    yown,
    yxs,
    yxr,
    yzs,
    yzr,
    vzs,
    vzr,
    vxs,
    vxr,
    fin,
    finr,
    load_sem,
    kv_sem,
    kc_s,
    kc_r,
    bc_s,
    bc_r,
    az_s,
    az_r,
    ax_s,
    ax_r,
    dc_s,
    dc_r,
    ec_s,
    ec_r,
    fc_s,
    fc_r,
    hx_s,
    hx_r,
    hz_s,
    hz_r,
    qz_s,
    qz_r,
    qx_s,
    qx_r,
    rx_s,
    rx_r,
    rz_s,
    rz_r,
    f_s,
    f_r,
    ox_s,
    ox_r,
    lx_s,
    lx_r,
    oz_s,
    oz_r,
    lz_s,
    lz_r,
    pz_s,
    pz_r,
    mz_s,
    mz_r,
    px_s,
    px_r,
    mx_s,
    mx_r,
    wc_s,
    wc_r,
    yx_s,
    yx_r,
    yz_s,
    yz_r,
    vz_s,
    vz_r,
    vx_s,
    vx_r,
    sec_s,
    sec_r,
):
    kvh = nz
    span = 2 * n
    half_span = span // CORES
    model = hid.shape[-1]
    wide = model // SPLIT
    thin = wide // 8
    pages = pool_hbm.shape[1]
    scale = HD ** (-0.5) * LOG2E

    me = lax.axis_index("kvp")
    section = lax.axis_index("section")
    c = me % CORES
    x = (me // CORES) % nx
    z = me // (CORES * nx)
    half = n // 2
    fresh_head = (me % half) // nx
    fresh_piece = (me // half) * nx + me % nx

    def at(zz, xx, cc):
        return (zz * nx + xx) * CORES + cc

    peer = at(z, x, 1 - c)

    def remote(src, dst, send, recv, target):
        return pltpu.make_async_remote_copy(
            src_ref=src,
            dst_ref=dst,
            send_sem=send,
            recv_sem=recv,
            device_id={"kvp": target},
            device_id_type=MESH,
        )

    def arrived(region, sem):
        remote(region, region, sem, sem, peer).wait_recv()

    def left(region, sem):
        remote(region, region, sem, sem, peer).wait_send()

    across = sorted(range(1, nx), key=lambda d: -min(d, nx - d))
    near_first = sorted(range(1, nz), key=lambda d: min(d, nz - d))
    far_first = sorted(range(1, nz), key=lambda d: -min(d, nz - d))

    def to_z(d):
        return at((z + d) % nz, x, c)

    def to_x(d):
        return at(z, (x + d) % nx, c)

    loads = [
        pltpu.make_async_copy(wq_hbm.at[0], wq.at[c], load_sem.at[0]),
        pltpu.make_async_copy(wkv_hbm.at[0], wkv.at[c], load_sem.at[1]),
        pltpu.make_async_copy(wout_hbm.at[0], wout.at[c], load_sem.at[2]),
    ]
    kv_loads = [
        pltpu.make_async_copy(pool_hbm.at[0, :, :, pl.ds(i * HD, HD)], kv.at[c, i], kv_sem.at[0])
        for i in range(2 * kvh)
    ]
    for load in loads[:2] + kv_loads + loads[2:]:
        load.start()

    barrier = pltpu.get_barrier_semaphore()

    def greet(target):
        pl.semaphore_signal(barrier, inc=1, device_id={"kvp": target}, device_id_type=MESH)

    for d in range(1, nz):
        greet(to_z(d))
    for d in range(1, nx):
        greet(to_x(d))
    greet(peer)
    before = (section + sections - 1) % sections
    after = (section + 1) % sections
    pl.semaphore_signal(barrier, inc=1, device_id={"section": before}, device_id_type=MESH)

    values = hid[0].astype(F32)
    inv_rms = lax.rsqrt(jnp.mean(values * values, axis=-1, keepdims=True) + EPSILON)
    normed = (values * inv_rms * gain[...].astype(F32)).astype(BF16).astype(F32)
    for q in range(SPLIT):
        for j in range(8):
            start = q * wide + j * thin
            stage_n[q, 2 * j : 2 * j + 2, :] = normed[:, start : start + thin]
            stage_x[q, 2 * j : 2 * j + 2, :] = values[:, start : start + thin]
    for q in range(SPLIT):
        if q > 0:
            gbuf[q, z] = stage_n[q].astype(BF16)
        else:
            hbuf[z, x] = stage_n[q].astype(BF16)
        fin[q] = stage_x[q].astype(BF16)

    pl.semaphore_wait(barrier, (nz - 1) + (nx - 1) + 1 + 1)

    def residual():
        return pltpu.make_async_remote_copy(
            src_ref=fin,
            dst_ref=finr,
            send_sem=sec_s.at[0],
            recv_sem=sec_r.at[0],
            device_id={"section": after},
            device_id_type=MESH,
        )

    def az(q, d):
        return remote(gbuf.at[q, z], gbuf.at[q, z], az_s.at[0], az_r.at[q], to_z(d))

    def ax(q, d):
        slot = xbuf.at[q, x]
        return remote(slot, slot, ax_s.at[0], ax_r.at[q], to_x(d))

    def hx(d):
        return remote(hbuf.at[z, x], hbuf.at[z, x], hx_s.at[0], hx_r.at[0], to_x(d))

    def hz(d):
        return remote(hbuf.at[z], hbuf.at[z], hz_s.at[0], hz_r.at[0], to_z(d))

    for d in across:
        hx(d).start()
    for q in range(1, SPLIT):
        for d in far_first:
            az(q, d).start()
    residual().start()

    row = lax.broadcasted_iota(jnp.int32, (8, span), 0)
    bounds = jnp.zeros((8, span), F32)
    for slot in range(pages):
        bound = jnp.float32(BIG)
        for j in range(pages):
            named = jnp.logical_and(table[0, 0, j] == slot, j < count[0, 0])
            bound = jnp.where(named, jnp.float32(-BIG), bound)
        bounds = jnp.where(row == slot, bound, bounds)
    limits[c] = bounds

    if wkv.shape[0] > CORES:
        wkv[CORES:] = jnp.zeros((wkv.shape[0] - CORES, *wkv.shape[1:]), BF16)
    loads[0].wait()
    remote(wq.at[c], wq.at[c], dc_s.at[0], dc_r.at[0], peer).start()
    loads[1].wait()
    remote(wkv.at[c], wkv.at[c], ec_s.at[0], ec_r.at[0], peer).start()
    pltpu.make_async_copy(kv.at[c], kv.at[c], kv_sem.at[0]).wait()
    remote(kv.at[c], kv.at[c], kc_s.at[0], kc_r.at[0], peer).start()
    remote(limits.at[c], limits.at[c], bc_s.at[0], bc_r.at[0], peer).start()
    loads[2].wait()
    remote(wout.at[c], wout.at[c], wc_s.at[0], wc_r.at[0], peer).start()

    def transpose_values(core):
        @pl.loop(0, kvh)
        def _(g):
            vt[core, g] = kv[core, kvh + g].reshape(pages * HD, HD).T

    arrived(hbuf.at[0, pl.ds(0, nx - 1)], hx_r.at[0])
    for d in far_first:
        hz(d).start()
    transpose_values(c)
    spread = row_order(16 * nz, nz, False)
    gather = row_order(16 * nz, nz, True)

    queries = [jnp.zeros((half_span, HD), F32) for _ in range(CORES)]
    fresh = jnp.zeros((half_span, HD), F32)
    order = [*range(1, SPLIT), 0]
    for t in range(SPLIT + 1):
        if t < SPLIT - 1:
            q = order[t]
            arrived(gbuf.at[q, pl.ds(0, nz - 1)], az_r.at[q])
            rows = dot(spread, gbuf[q].reshape(16 * nz, thin)).astype(BF16)
            for j in range(8):
                xbuf[q, x, :, j * thin : (j + 1) * thin] = rows[j * 2 * nz : (j + 1) * 2 * nz]
            for d in across:
                ax(q, d).start()
        elif t == SPLIT - 1:
            arrived(hbuf.at[pl.ds(0, nz - 1)], hz_r.at[0])
            for i in range(nx):
                block = jnp.concatenate([hbuf[k, i] for k in range(nz)], axis=0)
                rows = dot(spread, block).astype(BF16)
                for j in range(8):
                    xbuf[0, i, :, j * thin : (j + 1) * thin] = rows[j * 2 * nz : (j + 1) * 2 * nz]
        if t == 1:
            arrived(kv.at[0], kc_r.at[0])
            arrived(limits.at[0], bc_r.at[0])
            transpose_values(1 - c)
            arrived(wq.at[0], dc_r.at[0])
            arrived(wkv.at[0], ec_r.at[0])
        if t >= 1:
            q = order[t - 1]
            if q > 0:
                arrived(xbuf.at[q, pl.ds(0, nx - 1)], ax_r.at[q])
            block = xbuf[q].reshape(half_span, wide)
            cols = slice(q * wide, (q + 1) * wide)
            queries = [queries[h] + dot(block, wq[h, cols]) for h in range(CORES)]
            fresh = fresh + dot(block, wkv[:, :, cols].reshape(HD, wide), ((1,), (1,)))

    qbuf[z, x] = jnp.concatenate(queries, axis=0).T.astype(BF16)
    fpair[c] = fresh.astype(BF16)
    remote(fpair.at[c], fpair.at[c], fc_s.at[0], fc_r.at[0], peer).start()

    def qz(d):
        slot = qbuf.at[z, x, pl.ds(0, MAIN)]
        return remote(slot, slot, qz_s.at[0], qz_r.at[d - 1], to_z(d))

    def qx(g, d):
        slot = qbuf.at[g, x, pl.ds(0, MAIN)]
        return remote(slot, slot, qx_s.at[0], qx_r.at[g], to_x(d))

    def rx(d):
        slot = qbuf.at[z, x, pl.ds(MAIN, HD - MAIN)]
        return remote(slot, slot, rx_s.at[0], rx_r.at[0], to_x(d))

    def rz(d):
        slot = qbuf.at[z, :, pl.ds(MAIN, HD - MAIN)]
        return remote(slot, slot, rz_s.at[0], rz_r.at[d - 1], to_z(d))

    def fresh_out(i):
        return remote(
            fown,
            fbuf.at[fresh_piece],
            f_s.at[0],
            f_r.at[0],
            fresh_head * CORES * nx + i,
        )

    for d in across:
        rx(d).start()
    for d in near_first:
        qz(d).start()
    for d in across:
        qx(z, d).start()
    def attend(g):
        cols = jnp.concatenate([qbuf[g, i] for i in range(nx)], axis=1)
        parts = []
        bounds = []
        for core in range(CORES):
            scores = dot(kv[core, g].reshape(pages * HD, HD), cols)
            parts += [scores[p * HD : (p + 1) * HD] for p in range(pages)]
            bounds += [jnp.concatenate([limits[core, p : p + 1]] * nx, axis=1) for p in range(pages)]
        top = None
        for part, bound in zip(parts, bounds):
            here = jnp.minimum(jnp.max(part, axis=0, keepdims=True), -bound)
            top = here if top is None else jnp.maximum(top, here)
        total = None
        weights = []
        for part, bound in zip(parts, bounds):
            weight = jnp.exp2((part - jnp.maximum(top, bound)) * scale)
            add = jnp.sum(weight, axis=0, keepdims=True)
            total = add if total is None else total + add
            weights.append(weight.astype(BF16))
        mixed = None
        for core in range(CORES):
            here = jnp.concatenate(weights[core * pages : (core + 1) * pages], axis=0)
            here = dot(vt[core, g], here)
            mixed = here if mixed is None else mixed + here
        return mixed * (1.0 / total), top * scale + jnp.log(total) * LOG2E

    def along_x(send, recv, send_sem, recv_sem):
        def out_copy(g, d):
            return remote(
                send.at[g, (x + d) % nx], recv.at[g, x], send_sem.at[0], recv_sem.at[g], to_x(d)
            )

        return out_copy, lambda g: arrived(recv.at[g, pl.ds(0, nx - 1)], recv_sem.at[g])

    def along_z(send, recv, send_sem, recv_sem):
        def out_copy(g):
            return remote(send.at[g], recv.at[z], send_sem.at[0], recv_sem.at[0], at(g, x, c))

        return out_copy, lambda: arrived(recv.at[pl.ds(0, nz - 1)], recv_sem.at[0])

    ox, ox_in = along_x(oxs, oxr, ox_s, ox_r)
    lx, lx_in = along_x(lxs, lxr, lx_s, lx_r)
    oz, oz_in = along_z(ozs, ozr, oz_s, oz_r)
    lz, lz_in = along_z(lzs, lzr, lz_s, lz_r)
    pz, pz_in = along_z(pzs, pzr, pz_s, pz_r)
    mz, mz_in = along_z(mzs, mzr, mz_s, mz_r)
    px, px_in = along_x(pxs, pxr, px_s, px_r)
    mx, mx_in = along_x(mxs, mxr, mx_s, mx_r)

    def offset(s):
        return (nz + ((s + 1) // 2) * (2 * (s % 2) - 1)) % nz

    def forward(s):
        d = offset(s)
        g = (z + d) % nz
        arrived(qbuf.at[g, 0, pl.ds(0, MAIN)], qz_r.at[nz - d - 1])
        for e in across:
            qx(g, e).start()

    arrived(qbuf.at[0, pl.ds(0, nx - 1), pl.ds(MAIN, HD - MAIN)], rx_r.at[0])
    for d in near_first:
        rz(d).start()
    for s in range(1, min(AHEAD, nz)):
        forward(s)

    @pl.loop(0, nz + LAG)
    def _(t):
        @pl.when(t < nz - AHEAD)
        def _():
            forward(t + AHEAD)

        @pl.when(t < nz)
        def _():
            d = offset(t)
            g = (z + d) % nz
            arrived(qbuf.at[g, pl.ds(0, nx - 1), pl.ds(0, MAIN)], qx_r.at[g])

            @pl.when(t > 0)
            def _():
                arrived(qbuf.at[g, :, pl.ds(MAIN, HD - MAIN)], rz_r.at[nz - d - 1])

            mixed, level = attend(g)
            for i in range(nx):
                cols = slice(i * span, (i + 1) * span)
                oxs[g, i] = mixed[:MAIN, cols].astype(BF16)
                pzs[g, i] = mixed[MAIN:, cols].astype(BF16)
                lxs[g, i] = level[:, cols]
                mzs[g, i] = level[:, cols]
            for e in across:
                lx(g, e).start()
            for e in across:
                ox(g, e).start()

            @pl.when(t > 0)
            def _():
                mz(g).start()
                pz(g).start()

        @pl.when(t == 1)
        def _():
            arrived(fpair.at[0], fc_r.at[0])
            fturn[...] = fpair[...].astype(F32).reshape(span, HD).T.astype(BF16).reshape(fturn.shape)
            fown[...] = fturn[c]
            for i in range(2 * nx):
                target = fresh_head * CORES * nx + i

                @pl.when(target != me)
                def _():
                    fresh_out(i).start()

                @pl.when(target == me)
                def _():
                    pltpu.make_async_copy(fown, fbuf.at[fresh_piece], f_r.at[0]).start()


        @pl.when(t >= LAG)
        def _():
            d = offset(t - LAG)
            g = (z + d) % nz
            ox_in(g)
            lx_in(g)
            parts = [(oxs[g, x].astype(F32), lxs[g, x])]
            for e in range(1, nx):
                slot = (x + e) % nx
                parts.append((oxr[g, slot].astype(F32), lxr[g, slot]))
            value, level = merge(parts)
            ozs[g] = value.astype(BF16)
            lzs[g] = level

            @pl.when(t > LAG)
            def _():
                lz(g).start()
                oz(g).start()

    pz_in()
    mz_in()
    for i in range(nx):
        parts = [(pzs[z, i].astype(F32), mzs[z, i])]
        for d in range(1, nz):
            slot = (z + nz - d) % nz
            parts.append((pzr[slot, i].astype(F32), mzr[slot, i]))
        value, level = merge(parts)
        pxs[0, i] = value.astype(BF16)
        mxs[0, i] = level
    for e in across:
        mx(0, e).start()
        px(0, e).start()

    arrived(fbuf, f_r.at[0])
    new_keys = fbuf[:nx].reshape(HD, span)
    new_values = fbuf[nx:].reshape(HD, span)

    def token(row):
        r = row % 2
        tz = (row // 2) % nz
        tx = (row // (2 * nz)) % nx
        tc = row // (2 * nz * nx)
        return ((tz * nx + tx) * CORES + tc) * 2 + r

    key_row = lax.broadcasted_iota(jnp.int32, (span, span), 0)
    query_lane = lax.broadcasted_iota(jnp.int32, (span, span), 1)
    causal = token(key_row) <= token(c * half_span + query_lane % half_span)
    scores = dot(new_keys.T, qbuf[z, x])
    scores = jnp.where(causal, scores, -BIG)
    top = jnp.max(scores, axis=0, keepdims=True)
    weights = jnp.where(causal, jnp.exp2((scores - top) * scale), 0.0)
    total = jnp.sum(weights, axis=0, keepdims=True)
    own = dot(new_values, weights.astype(BF16)) * (1.0 / total)
    own_lsum = top * scale + jnp.log(total) * LOG2E
    parts = [(own[:MAIN], own_lsum), (ozs[z].astype(F32), lzs[z])]
    oz_in()
    lz_in()
    for d in range(1, nz):
        slot = (z + nz - d) % nz
        parts.append((ozr[slot].astype(F32), lzr[slot]))
    first_rows, _ = merge(parts)
    parts = [(own[MAIN:], own_lsum), (pxs[0, x].astype(F32), mxs[0, x])]
    px_in(0)
    mx_in(0)
    for e in range(1, nx):
        slot = (x + nx - e) % nx
        parts.append((pxr[0, slot].astype(F32), mxr[0, slot]))
    last_rows, _ = merge(parts)
    attention = jnp.concatenate([first_rows, last_rows], axis=0)
    attention = attention.T.astype(BF16)
    both = jnp.concatenate([attention[:half_span], attention[half_span:]], axis=1)
    arrived(wout.at[0], wc_r.at[0])


    def yx(q, d):
        return remote(
            yxs.at[q, (x + d) % nx], yxr.at[q, x], yx_s.at[0], yx_r.at[q], to_x(d)
        )

    def yz(q, d):
        return pltpu.make_async_remote_copy(
            src_ref=yzs.at[q, (z + d) % nz],
            dst_ref=yzr.at[q, z],
            send_sem=yz_s.at[0],
            recv_sem=yz_r.at[q],
            device_id={"kvp": to_z(d), "section": after},
            device_id_type=MESH,
        )

    def vz(d):
        return remote(vzs.at[(z + d) % nz], vzr.at[z], vz_s.at[0], vz_r.at[0], to_z(d))

    def vx(d):
        return pltpu.make_async_remote_copy(
            src_ref=vxs.at[(x + d) % nx],
            dst_ref=vxr.at[x],
            send_sem=vx_s.at[0],
            recv_sem=vx_r.at[0],
            device_id={"kvp": to_x(d), "section": after},
            device_id_type=MESH,
        )

    def by_owner(sums):
        rows = jnp.concatenate([sums[:, j * thin : (j + 1) * thin] for j in range(8)], axis=0)
        return dot(gather, rows).astype(BF16).reshape(nz, 16, thin)

    def sum_x(q):
        sums = yown[q, pl.ds(pl.multiple_of(x * 2 * nz, 2 * nz), 2 * nz)]
        arrived(yxr.at[q, pl.ds(0, nx - 1)], yx_r.at[q])
        for d in range(1, nx):
            sums = sums + yxr[q, (x + nx - d) % nx].astype(F32)
        yzs[q] = by_owner(sums.astype(BF16))
        for d in [*far_first, 0]:
            yz(q, d).start()

    for q in [1, 0, *range(2, SPLIT)]:
        sums = dot(both, wout[:, :, q * wide : (q + 1) * wide].reshape(CORES * HD, wide))
        blocks = sums.astype(BF16).reshape(nx, 2 * nz, wide)
        if q > 0:
            yown[q] = sums
            yxs[q] = blocks
            for d in across:
                yx(q, d).start()
        else:
            for i in range(nx):
                vzs[:, i] = by_owner(blocks[i])
            for d in far_first:
                vz(d).start()
    for q in range(1, SPLIT - 1):
        sum_x(q)
    arrived(vzr.at[pl.ds(0, nz - 1)], vz_r.at[0])
    for i in range(nx):
        sums = vzs[z, i].astype(F32)
        for d in range(1, nz):
            sums = sums + vzr[(z + nz - d) % nz, i].astype(F32)
        vxs[i] = sums.astype(BF16)
    for d in range(nx):
        vx((d + 1) % nx).start()
    sum_x(SPLIT - 1)

    residual().wait_recv()
    for q in [*range(1, SPLIT - 1), 0, SPLIT - 1]:
        sums = finr[q].astype(F32)
        if q > 0:
            arrived(yzr.at[q], yz_r.at[q])
            for d in range(nz):
                sums = sums + yzr[q, (z + nz - d) % nz].astype(F32)
        else:
            arrived(vxr, vx_r.at[0])
            for d in range(nx):
                sums = sums + vxr[(x + nx - d) % nx].astype(F32)
        stage_o[...] = sums
        for j in range(8):
            start = q * wide + j * thin
            out[0, :, start : start + thin] = stage_o[2 * j : 2 * j + 2, :].astype(BF16)

    tail = pl.ds(1, SPLIT - 1)
    near_x = pl.ds(0, nx - 1)
    near_z = pl.ds(0, nz - 1)
    main = pl.ds(0, MAIN)
    rest = pl.ds(MAIN, HD - MAIN)
    left(hbuf.at[0, near_x], hx_s.at[0])
    left(hbuf.at[near_z], hz_s.at[0])
    left(gbuf.at[tail, near_z], az_s.at[0])
    left(xbuf.at[tail, near_x], ax_s.at[0])
    left(wq.at[0], dc_s.at[0])
    left(wkv.at[0], ec_s.at[0])
    left(fpair.at[0], fc_s.at[0])
    left(kv.at[0], kc_s.at[0])
    left(limits.at[0], bc_s.at[0])
    left(qbuf.at[near_z, 0, main], qz_s.at[0])
    left(qbuf.at[:, near_x, main], qx_s.at[0])
    left(qbuf.at[0, near_x, rest], rx_s.at[0])
    left(qbuf.at[near_z, :, rest], rz_s.at[0])
    left(oxs.at[:, near_x], ox_s.at[0])
    left(lxs.at[:, near_x], lx_s.at[0])
    left(ozs.at[near_z], oz_s.at[0])
    left(lzs.at[near_z], lz_s.at[0])
    left(pzs.at[near_z], pz_s.at[0])
    left(mzs.at[near_z], mz_s.at[0])
    left(pxs.at[0, near_x], px_s.at[0])
    left(mxs.at[0, near_x], mx_s.at[0])
    left(wout.at[0], wc_s.at[0])
    left(yxs.at[tail, near_x], yx_s.at[0])
    left(yzs.at[tail], yz_s.at[0])
    left(vzs.at[near_z], vz_s.at[0])
    left(vxs, vx_s.at[0])
    left(fin, sec_s.at[0])

    @pl.when(fresh_head == z)
    def _():
        left(fbuf.at[pl.ds(0, 2 * nx - 1)], f_s.at[0])

    @pl.when(fresh_head != z)
    def _():
        left(fbuf, f_s.at[0])


def local(n, nx, sections, hidden, norm_gain, w_query, w_kv, w_out, doc_cache, page_table, page_count):
    nz = n // (CORES * nx)
    span = 2 * n
    model = hidden.shape[-1]
    wide = model // SPLIT
    thin = wide // 8
    fresh_rows = w_kv.shape[-1]
    pages = doc_cache.shape[1]
    rest = HD - MAIN
    vmem = pl.BlockSpec(memory_space=pltpu.VMEM)
    smem = pl.BlockSpec(memory_space=pltpu.SMEM)
    anywhere = pl.BlockSpec(memory_space=pl.ANY)
    dma = pltpu.SemaphoreType.DMA

    def pair(waits):
        return [dma((1,)), dma((waits,))]

    scratch = [
        pltpu.VMEM((CORES, model, HD), BF16),
        pltpu.VMEM((nx, fresh_rows, model), BF16),
        pltpu.VMEM((CORES, HD, model), BF16),
        pltpu.VMEM((CORES, 2 * nz, pages, HD, HD), BF16),
        pltpu.VMEM((CORES, nz, HD, pages * HD), BF16),
        pltpu.VMEM((CORES, 8, span), F32),
        pltpu.VMEM((SPLIT, 16, thin), F32),
        pltpu.VMEM((SPLIT, 16, thin), F32),
        pltpu.VMEM((16, thin), F32),
        pltpu.VMEM((SPLIT, nz, 16, thin), BF16),
        pltpu.VMEM((nz, nx, 16, thin), BF16),
        pltpu.VMEM((SPLIT, nx, 2 * nz, wide), BF16),
        pltpu.VMEM((nz, nx, HD, span), BF16),
        pltpu.VMEM((CORES, span // CORES, HD), BF16),
        pltpu.VMEM((nx, fresh_rows, span), BF16),
        pltpu.VMEM((fresh_rows, span), BF16),
        pltpu.VMEM((2 * nx, fresh_rows, span), BF16),
        pltpu.VMEM((nz, nx, MAIN, span), BF16),
        pltpu.VMEM((nz, nx, MAIN, span), BF16),
        pltpu.VMEM((nz, nx, 1, span), F32),
        pltpu.VMEM((nz, nx, 1, span), F32),
        pltpu.VMEM((nz, MAIN, span), BF16),
        pltpu.VMEM((nz, MAIN, span), BF16),
        pltpu.VMEM((nz, 1, span), F32),
        pltpu.VMEM((nz, 1, span), F32),
        pltpu.VMEM((nz, nx, rest, span), BF16),
        pltpu.VMEM((nz, nx, rest, span), BF16),
        pltpu.VMEM((nz, nx, 1, span), F32),
        pltpu.VMEM((nz, nx, 1, span), F32),
        pltpu.VMEM((1, nx, rest, span), BF16),
        pltpu.VMEM((1, nx, rest, span), BF16),
        pltpu.VMEM((1, nx, 1, span), F32),
        pltpu.VMEM((1, nx, 1, span), F32),
        pltpu.VMEM((SPLIT, span // CORES, wide), F32),
        pltpu.VMEM((SPLIT, nx, 2 * nz, wide), BF16),
        pltpu.VMEM((SPLIT, nx, 2 * nz, wide), BF16),
        pltpu.VMEM((SPLIT, nz, 16, thin), BF16),
        pltpu.VMEM((SPLIT, nz, 16, thin), BF16),
        pltpu.VMEM((nz, nx, 16, thin), BF16),
        pltpu.VMEM((nz, nx, 16, thin), BF16),
        pltpu.VMEM((nx, 16, thin), BF16),
        pltpu.VMEM((nx, 16, thin), BF16),
        pltpu.VMEM((SPLIT, 16, thin), BF16),
        pltpu.VMEM((SPLIT, 16, thin), BF16),
        dma((3,)),
        dma((1,)),
        *pair(1),
        *pair(1),
        *pair(SPLIT),
        *pair(SPLIT),
        *pair(1),
        *pair(1),
        *pair(1),
        *pair(1),
        *pair(1),
        *pair(nz - 1),
        *pair(nz),
        *pair(1),
        *pair(nz - 1),
        *pair(1),
        *pair(nz),
        *pair(nz),
        *pair(1),
        *pair(1),
        *pair(1),
        *pair(1),
        *pair(1),
        *pair(1),
        *pair(1),
        *pair(SPLIT),
        *pair(SPLIT),
        *pair(1),
        *pair(1),
        *pair(1),
    ]
    return pl.pallas_call(
        functools.partial(kernel, n, nz, nx, sections),
        out_shape=jax.ShapeDtypeStruct(hidden.shape, BF16),
        in_specs=[vmem, vmem, anywhere, anywhere, anywhere, anywhere, smem, smem],
        out_specs=vmem,
        scratch_shapes=scratch,
        compiler_params=pltpu.CompilerParams(
            collective_id=0, has_side_effects=True, vmem_limit_bytes=56 * 1024 * 1024
        ),
    )(hidden, norm_gain, w_query, jnp.swapaxes(w_kv, 1, 2), w_out, doc_cache, page_table, page_count)


def solution(mesh):
    placed = (
        P("section", "kvp", None),
        P("section", None),
        P("section", None, "kvp"),
        P("section", None, "kvp"),
        P("section", "kvp", None),
        P("section", "kvp", None, None),
        P("section", "kvp", None),
        P("section", "kvp"),
    )
    n = mesh.shape["kvp"]
    nx = RINGX if n >= 32 else 2
    return jax.shard_map(
        functools.partial(local, n, nx, mesh.shape["section"]),
        mesh=mesh,
        in_specs=placed,
        out_specs=P("section", "kvp", None),
        check_vma=False,
    )
```
